32 devices in a mesh: dp: 16 (over z, x, core), tensor: 2 (over y).
Axes of the slice: x: 2, y: 2, z: 4, core: 2. Of those that a mesh axis runs over, the one named last changes fastest.
Arguments:
- small_rows: bfloat16 [32768, 192], P(('dp', 'tensor')), may hold values from -6 to 6
- large_rows: bfloat16 [32768, 384], P(('dp', 'tensor')), may hold values from -6 to 6
- patch_counts: int32 [2, 192], P(None, ('dp', 'tensor')), may hold values from 37 to 197, as said below
- small_cotangent: bfloat16 [32768, 192], P(('dp', 'tensor')), may hold values from -6 to 6
- large_cotangent: bfloat16 [32768, 384], P(('dp', 'tensor')), may hold values from -6 to 6
- small_heads_in: bfloat16 [192, 576], replicated, may hold values from -0.4375 to 0.4375
- small_heads_out: bfloat16 [192, 192], replicated, may hold values from -3.5 to 3.5
- small_up: bfloat16 [192, 768], P(None, 'tensor'), may hold values from -0.4375 to 0.4375
- small_up_bias: bfloat16 [768], P('tensor'), may hold values from -3 to 3
- small_down: bfloat16 [768, 192], P('tensor'), may hold values from -0.21875 to 0.21875
- large_heads_in: bfloat16 [384, 1152], replicated, may hold values from -0.3125 to 0.3125
- large_heads_out: bfloat16 [384, 384], replicated, may hold values from -2.5 to 2.5
- large_up: bfloat16 [384, 1536], P(None, 'tensor'), may hold values from -0.3125 to 0.3125
- large_up_bias: bfloat16 [1536], P('tensor'), may hold values from -3 to 3
- large_down: bfloat16 [1536, 384], P('tensor'), may hold values from -0.15625 to 0.15625
- small_cls_enter: bfloat16 [192, 384], replicated, may hold values from -0.4375 to 0.4375
- large_cross_in: bfloat16 [384, 1152], replicated, may hold values from -0.3125 to 0.3125
- large_cross_out: bfloat16 [384, 384], replicated, may hold values from -2.5 to 2.5
- small_cls_leave: bfloat16 [384, 192], replicated, may hold values from -0.3125 to 0.3125
- large_cls_enter: bfloat16 [384, 192], replicated, may hold values from -0.3125 to 0.3125
- small_cross_in: bfloat16 [192, 576], replicated, may hold values from -0.4375 to 0.4375
- small_cross_out: bfloat16 [192, 192], replicated, may hold values from -3.5 to 3.5
- large_cls_leave: bfloat16 [192, 384], replicated, may hold values from -0.4375 to 0.4375
- small_gains: bfloat16 [5, 192], replicated, may hold values from 0.099609375 to 1.8984375
- small_shifts: bfloat16 [14, 192], replicated, may hold values from -1.5 to 1.5
- large_gains: bfloat16 [5, 384], replicated, may hold values from 0.099609375 to 1.8984375
- large_shifts: bfloat16 [14, 384], replicated, may hold values from -1.5 to 1.5
Outputs:
- small_out: bfloat16 [32768, 192], P(('dp', 'tensor'))
- large_out: bfloat16 [32768, 384], P(('dp', 'tensor'))
- small_rows_grad: float32 [32768, 192], P(('dp', 'tensor'))
- large_rows_grad: float32 [32768, 384], P(('dp', 'tensor'))
- grad_small_heads_in: float32 [192, 576], replicated
- grad_small_heads_out: float32 [192, 192], replicated
- grad_small_up: float32 [192, 768], P(None, 'tensor')
- grad_small_up_bias: float32 [768], P('tensor')
- grad_small_down: float32 [768, 192], P('tensor')
- grad_large_heads_in: float32 [384, 1152], replicated
- grad_large_heads_out: float32 [384, 384], replicated
- grad_large_up: float32 [384, 1536], P(None, 'tensor')
- grad_large_up_bias: float32 [1536], P('tensor')
- grad_large_down: float32 [1536, 384], P('tensor')
- grad_small_cls_enter: float32 [192, 384], replicated
- grad_large_cross_in: float32 [384, 1152], replicated
- grad_large_cross_out: float32 [384, 384], replicated
- grad_small_cls_leave: float32 [384, 192], replicated
- grad_large_cls_enter: float32 [384, 192], replicated
- grad_small_cross_in: float32 [192, 576], replicated
- grad_small_cross_out: float32 [192, 192], replicated
- grad_large_cls_leave: float32 [192, 384], replicated
- grad_small_gains: float32 [5, 192], replicated
- grad_small_shifts: float32 [14, 192], replicated
- grad_large_gains: float32 [5, 384], replicated
- grad_large_shifts: float32 [14, 384], replicated
The draws below stay inside these ranges and needn't reach their ends.
Inputs may be any that keep to these rules, and one draw needn't show every extreme that they name: `patch_counts`: each column is one crop, global or local: a global crop has 197 small and 145 large rows, a local one 37 and 65. Each run of 6 columns holds exactly 4 global crops, in drawn order, so the crops of one block take 4 * 197 + 2 * 37 small rows and 710 large rows.
All inputs are finite; a program needn't handle non-finite values.
Results may differ from the reference program's by a relative error of at most 0.024.
Values may be sent and summed in bfloat16 or wider, within the bound.
A program may use at most 256 MiB of HBM per device.

```python
import jax
import jax.numpy as jnp
from jax import lax

DS = 192
DL = 384
HEADS = 6
HS = 768
HL = 1536
NG = 4
G_SMALL = 197
L_SMALL = 37
G_LARGE = 145
L_LARGE = 65
QBLK = 512
CROPS_DEV = 6
RS_DEV = 1024
RL_DEV = 1024
CROPS = 192
ROWS_S = 32768
ROWS_L = 32768
N_DP = 16
N_TENSOR = 2


def draw_patch_counts(key, part):
    key = jax.random.fold_in(key, 11)
    devices = CROPS // CROPS_DEV
    scores = jax.random.randint(key, (devices, CROPS_DEV), 0, 1 << 20) * CROPS_DEV + jnp.arange(CROPS_DEV, dtype=jnp.int32)[None, :]
    ranks = jnp.argsort(jnp.argsort(scores, axis=1, stable=True), axis=1, stable=True)
    global_crop = ranks < NG
    small_counts = jnp.where(global_crop, G_SMALL, L_SMALL)
    large_counts = jnp.where(global_crop, G_LARGE, L_LARGE)
    return jnp.stack([small_counts.reshape(-1), large_counts.reshape(-1)]).astype(jnp.int32)


def block_scale(key, extent, split, smallest, largest):
    level, own = 1.0, jax.random.fold_in(key, 6)
    for axis_at, blocks in split:
        draws = jnp.exp(jax.random.uniform(jax.random.fold_in(own, axis_at), (blocks,), jnp.float32, smallest / len(split), largest / len(split)))
        level = level * jnp.repeat(draws, extent[axis_at] // blocks).reshape([-1 if axis == axis_at else 1 for axis in range(len(extent))])
    return level


def gaussian(stream_key, extent, scale, reach, shards=(), kind=jnp.bfloat16):
    values = jax.random.normal(stream_key, extent, jnp.float32) * scale
    if len(shards) > 0:
        values = block_scale(stream_key, extent, shards, -0.22, 0.18) * values
    return jnp.clip(values, min=-reach, max=reach).astype(kind)


def setup_inputs(seed: int = 0) -> dict:
    keys = jax.random.split(jax.random.key(seed), 28)
    return {
        "small_rows": gaussian(keys[0], (ROWS_S, DS), 1.0, 6.0, ((0, 32),)),
        "large_rows": gaussian(keys[1], (ROWS_L, DL), 1.0, 6.0, ((0, 32),)),
        "patch_counts": draw_patch_counts(jax.random.fold_in(keys[27], 71), 0),
        "small_cotangent": gaussian(keys[3], (ROWS_S, DS), 1.0, 6.0, ((0, 32),)),
        "large_cotangent": gaussian(keys[4], (ROWS_L, DL), 1.0, 6.0, ((0, 32),)),
        "small_heads_in": gaussian(keys[5], (DS, 3 * DS), DS ** -0.5, 0.4375),
        "small_heads_out": gaussian(keys[6], (DS, DS), (max(DS // 64, 1)) ** -0.5, 3.5),
        "small_up": gaussian(keys[7], (DS, HS), DS ** -0.5, 0.4375, ((1, 2),)),
        "small_up_bias": gaussian(keys[8], (HS,), 0.5, 3.0, ((0, 2),)),
        "small_down": gaussian(keys[9], (HS, DS), HS ** -0.5, 0.21875, ((0, 2),)),
        "large_heads_in": gaussian(keys[10], (DL, 3 * DL), DL ** -0.5, 0.3125),
        "large_heads_out": gaussian(keys[11], (DL, DL), (max(DL // 64, 1)) ** -0.5, 2.5),
        "large_up": gaussian(keys[12], (DL, HL), DL ** -0.5, 0.3125, ((1, 2),)),
        "large_up_bias": gaussian(keys[13], (HL,), 0.5, 3.0, ((0, 2),)),
        "large_down": gaussian(keys[14], (HL, DL), HL ** -0.5, 0.15625, ((0, 2),)),
        "small_cls_enter": gaussian(keys[15], (DS, DL), DS ** -0.5, 0.4375),
        "large_cross_in": gaussian(keys[16], (DL, 3 * DL), DL ** -0.5, 0.3125),
        "large_cross_out": gaussian(keys[17], (DL, DL), (max(DL // 64, 1)) ** -0.5, 2.5),
        "small_cls_leave": gaussian(keys[18], (DL, DS), DL ** -0.5, 0.3125),
        "large_cls_enter": gaussian(keys[19], (DL, DS), DL ** -0.5, 0.3125),
        "small_cross_in": gaussian(keys[20], (DS, 3 * DS), DS ** -0.5, 0.4375),
        "small_cross_out": gaussian(keys[21], (DS, DS), (max(DS // 64, 1)) ** -0.5, 3.5),
        "large_cls_leave": gaussian(keys[22], (DS, DL), DS ** -0.5, 0.4375),
        "small_gains": jnp.clip(1.0 + 0.18 * jax.random.normal(keys[23], (5, DS), jnp.float32), 0.099609375, 1.8984375).astype(jnp.bfloat16),
        "small_shifts": gaussian(keys[24], (14, DS), 0.3, 1.5),
        "large_gains": jnp.clip(1.0 + 0.18 * jax.random.normal(keys[25], (5, DL), jnp.float32), 0.099609375, 1.8984375).astype(jnp.bfloat16),
        "large_shifts": gaussian(keys[26], (14, DL), 0.3, 1.5),
    }


NEGATIVE = -1e+30
EPSILON = 1e-06
HIGHEST = lax.Precision.HIGHEST

@jax.custom_vjp
def low(v):
    return lax.optimization_barrier(v.astype(jnp.bfloat16)).astype(jnp.float32)

@jax.custom_vjp
def low_back(v):
    return v

def low_keep(v):
    return (low(v), None)

def low_pass(kept, grad):
    return (grad,)

def back_keep(v):
    return (v, None)

def back_low(kept, grad):
    return (low(grad),)
low.defvjp(low_keep, low_pass)
low_back.defvjp(back_keep, back_low)

def product(left, right):
    return jnp.dot(left, right, precision=HIGHEST, preferred_element_type=jnp.float32)

def layer_norm(values, gain, shift):
    center = values - lax.optimization_barrier(jnp.mean(values, -1, keepdims=True))
    spread = lax.optimization_barrier(jnp.mean(center * center, -1, keepdims=True))
    return center * lax.rsqrt(spread + EPSILON) * gain + shift

def smooth(values):
    return jax.nn.gelu(values, approximate=False)

def crop_layout(lengths, row_count):
    lengths = lengths.astype(jnp.int32)
    crop_ends = jnp.cumsum(lengths).astype(jnp.int32)
    firsts = (crop_ends - lengths).astype(jnp.int32)
    places = jnp.arange(row_count, dtype=jnp.int32)
    segment = lax.optimization_barrier(jnp.sum((places[:, None] >= crop_ends[None, :]).astype(jnp.int32), 1)).astype(jnp.int32)
    return (segment, firsts)

def self_attention(packed, segment):
    row_count = packed.shape[0]
    columns = packed.shape[1] // 3
    head_size = columns // HEADS
    factor = float(head_size) ** (-0.5)
    blocks = row_count // QBLK
    queries = packed[:, :columns].reshape(blocks, QBLK, HEADS, head_size)
    all_keys = packed[:, columns:2 * columns].reshape(row_count, HEADS, head_size)
    all_values = packed[:, 2 * columns:].reshape(row_count, HEADS, head_size)

    def one_block(pieces):
        block_queries, block_segment = pieces
        raw_scores = jnp.einsum('qhd,khd->hqk', block_queries, all_keys, precision=HIGHEST)
        scores = low_back(raw_scores) * factor
        scores = jnp.where((block_segment[:, None] == segment[None, :])[None], scores, NEGATIVE)
        chances = jax.nn.softmax(scores, axis=-1)
        return jnp.einsum('hqk,khd->qhd', low(chances), all_values, precision=HIGHEST)
    result = lax.map(jax.checkpoint(one_block), (queries, segment.reshape(blocks, QBLK)))
    return result.reshape(row_count, columns)

def encoder_block(values, segment, gains, shifts, heads_in, heads_out, up_weight, up_bias, down_weight):
    nothing = jnp.zeros(shifts.shape[1:], jnp.float32)
    normed_in = low(layer_norm(values, gains[0], shifts[0]))
    packed = low(low_back(product(normed_in, heads_in)) + jnp.concatenate([shifts[1], nothing, shifts[2]]))
    attended = low(low_back(self_attention(packed, segment)))
    middle = values + low_back(product(attended, heads_out)) + shifts[3]
    normed_mid = low(layer_norm(middle, gains[1], shifts[4]))
    hidden = low_back(product(normed_mid, up_weight)) + up_bias
    active = low(smooth(hidden))
    return middle + low_back(product(active, down_weight)) + shifts[5]

def class_cross(cls_rows, other_rows, other_segment, other_firsts, gains_own, shifts_own, gains_other, shifts_other, weight_enter, weight_cross, weight_out, weight_leave):
    crops = cls_rows.shape[0]
    other_count = other_rows.shape[0]
    columns = other_rows.shape[1]
    head_size = columns // HEADS
    factor = float(head_size) ** (-0.5)
    nothing = jnp.zeros((columns,), jnp.float32)
    lifted = low(smooth(layer_norm(cls_rows, gains_own[2], shifts_own[6])))
    moved = low_back(product(lifted, weight_enter)) + shifts_other[8]
    query_norm = low(layer_norm(moved, gains_other[3], shifts_other[9]))
    key_norm = low(layer_norm(other_rows, gains_other[3], shifts_other[9]))
    own_proj = low(low_back(product(query_norm, weight_cross)) + jnp.concatenate([shifts_other[10], nothing, shifts_other[11]]))
    row_proj = low(low_back(product(key_norm, weight_cross[:, columns:])) + jnp.concatenate([nothing, shifts_other[11]]))
    queries = own_proj[:, :columns].reshape(crops, HEADS, head_size)
    own_keys = own_proj[:, columns:2 * columns].reshape(crops, HEADS, head_size)
    own_values = own_proj[:, 2 * columns:].reshape(crops, HEADS, head_size)
    row_keys = row_proj[:, :columns].reshape(other_count, HEADS, head_size)
    row_values = row_proj[:, columns:].reshape(other_count, HEADS, head_size)
    own_scores = low_back(lax.optimization_barrier(jnp.sum(queries * own_keys, -1))) * factor
    row_scores = low_back(jnp.einsum('chd,khd->chk', queries, row_keys, precision=HIGHEST)) * factor
    places = jnp.arange(other_count, dtype=jnp.int32)
    crop_ids = jnp.arange(crops, dtype=jnp.int32)
    usable = (other_segment[None, :] == crop_ids[:, None]) & (places[None, :] != other_firsts[:, None])
    row_scores = jnp.where(usable[:, None, :], row_scores, NEGATIVE)
    chances = low(jax.nn.softmax(jnp.concatenate([own_scores[:, :, None], row_scores], 2), axis=-1))
    mixed = chances[:, :, 0:1] * own_values + jnp.einsum('chk,khd->chd', chances[:, :, 1:], row_values, precision=HIGHEST)
    attended = low(low_back(mixed.reshape(crops, columns)))
    joined = moved + low_back(product(attended, weight_out)) + shifts_other[12]
    spread_out = low(smooth(layer_norm(joined, gains_other[4], shifts_other[13])))
    return low_back(product(spread_out, weight_leave)) + shifts_own[7]

def device_forward(params, small_values, large_values, crop_counts):
    small_heads_in, small_heads_out, small_up, small_up_bias, small_down, large_heads_in, large_heads_out, large_up, large_up_bias, large_down, small_cls_enter, large_cross_in, large_cross_out, small_cls_leave, large_cls_enter, small_cross_in, small_cross_out, large_cls_leave, small_gains, small_shifts, large_gains, large_shifts = params
    small_segment, small_firsts = crop_layout(crop_counts[0], small_values.shape[0])
    large_segment, large_firsts = crop_layout(crop_counts[1], large_values.shape[0])
    small_block = encoder_block(small_values, small_segment, small_gains, small_shifts, small_heads_in, small_heads_out, small_up, small_up_bias, small_down)
    large_block = encoder_block(large_values, large_segment, large_gains, large_shifts, large_heads_in, large_heads_out, large_up, large_up_bias, large_down)
    small_cls = class_cross(small_block[small_firsts], large_block, large_segment, large_firsts, small_gains, small_shifts, large_gains, large_shifts, small_cls_enter, large_cross_in, large_cross_out, small_cls_leave)
    large_cls = class_cross(large_block[large_firsts], small_block, small_segment, small_firsts, large_gains, large_shifts, small_gains, small_shifts, large_cls_enter, small_cross_in, small_cross_out, large_cls_leave)
    return (small_block.at[small_firsts].set(small_cls), large_block.at[large_firsts].set(large_cls))

def reference(small_rows, large_rows, patch_counts, small_cotangent, large_cotangent, small_heads_in, small_heads_out, small_up, small_up_bias, small_down, large_heads_in, large_heads_out, large_up, large_up_bias, large_down, small_cls_enter, large_cross_in, large_cross_out, small_cls_leave, large_cls_enter, small_cross_in, small_cross_out, large_cls_leave, small_gains, small_shifts, large_gains, large_shifts):
    params = tuple((weight.astype(jnp.float32) for weight in (small_heads_in, small_heads_out, small_up, small_up_bias, small_down, large_heads_in, large_heads_out, large_up, large_up_bias, large_down, small_cls_enter, large_cross_in, large_cross_out, small_cls_leave, large_cls_enter, small_cross_in, small_cross_out, large_cls_leave, small_gains, small_shifts, large_gains, large_shifts)))
    devices = N_DP * N_TENSOR
    counts = jnp.transpose(patch_counts.astype(jnp.int32).reshape(2, devices, CROPS_DEV), (1, 0, 2))
    inputs = (small_rows.astype(jnp.float32).reshape(devices, RS_DEV, DS), large_rows.astype(jnp.float32).reshape(devices, RL_DEV, DL), counts, small_cotangent.astype(jnp.float32).reshape(devices, RS_DEV, DS), large_cotangent.astype(jnp.float32).reshape(devices, RL_DEV, DL))

    def one_device(summed, pieces):
        small_in, large_in, crop_counts, small_cot, large_cot = pieces

        def forward(weights, small_values, large_values):
            return device_forward(weights, small_values, large_values, crop_counts)
        outputs, pullback = jax.vjp(forward, params, small_in, large_in)
        grad_params, grad_small, grad_large = pullback((small_cot, large_cot))
        summed = tuple((left + right for left, right in zip(summed, grad_params)))
        return (summed, (outputs[0].astype(jnp.bfloat16), outputs[1].astype(jnp.bfloat16), grad_small, grad_large))
    begin = tuple((jnp.zeros(weight.shape, jnp.float32) for weight in params))
    summed, (small_out, large_out, small_grad, large_grad) = lax.scan(one_device, begin, inputs)
    grad_small_heads_in, grad_small_heads_out, grad_small_up, grad_small_up_bias, grad_small_down, grad_large_heads_in, grad_large_heads_out, grad_large_up, grad_large_up_bias, grad_large_down, grad_small_cls_enter, grad_large_cross_in, grad_large_cross_out, grad_small_cls_leave, grad_large_cls_enter, grad_small_cross_in, grad_small_cross_out, grad_large_cls_leave, grad_small_gains, grad_small_shifts, grad_large_gains, grad_large_shifts = summed
    return (small_out.reshape(ROWS_S, DS), large_out.reshape(ROWS_L, DL), small_grad.reshape(ROWS_S, DS), large_grad.reshape(ROWS_L, DL), grad_small_heads_in, grad_small_heads_out, grad_small_up, grad_small_up_bias, grad_small_down, grad_large_heads_in, grad_large_heads_out, grad_large_up, grad_large_up_bias, grad_large_down, grad_small_cls_enter, grad_large_cross_in, grad_large_cross_out, grad_small_cls_leave, grad_large_cls_enter, grad_small_cross_in, grad_small_cross_out, grad_large_cls_leave, grad_small_gains, grad_small_shifts, grad_large_gains, grad_large_shifts)
```

```python
import functools
import collections
import jax
import jax.numpy as jnp
from jax import lax
from jax.experimental import pallas as pl
from jax.experimental.pallas import tpu as pltpu
from jax.sharding import PartitionSpec as P

HEADS = 6
VMEM_LIMIT = 64 * 1024 * 1024
NEGATIVE = -1e30
EPSILON = 1e-06
F32, BF16 = jnp.float32, jnp.bfloat16
LANES = 384
CLS = 16
STACK = HEADS * CLS

GLOBAL_ROWS, LOCAL_ROWS = (197, 145), (37, 65)
LOG2E = 1.4426950408889634


def low(values):
    return values.astype(BF16)


def dot(left, right, left_axis, right_axis):
    return lax.dot_general(
        left, right, (((left_axis,), (right_axis,)), ((), ())), preferred_element_type=F32
    )


def nn(left, right):
    return dot(left, right, 1, 0)


def nt(left, right):
    return dot(left, right, 1, 1)


def tn(left, right):
    return dot(left, right, 0, 0)


class Branch:
    def __init__(self, index, rows, columns, hidden, width, layout):
        self.index, self.rows, self.columns, self.hidden = index, rows, columns, hidden
        self.head = columns // HEADS
        self.width, self.slots = width, len(layout)
        self.tokens = width * self.slots
        self.pieces = []
        self.bounds = []
        g_rows, l_rows = GLOBAL_ROWS[index], LOCAL_ROWS[index]
        for slot, crops in enumerate(layout):
            lane, ends = 0, []
            for crop in crops:
                length = g_rows if crop < 4 else l_rows if crop < 6 else rows - 4 * g_rows - 2 * l_rows
                self.pieces.append((slot * width + lane, length, crop))
                lane += length
                ends.append(lane)
            assert lane <= width
            self.bounds.append(ends)


def norm(values, axis):
    center = values - jnp.mean(values, axis, keepdims=True)
    scale = lax.rsqrt(jnp.mean(center * center, axis, keepdims=True) + EPSILON)
    return center * scale, scale


def norm_back(grad, unit, scale, axis):
    return scale * (
        grad
        - jnp.mean(grad, axis, keepdims=True)
        - unit * jnp.mean(grad * unit, axis, keepdims=True)
    )


def smooth_parts(values):
    chance = 0.5 + 0.5 * lax.erf(values * (0.5**0.5))
    slope = chance + values * (jnp.exp(values * values * -0.5) * 0.3989422804014327)
    return values * chance, slope


def pick(at, values):
    result = values[-1]
    for place in range(len(values) - 2, -1, -1):
        result = jnp.where(at == place, values[place], result)
    return result


def iota(shape, axis):
    return lax.broadcasted_iota(jnp.int32, shape, axis)


def slot_columns(branch, slot):
    return pl.ds(pl.multiple_of(slot * branch.width, branch.width), branch.width)


def places(counts, b):
    starts = [jnp.int32(0)] * 7
    begin, globals_seen, locals_seen = jnp.int32(0), jnp.int32(0), jnp.int32(0)
    for crop in range(6):
        rows = counts[b.index, crop]
        is_global = counts[0, crop] == GLOBAL_ROWS[0]
        for k in range(4):
            starts[k] = jnp.where(is_global & (globals_seen == k), begin, starts[k])
        for k in range(2):
            starts[4 + k] = jnp.where((~is_global) & (locals_seen == k), begin, starts[4 + k])
        begin = begin + rows
        globals_seen = globals_seen + jnp.where(is_global, 1, 0)
        locals_seen = locals_seen + jnp.where(is_global, 0, 1)
    starts[6] = begin
    return starts


def lay_out(b, r, counts):
    starts = places(counts, b)
    lane = iota((1, b.tokens), 1)
    source = jnp.full((1, b.tokens), -1, jnp.int32)
    patch = jnp.full((1, b.tokens), -1, jnp.int32)
    cls = jnp.full((1, b.tokens), -1, jnp.int32)
    for first, length, crop in b.pieces:
        inside = (lane >= first) & (lane < first + length)
        source = jnp.where(inside, lane - first + starts[crop], source)
        if crop < 6:
            patch = jnp.where(inside & (lane > first), crop, patch)
            cls = jnp.where(lane == first, crop, cls)
    r.index[0:1, :] = source
    r.index[1:2, :] = patch
    r.index[2:3, :] = cls
    at = iota((CLS, 1), 0)
    first_rows = jnp.full((CLS, 1), -1, jnp.int32)
    for crop in range(6):
        first_rows = jnp.where(at == crop, starts[crop], first_rows)
    chosen = low((iota((CLS, b.rows), 1) == first_rows).astype(F32))
    r.cot_cls[...] = nn(chosen, r.cot[...])


def bring_in(b, r):
    r.stack[0 : b.columns, :] = r.rows[...].T
    r.stack[b.columns : 2 * b.columns, :] = r.cot[...].T

    def body(slot, carry):
        cols = slot_columns(b, slot)
        chosen = low((iota((b.rows, b.width), 0) == r.index[0:1, cols]).astype(F32))
        both = nn(r.stack[...], chosen)
        r.x[:, cols] = low(both[: b.columns])
        keep = r.index[2:3, cols] < 0
        r.cotT[:, cols] = low(jnp.where(keep, both[b.columns :], 0.0))
        return carry

    lax.fori_loop(0, b.slots, body, 0)


def slot_mask(b, slot):
    ends = [pick(slot, [e[min(i, len(e) - 1)] for e in b.bounds]) for i in range(3)]

    def segment(axis):
        at = iota((b.width, b.width), axis)
        total = jnp.zeros((b.width, b.width), jnp.int32)
        for end in ends:
            total = total + (at >= end).astype(jnp.int32)
        return total

    return jnp.where(segment(0) == segment(1), 0.0, NEGATIVE)


def forward_attention(b, r):
    columns, head, width = b.columns, b.head, b.width
    factor = float(head) ** (-0.5) * LOG2E

    def body(slot, carry):
        cols = slot_columns(b, slot)
        x = r.x[:, cols].astype(F32)
        unit, scale = norm(x, 0)
        a = low(unit * r.gainT[:, 0:1] + r.shiftT[:, 0:1])
        r.a[0:columns, cols] = a
        nothing = jnp.zeros((columns, 1), F32)
        bias = jnp.concatenate([r.shiftT[:, 1:2], nothing, r.shiftT[:, 2:3]], 0)
        r.qkv[:, cols] = low(nn(r.w_inT[...], a) + bias)
        mask = slot_mask(b, slot)
        for h in range(HEADS):
            q = r.qkv[h * head : (h + 1) * head, cols]
            k = r.qkv[columns + h * head : columns + (h + 1) * head, cols]
            v = r.qkv[2 * columns + h * head : 2 * columns + (h + 1) * head, cols]
            scores = tn(k, q) * factor + mask
            highest = jnp.max(scores, 0, keepdims=True)
            powers = jnp.exp2(scores - highest)
            total = jnp.sum(powers, 0, keepdims=True)
            r.logs[h : h + 1, cols] = highest + jnp.log2(total)
            chances = low(powers * (1.0 / total))
            r.o[h * head : (h + 1) * head, cols] = low(nn(v, chances))
        y = x + nn(r.w_outT[...], r.o[0:columns, cols]) + r.shiftT[:, 3:4]
        r.y[:, cols] = y
        unit, scale = norm(y, 0)
        r.c[0:columns, cols] = low(unit * r.gainT[:, 1:2] + r.shiftT[:, 4:5])
        return carry

    lax.fori_loop(0, b.slots, body, 0)


def forward_mlp(b, r):
    chunk = 256 if b.hidden % 512 == 0 else b.hidden // 4
    r.cls[...] = jnp.zeros_like(r.cls)

    def body(slot, carry):
        cols = slot_columns(b, slot)
        c = r.c[0 : b.columns, cols]
        for at in range(0, b.hidden, chunk):
            hidden = nn(r.w_upT[at : at + chunk, :], c) + r.up_biasT[at : at + chunk, 0:1]
            active, slope = smooth_parts(hidden)
            r.u[at : at + chunk, cols] = low(active)
            r.g[at : at + chunk, cols] = low(slope)
        z = r.y[:, cols] + nn(r.w_downT[...], r.u[0 : b.hidden, cols]) + r.shiftT[:, 5:6]
        r.z[:, cols] = z
        z_low = low(z)
        r.out[:, cols] = z_low
        chosen = low((iota((CLS, b.width), 0) == r.index[2:3, cols]).astype(F32))
        r.cls[...] += nt(chosen, z_low) + nt(chosen, low(z - z_low.astype(F32)))
        unit, scale = norm(z, 0)
        r.n[:, cols] = low(unit * r.gainT[:, 3:4] + r.shiftT[:, 9:10])
        return carry

    lax.fori_loop(0, b.slots, body, 0)


def head_mask(columns):
    head = columns // HEADS
    at = iota((STACK, columns), 1)
    first = iota((STACK, columns), 0) // CLS * head
    return (at >= first) & (at < first + head)


def spread(values, mask):
    return jnp.where(mask, jnp.concatenate([values] * HEADS, 0), 0.0)


def gather_heads(values, mask):
    values = jnp.where(mask, values, 0.0)
    total = values[0:CLS]
    for h in range(1, HEADS):
        total = total + values[h * CLS : (h + 1) * CLS]
    return total


def column_sum(values):
    return jnp.sum(values, 0, keepdims=True)


def cross(b, r, o, ro, g):
    wide = o.columns
    factor = float(o.head) ** (-0.5)
    mask = head_mask(wide)
    og, ob = ro.gains, ro.shifts

    def row(table, at):
        return table[at : at + 1, :].astype(F32)

    xc = r.cls[...]
    unit2, scale2 = norm(xc, 1)
    lifted, slope2 = smooth_parts(unit2 * row(r.gains, 2) + row(r.shifts, 6))
    lifted = low(lifted)
    moved = nn(lifted, r.enter[...]) + row(ob, 8)
    unit3, scale3 = norm(moved, 1)
    query_norm = low(unit3 * row(og, 3) + row(ob, 9))
    q = low(nn(query_norm, ro.cross_in[:, 0:wide]) + row(ob, 10))
    own_k = low(nn(query_norm, ro.cross_in[:, wide : 2 * wide]))
    own_v = low(nn(query_norm, ro.cross_in[:, 2 * wide : 3 * wide]) + row(ob, 11))
    q_all = spread(q.astype(F32), mask)
    k_all = spread(own_k.astype(F32), mask)
    v_all = spread(own_v.astype(F32), mask)
    key_map = low(nt(low(q_all), ro.cross_in[:, wide : 2 * wide]))
    own_score = jnp.sum(q_all * k_all, 1, keepdims=True) * factor
    usable = ro.index[1:2, :] == iota((STACK, o.tokens), 0) % CLS
    scores = jnp.where(usable, nn(key_map, ro.n[...]) * factor, NEGATIVE)
    highest = jnp.maximum(own_score, jnp.max(scores, 1, keepdims=True))
    powers = jnp.exp(scores - highest)
    own_power = jnp.exp(own_score - highest)
    inverse = 1.0 / (own_power + jnp.sum(powers, 1, keepdims=True))
    chances = powers * inverse
    own_chance = own_power * inverse
    chances_low = low(chances)
    own_low = low(own_chance).astype(F32)
    ro.sp[STACK : 2 * STACK, :] = chances_low
    total = jnp.sum(chances_low.astype(F32), 1, keepdims=True)
    mean_row = low(nt(chances_low, ro.n[...]))
    value_bias = row(ob, 11)
    mixed = own_low * v_all + nn(mean_row, ro.cross_in[:, 2 * wide : 3 * wide]) + total * value_bias
    attended = low(gather_heads(mixed, mask))
    joined = moved + nn(attended, ro.cross_out[...]) + row(ob, 12)
    unit4, scale4 = norm(joined, 1)
    spread_out, slope4 = smooth_parts(unit4 * row(og, 4) + row(ob, 13))
    spread_out = low(spread_out)
    r.new_cls[...] = low(nn(spread_out, r.leave[...]) + row(r.shifts, 7))

    new_grad = r.cot_cls[...]
    new_low = low(new_grad)
    r.table[5 + 7 : 5 + 8, :] = column_sum(new_grad)
    g.leave(tn(spread_out, new_low))
    back = nt(new_low, r.leave[...]) * slope4
    ro.table[4:5, :] = column_sum(back * unit4)
    ro.table[5 + 13 : 5 + 14, :] = column_sum(back)
    joined_grad = norm_back(back * row(og, 4), unit4, scale4, 1)
    ro.table[5 + 12 : 5 + 13, :] = column_sum(joined_grad)
    joined_low = low(joined_grad)
    g.cross_out(tn(attended, joined_low))
    mixed_grad = low(nt(joined_low, ro.cross_out[...])).astype(F32)
    mixed_all = spread(mixed_grad, mask)
    mixed_all_low = low(mixed_all)
    own_v_grad = gather_heads(own_low * mixed_all, mask)
    own_chance_grad = jnp.sum(mixed_all * v_all, 1, keepdims=True)
    value_map = low(nt(mixed_all_low, ro.cross_in[:, 2 * wide : 3 * wide]))
    chance_grad = nn(value_map, ro.n[...]) + jnp.sum(mixed_all * value_bias, 1, keepdims=True)
    inner = own_chance_grad * own_chance + jnp.sum(chance_grad * chances, 1, keepdims=True)
    score_grad = low(chances * (chance_grad - inner) * factor)
    own_score_grad = low(own_chance * (own_chance_grad - inner) * factor).astype(F32)
    ro.sp[0:STACK, :] = score_grad
    mean_back = low(nt(score_grad, ro.n[...]))
    q_grad = gather_heads(
        own_score_grad * k_all + nn(mean_back, ro.cross_in[:, wide : 2 * wide]), mask
    )
    own_k_grad = gather_heads(own_score_grad * q_all, mask)
    ro.table[5 + 10 : 5 + 11, :] = column_sum(q_grad)
    ro.table[5 + 11 : 5 + 12, :] = column_sum(own_v_grad) + column_sum(total * mixed_all)
    q_low, k_low, v_low = low(q_grad), low(own_k_grad), low(own_v_grad)
    g.cross_in(
        0,
        tn(query_norm, q_low),
    )
    g.cross_in(
        1,
        tn(
            jnp.concatenate([query_norm, mean_back], 0),
            jnp.concatenate([k_low, low(q_all)], 0),
        ),
    )
    g.cross_in(
        2,
        tn(
            jnp.concatenate([query_norm, mean_row], 0),
            jnp.concatenate([v_low, mixed_all_low], 0),
        ),
    )
    back = (
        nt(q_low, ro.cross_in[:, 0:wide])
        + nt(k_low, ro.cross_in[:, wide : 2 * wide])
        + nt(v_low, ro.cross_in[:, 2 * wide : 3 * wide])
    )
    ro.table[3:4, :] = column_sum(back * unit3)
    ro.table[5 + 9 : 5 + 10, :] = column_sum(back)
    moved_grad = joined_grad + norm_back(back * row(og, 3), unit3, scale3, 1)
    ro.table[5 + 8 : 5 + 9, :] = column_sum(moved_grad)
    moved_low = low(moved_grad)
    g.enter(tn(lifted, moved_low))
    back = nt(moved_low, r.enter[...]) * slope2
    r.table[2:3, :] = column_sum(back * unit2)
    r.table[5 + 6 : 5 + 7, :] = column_sum(back)
    r.cls_grad[...] = norm_back(back * row(r.gains, 2), unit2, scale2, 1)
    ro.maps[0:STACK, :] = key_map
    ro.maps[STACK : 2 * STACK, :] = value_map


def backward_cross(b, r):
    r.sums[...] = jnp.zeros_like(r.sums)
    maps = r.maps[...].astype(F32).T.astype(BF16)
    cls_grad = r.cls_grad[...]
    high = low(cls_grad)
    pair = jnp.concatenate([high, low(cls_grad - high.astype(F32))], 0)

    def body(slot, carry):
        cols = slot_columns(b, slot)
        z = r.z[:, cols]
        unit, scale = norm(z, 0)
        grad = nn(maps, r.sp[:, cols])
        ones = jnp.ones((16, b.width), BF16)
        r.sums[0] += nt(ones, low(grad))
        r.sums[1] += nt(ones, low(grad * unit))
        chosen = low((iota((CLS, b.width), 0) == r.index[2:3, cols]).astype(F32))
        scatter = tn(pair, jnp.concatenate([chosen, chosen], 0))
        grad = norm_back(grad * r.gainT[:, 3:4], unit, scale, 0)
        r.z[:, cols] = r.cotT[:, cols].astype(F32) + scatter + grad
        return carry

    lax.fori_loop(0, b.slots, body, 0)
    r.table[3:4, :] += r.sums[1, 0:1, :]
    r.table[5 + 9 : 5 + 10, :] += r.sums[0, 0:1, :]


def put_out(b, r):
    def replace(slot, carry):
        cols = slot_columns(b, slot)
        cls = r.index[2:3, cols]
        chosen = low((iota((CLS, b.width), 0) == cls).astype(F32))
        new = low(tn(r.new_cls[...], chosen))
        r.out[:, cols] = jnp.where(cls >= 0, new.astype(F32), r.out[:, cols].astype(F32)).astype(BF16)
        return carry

    lax.fori_loop(0, b.slots, replace, 0)
    put_back(b, r, r.out, r.result, r.out_tiles)


def put_back(b, r, values, target, tiles):
    tile = tiles.shape[1]

    def body(step, carry):
        first = pl.multiple_of(step * tile, tile)
        chosen = low((iota((tile, b.tokens), 0) + first == r.index[0:1, :]).astype(F32))
        copy = pltpu.make_async_copy(tiles.at[0], target.at[pl.ds(first, tile), :], r.sem)
        tiles[0] = nt(chosen, values[...]).astype(target.dtype)
        copy.start()
        copy.wait()
        return carry

    lax.fori_loop(0, b.rows // tile, body, 0)


def backward_mlp(b, r):
    chunk = 256 if b.hidden % 512 == 0 else b.hidden // 4
    half = b.hidden // 2
    r.sums[...] = jnp.zeros_like(r.sums)

    def body(slot, carry):
        cols = slot_columns(b, slot)
        z_grad = r.z[:, cols]
        z_low = low(z_grad)
        r.zg[:, cols] = z_low
        for part in range(2):
            for at in range(0, half, chunk):
                here = part * half + at
                active = nn(r.down[part][at : at + chunk, :], z_low)
                r.g[here : here + chunk, cols] = low(
                    active * r.g[here : here + chunk, cols].astype(F32)
                )
        grad = nn(r.up[0][...], r.g[0:half, cols]) + nn(r.up[1][...], r.g[half:, cols])
        unit, scale = norm(r.y[:, cols], 0)
        ones = jnp.ones((16, b.width), BF16)
        r.sums[0] += nt(ones, low(grad))
        r.sums[1] += nt(ones, low(grad * unit))
        grad = z_grad + norm_back(grad * r.gainT[:, 1:2], unit, scale, 0)
        r.z[:, cols] = grad
        y_low = low(grad)
        r.yg[:, cols] = y_low
        r.og[:, cols] = low(nn(r.w_out[...], y_low))
        return carry

    lax.fori_loop(0, b.slots, body, 0)
    r.table[1:2, :] = r.sums[1, 0:1, :]
    r.table[5 + 4 : 5 + 5, :] = r.sums[0, 0:1, :]


def backward_attention(b, r):
    columns, head, width = b.columns, b.head, b.width
    factor = float(head) ** (-0.5)
    r.sums[...] = jnp.zeros_like(r.sums)

    def body(slot, carry):
        cols = slot_columns(b, slot)
        mask = slot_mask(b, slot)
        for h in range(HEADS):
            at_q = slice(h * head, (h + 1) * head)
            at_k = slice(columns + h * head, columns + (h + 1) * head)
            at_v = slice(2 * columns + h * head, 2 * columns + (h + 1) * head)
            q, k, v = r.qkv[at_q, cols], r.qkv[at_k, cols], r.qkv[at_v, cols]
            o_grad = r.og[at_q, cols]
            wide = jnp.exp2(tn(k, q) * (factor * LOG2E) + (mask - r.logs[h : h + 1, cols]))
            chances = low(wide)
            chance_grad = tn(v, o_grad)
            inner = jnp.sum(chance_grad * wide, 0, keepdims=True)
            score_grad = low(wide * ((chance_grad - inner) * factor))
            r.qkv[at_q, cols] = low(nn(k, score_grad))
            r.qkv[at_k, cols] = low(nt(q, score_grad))
            r.qkv[at_v, cols] = low(nt(o_grad, chances))
        grad = nn(r.w_in[...], r.qkv[:, cols])
        unit, scale = norm(r.x[:, cols].astype(F32), 0)
        ones = jnp.ones((16, b.width), BF16)
        r.sums[0] += nt(ones, low(grad))
        r.sums[1] += nt(ones, low(grad * unit))
        r.x[:, cols] = low(r.z[:, cols] + norm_back(grad * r.gainT[:, 0:1], unit, scale, 0))
        return carry

    lax.fori_loop(0, b.slots, body, 0)
    r.table[0:1, :] = r.sums[1, 0:1, :]
    r.table[5:6, :] = r.sums[0, 0:1, :]


class Place:
    def __init__(self, small, large):
        ds, dl = small.columns, large.columns
        self.first, self.size, at = {}, {}, 0
        for name, rows in (
            ("small_up", ds), ("small_down", ds), ("large_up", 2 * dl), ("large_down", 2 * dl), ("bias", 16),
            ("other", 2 * ds + 4 * dl + 16),
            ("large_cross", 4 * dl), ("small_cross", 2 * ds), ("small_enter", ds), ("small_leave", ds),
            ("large_enter", ds), ("large_leave", ds),
            ("large_heads", 4 * dl), ("small_heads", 2 * ds), ("tables", 64),
        ):
            self.first[name], self.size[name] = at, rows
            at += rows
        self.total = at

    def rows(self, name, part=0, size=None):
        first = self.first[name] + part
        return slice(first, first + (self.size[name] if size is None else size))


class CrossGrads:
    def __init__(self, own, other, place, buffer):
        self.own, self.other, self.place, self.buffer = own, other, place, buffer
        self.kept = {}

    def put(self, name, part, values):
        first = self.place.first[name] + part
        self.buffer[first : first + values.shape[0], :] = low(values)

    def cross_in(self, third, values):
        if self.other.index == 1:
            self.put("large_cross", third * self.other.columns, values)
            return
        self.kept[third] = values
        if third == 1:
            self.put("small_cross", 0, jnp.concatenate([self.kept[0], values], 1))
        if third == 2:
            self.put(
                "small_cross", self.other.columns, jnp.concatenate([values, self.kept["out"]], 1)
            )

    def cross_out(self, values):
        if self.other.index == 1:
            self.put("large_cross", 3 * self.other.columns, values)
        else:
            self.kept["out"] = values

    def enter(self, values):
        if self.own.index == 0:
            self.put("small_enter", 0, values)
        else:
            self.put("large_enter", 0, side_by_side(values))

    def leave(self, values):
        if self.own.index == 1:
            self.put("large_leave", 0, values)
        else:
            self.put("small_leave", 0, side_by_side(values))


def side_by_side(values):
    half = values.shape[0] // 2
    return jnp.concatenate([values[:half], values[half:]], 1)


def mlp_grads(b, r, place, buffer):
    half, columns = b.hidden // 2, b.columns
    name = ("small", "large")[b.index]
    r.table[5 + 5 : 5 + 6, :] = nt(r.u[b.hidden : b.hidden + 16, :], r.zg[...])[0:1]
    for part in range(2):
        base = place.first["other"] * part
        mine = slice(part * half, (part + 1) * half)
        up = nt(r.c[...], r.g[mine, :])
        first = base + place.first[name + "_up"]
        for at in range(0, half, LANES):
            buffer[first : first + columns, :] = low(up[0:columns, at : at + LANES])
            first += columns
        bias_row = base + place.first["bias"]
        bias = low(up[columns : columns + 16, :])
        first = base + place.first[name + "_down"]
        down = nt(r.u[mine, :], r.zg[...])
        if b.index == 0:
            buffer[first : first + columns, :] = low(side_by_side(down))
            r.bias_rows[part, 0:1, :] = bias[0:1, :].astype(F32)
        else:
            buffer[first : first + half, :] = low(down)
            r.bias_rows[part, 1:2, :] = bias[0:1, 0:LANES].astype(F32)
            r.bias_rows[part, 2:3, :] = bias[0:1, LANES:].astype(F32)


def bias_rows(rows, place, buffer):
    for part in range(2):
        first = place.first["other"] * part + place.first["bias"]
        buffer[first : first + 16, :] = low(rows[part])


def head_grads(b, r, place, buffer):
    columns = b.columns
    w_in = nt(r.a[...], r.qkv[...])
    w_out = nt(r.o[...], r.yg[...])
    r.table[5 + 1 : 5 + 2, :] = w_in[columns : columns + 1, 0:columns]
    r.table[5 + 2 : 5 + 3, :] = w_in[columns : columns + 1, 2 * columns : 3 * columns]
    r.table[5 + 3 : 5 + 4, :] = w_out[columns : columns + 1, :]
    if b.index == 1:
        first = place.first["large_heads"]
        for third in range(3):
            buffer[first : first + columns, :] = low(
                w_in[0:columns, third * columns : (third + 1) * columns]
            )
            first += columns
        buffer[first : first + columns, :] = low(w_out[0:columns])
    else:
        first = place.first["small_heads"]
        buffer[first : first + columns, :] = low(w_in[0:columns, 0:LANES])
        buffer[first + columns : first + 2 * columns, :] = low(
            jnp.concatenate([w_in[0:columns, LANES:], w_out[0:columns]], 1)
        )


NAMES = (
    "counts", "small_rows", "large_rows", "small_cot", "large_cot",
    "small_in", "small_out", "small_up", "small_up_bias", "small_down",
    "large_in", "large_out", "large_up", "large_up_bias", "large_down",
    "small_enter", "large_cross_in", "large_cross_out", "small_leave",
    "large_enter", "small_cross_in", "small_cross_out", "large_leave",
    "small_gains", "small_shifts", "large_gains", "large_shifts",
    "other_small_up", "other_small_up_bias", "other_small_down",
    "other_large_up", "other_large_up_bias", "other_large_down",
)


def scratch_of(b):
    d, t, h = b.columns, b.tokens, b.hidden
    return dict(
        logs=pltpu.VMEM((8, t), F32),
        out_tiles=pltpu.VMEM((2, 256, d), BF16),
        grad_tiles=pltpu.VMEM((2, 256, d), F32),
        sem=pltpu.SemaphoreType.DMA(()),
        index=pltpu.VMEM((8, t), jnp.int32),
        x=pltpu.VMEM((d, t), BF16),
        cotT=pltpu.VMEM((d, t), BF16),
        a=pltpu.VMEM((d + 16, t), BF16),
        qkv=pltpu.VMEM((3 * d, t), BF16),
        o=pltpu.VMEM((d + 16, t), BF16),
        y=pltpu.VMEM((d, t), F32),
        c=pltpu.VMEM((d + 16, t), BF16),
        u=pltpu.VMEM((h + 16, t), BF16),
        g=pltpu.VMEM((h, t), BF16),
        z=pltpu.VMEM((d, t), F32),
        n=pltpu.VMEM((d, t), BF16),
        og=pltpu.VMEM((d, t), BF16),
        sp=pltpu.VMEM((2 * STACK, t), BF16),
        maps=pltpu.VMEM((2 * STACK, d), BF16),
        cls=pltpu.VMEM((CLS, d), F32),
        cot_cls=pltpu.VMEM((CLS, d), F32),
        new_cls=pltpu.VMEM((CLS, d), BF16),
        cls_grad=pltpu.VMEM((CLS, d), F32),
        sums=pltpu.VMEM((2, 16, d), F32),
        table=pltpu.VMEM((24, d), F32),
        gainT=pltpu.VMEM((d, 128), F32),
        shiftT=pltpu.VMEM((d, 128), F32),
        up_biasT=pltpu.VMEM((h, 128), F32),
        w_inT=pltpu.VMEM((3 * d, d), BF16),
        w_outT=pltpu.VMEM((d, d), BF16),
        w_upT=pltpu.VMEM((h, d), BF16),
        w_downT=pltpu.VMEM((d, h), BF16),
    )


def columns_of(rows):
    rows = rows.astype(F32)
    return jnp.concatenate([rows, jnp.zeros((128 - rows.shape[0], rows.shape[1]), F32)], 0).T


def prepare(b, r):
    r.gainT[...] = columns_of(r.gains[...])
    r.shiftT[...] = columns_of(r.shifts[...])
    half = b.hidden // 2
    for part in range(2):
        r.up_biasT[part * half : (part + 1) * half, :] = columns_of(r.up_bias[part][...])
        r.w_upT[part * half : (part + 1) * half, :] = r.up[part][...].T
        r.w_downT[:, part * half : (part + 1) * half] = r.down[part][...].T
    r.w_inT[...] = r.w_in[...].T
    r.w_outT[...] = r.w_out[...].T
    r.a[b.columns : b.columns + 16, :] = jnp.ones((16, b.tokens), BF16)
    r.o[b.columns : b.columns + 16, :] = jnp.ones((16, b.tokens), BF16)
    r.c[b.columns : b.columns + 16, :] = jnp.ones((16, b.tokens), BF16)
    r.u[b.hidden : b.hidden + 16, :] = jnp.ones((16, b.tokens), BF16)
    r.table[...] = jnp.zeros_like(r.table)


class Refs:
    pass


def layer_kernel(small, large, place, keys, *refs):
    ins = dict(zip(NAMES, refs))
    refs = refs[len(NAMES) :]
    small_out, large_out, small_grad, large_grad, buffer = refs[:5]
    refs = refs[5:]
    groups = []
    for b, name, result, grad in (
        (small, "small", small_out, small_grad),
        (large, "large", large_out, large_grad),
    ):
        r = Refs()
        for key in keys:
            setattr(r, key, refs[0])
            refs = refs[1:]
        r.rows, r.cot = ins[name + "_rows"], ins[name + "_cot"]
        r.w_in, r.w_out = ins[name + "_in"], ins[name + "_out"]
        r.up = (ins[name + "_up"], ins["other_" + name + "_up"])
        r.down = (ins[name + "_down"], ins["other_" + name + "_down"])
        r.up_bias = (ins[name + "_up_bias"], ins["other_" + name + "_up_bias"])
        r.gains, r.shifts = ins[name + "_gains"], ins[name + "_shifts"]
        r.enter, r.leave = ins[name + "_enter"], ins[name + "_leave"]
        r.cross_in, r.cross_out = ins[name + "_cross_in"], ins[name + "_cross_out"]
        r.result, r.grad = result, grad
        r.stack = r.g.at[0 : 2 * b.columns, 0 : b.rows]
        r.out, r.zg, r.yg = r.og, r.n, r.cotT
        groups.append((b, r))
    biases = refs[0]
    (bs, rs), (bl, rl) = groups
    rs.bias_rows = rl.bias_rows = biases
    biases[...] = jnp.zeros_like(biases)
    for b, r in groups:
        prepare(b, r)
        lay_out(b, r, ins["counts"])
        bring_in(b, r)
    for b, r in groups:
        forward_attention(b, r)
    for b, r in groups:
        forward_mlp(b, r)
    cross(bs, rs, bl, rl, CrossGrads(bs, bl, place, buffer))
    cross(bl, rl, bs, rs, CrossGrads(bl, bs, place, buffer))
    for b, r in groups:
        backward_cross(b, r)
        put_out(b, r)
    for b, r in groups:
        backward_mlp(b, r)
        mlp_grads(b, r, place, buffer)
    bias_rows(biases, place, buffer)
    for b, r in reversed(groups):
        backward_attention(b, r)
        head_grads(b, r, place, buffer)
        put_back(b, r, r.x, r.grad, r.grad_tiles)
    first = place.first["tables"]
    buffer[first : first + 32, :] = jnp.concatenate(
        [low(rl.table[...]), jnp.zeros((8, LANES), BF16)], 0
    )
    buffer[first + 32 : first + 64, :] = jnp.concatenate(
        [
            jnp.concatenate([low(rs.table[...]), jnp.zeros((8, small.columns), BF16)], 0),
            jnp.zeros((32, LANES - small.columns), BF16),
        ],
        1,
    )


def run_layer(args):
    rows_s, rows_l = args[1].shape[0], args[2].shape[0]
    small = Branch(0, rows_s, args[1].shape[1], 2 * args[7].shape[1], 256, ((0, 4), (1, 5), (2,), (3,), (6,)))
    large = Branch(1, rows_l, args[2].shape[1], 2 * args[12].shape[1], 384, ((0, 1, 4), (2, 3, 5), (6,)))
    place = Place(small, large)
    keys = tuple(scratch_of(small))
    scratch = [s for b in (small, large) for s in scratch_of(b).values()]
    scratch.append(pltpu.VMEM((2, 16, LANES), F32))
    vmem = pl.BlockSpec(memory_space=pltpu.VMEM)
    return pl.pallas_call(
        functools.partial(layer_kernel, small, large, place, keys),
        out_shape=(
            jax.ShapeDtypeStruct(args[1].shape, BF16),
            jax.ShapeDtypeStruct(args[2].shape, BF16),
            jax.ShapeDtypeStruct(args[1].shape, F32),
            jax.ShapeDtypeStruct(args[2].shape, F32),
            jax.ShapeDtypeStruct((place.total, LANES), BF16),
        ),
        in_specs=[pl.BlockSpec(memory_space=pltpu.SMEM)] + [vmem] * (len(NAMES) - 1),
        out_specs=(pl.BlockSpec(memory_space=pl.ANY),) * 4 + (vmem,),
        scratch_shapes=scratch,
        compiler_params=pltpu.CompilerParams(vmem_limit_bytes=VMEM_LIMIT),
        name="layer",
    )(*args), place


def matrix(buffer, first, rows, count):
    parts = [buffer[first + i * rows : first + (i + 1) * rows] for i in range(count)]
    return jnp.concatenate(parts, 1) if count > 1 else parts[0]


def stacked(values):
    half = values.shape[1] // 2
    return jnp.concatenate([values[:, :half], values[:, half:]], 0)


def shards(*args):
    (
        small_rows, large_rows, counts, small_cot, large_cot,
        small_in, small_out, small_up, small_up_bias, small_down,
        large_in, large_out, large_up, large_up_bias, large_down,
    ) = args[:15]
    mine = (
        small_up, small_up_bias[None], small_down, large_up, large_up_bias[None], large_down,
    )
    theirs = tuple(lax.ppermute(value, "tensor", [(0, 1), (1, 0)]) for value in mine)
    inputs = (
        counts, small_rows, large_rows, small_cot, large_cot,
        small_in, small_out, small_up, mine[1], small_down,
        large_in, large_out, large_up, mine[4], large_down,
    ) + args[15:] + theirs
    (small_result, large_result, small_grad, large_grad, buffer), place = run_layer(inputs)
    other = place.first["other"]
    mlp = buffer[:other] + lax.ppermute(buffer[other : 2 * other], "tensor", [(0, 1), (1, 0)])
    mlp = lax.psum(mlp, "dp").astype(F32)
    rest = lax.psum(buffer[2 * other :], ("dp", "tensor")).astype(F32)
    first = {key: value - 2 * other for key, value in place.first.items()}
    ds, dl = small_rows.shape[1], large_rows.shape[1]
    cross_l = matrix(rest, first["large_cross"], dl, 4)
    cross_s = matrix(rest, first["small_cross"], ds, 2)
    heads_l = matrix(rest, first["large_heads"], dl, 4)
    heads_s = matrix(rest, first["small_heads"], ds, 2)
    tables = rest[first["tables"] :]
    bias = mlp[place.first["bias"] :]
    place = place.first
    return (
        small_result,
        large_result,
        small_grad,
        large_grad,
        heads_s[:, : 3 * ds],
        heads_s[:, 3 * ds :],
        matrix(mlp, place["small_up"], ds, 1),
        bias[0],
        stacked(mlp[place["small_down"] : place["small_down"] + ds]),
        heads_l[:, : 3 * dl],
        heads_l[:, 3 * dl :],
        matrix(mlp, place["large_up"], dl, 2),
        bias[1:3].reshape(-1),
        mlp[place["large_down"] : place["large_down"] + 2 * dl],
        matrix(rest, first["small_enter"], ds, 1),
        cross_l[:, : 3 * dl],
        cross_l[:, 3 * dl :],
        stacked(matrix(rest, first["small_leave"], ds, 1)),
        stacked(matrix(rest, first["large_enter"], ds, 1)),
        cross_s[:, : 3 * ds],
        cross_s[:, 3 * ds :],
        matrix(rest, first["large_leave"], ds, 1),
        tables[32:37, :ds],
        tables[37:51, :ds],
        tables[0:5],
        tables[5:19],
    )


def solution(mesh):
    both = ("dp", "tensor")
    rows = P(both, None)
    mlp = (P(None, "tensor"), P("tensor"), P("tensor", None))
    return jax.shard_map(
        shards,
        mesh=mesh,
        in_specs=(rows, rows, P(None, both), rows, rows)
        + ((P(), P()) + mlp) * 2
        + (P(),) * 12,
        out_specs=(rows,) * 4 + ((P(), P()) + mlp) * 2 + (P(),) * 12,
        check_vma=False,
    )
```

```python
import functools
import collections
import jax
import jax.numpy as jnp
from jax import lax
from jax.experimental import pallas as pl
from jax.experimental.pallas import tpu as pltpu
from jax.sharding import PartitionSpec as P

HEADS = 6
VMEM_LIMIT = 64 * 1024 * 1024
NEGATIVE = -1e30
EPSILON = 1e-06
F32, BF16 = jnp.float32, jnp.bfloat16
LANES = 384
CLS = 16
STACK = HEADS * CLS

GLOBAL_ROWS, LOCAL_ROWS = (197, 145), (37, 65)
LOG2E = 1.4426950408889634


def low(values):
    return values.astype(BF16)


def dot(left, right, left_axis, right_axis):
    return lax.dot_general(
        left, right, (((left_axis,), (right_axis,)), ((), ())), preferred_element_type=F32
    )


def nn(left, right):
    return dot(left, right, 1, 0)


def nt(left, right):
    return dot(left, right, 1, 1)


def tn(left, right):
    return dot(left, right, 0, 0)


class Branch:
    def __init__(self, index, rows, columns, hidden, width, layout):
        self.index, self.rows, self.columns, self.hidden = index, rows, columns, hidden
        self.head = columns // HEADS
        self.width, self.slots = width, len(layout)
        self.tokens = width * self.slots
        self.pieces = []
        self.bounds = []
        g_rows, l_rows = GLOBAL_ROWS[index], LOCAL_ROWS[index]
        for slot, crops in enumerate(layout):
            lane, ends = 0, []
            for crop in crops:
                length = g_rows if crop < 4 else l_rows if crop < 6 else rows - 4 * g_rows - 2 * l_rows
                self.pieces.append((slot * width + lane, length, crop))
                lane += length
                ends.append(lane)
            assert lane <= width
            self.bounds.append(ends)


def norm(values, axis):
    center = values - jnp.mean(values, axis, keepdims=True)
    scale = lax.rsqrt(jnp.mean(center * center, axis, keepdims=True) + EPSILON)
    return center * scale, scale


def norm_back(grad, unit, scale, axis):
    return scale * (
        grad
        - jnp.mean(grad, axis, keepdims=True)
        - unit * jnp.mean(grad * unit, axis, keepdims=True)
    )


def smooth_parts(values):
    chance = 0.5 + 0.5 * lax.erf(values * (0.5**0.5))
    slope = chance + values * (jnp.exp(values * values * -0.5) * 0.3989422804014327)
    return values * chance, slope


def pick(at, values):
    result = values[-1]
    for place in range(len(values) - 2, -1, -1):
        result = jnp.where(at == place, values[place], result)
    return result


def iota(shape, axis):
    return lax.broadcasted_iota(jnp.int32, shape, axis)


def slot_columns(branch, slot):
    return pl.ds(pl.multiple_of(slot * branch.width, branch.width), branch.width)


def places(counts, b):
    starts = [jnp.int32(0)] * 7
    begin, globals_seen, locals_seen = jnp.int32(0), jnp.int32(0), jnp.int32(0)
    for crop in range(6):
        rows = counts[b.index, crop]
        is_global = counts[0, crop] == GLOBAL_ROWS[0]
        for k in range(4):
            starts[k] = jnp.where(is_global & (globals_seen == k), begin, starts[k])
        for k in range(2):
            starts[4 + k] = jnp.where((~is_global) & (locals_seen == k), begin, starts[4 + k])
        begin = begin + rows
        globals_seen = globals_seen + jnp.where(is_global, 1, 0)
        locals_seen = locals_seen + jnp.where(is_global, 0, 1)
    starts[6] = begin
    return starts


def lay_out(b, r, counts):
    starts = places(counts, b)
    lane = iota((1, b.tokens), 1)
    source = jnp.full((1, b.tokens), -1, jnp.int32)
    patch = jnp.full((1, b.tokens), -1, jnp.int32)
    cls = jnp.full((1, b.tokens), -1, jnp.int32)
    for first, length, crop in b.pieces:
        inside = (lane >= first) & (lane < first + length)
        source = jnp.where(inside, lane - first + starts[crop], source)
        if crop < 6:
            patch = jnp.where(inside & (lane > first), crop, patch)
            cls = jnp.where(lane == first, crop, cls)
    r.index[0:1, :] = source
    r.index[1:2, :] = patch
    r.index[2:3, :] = cls
    at = iota((CLS, 1), 0)
    first_rows = jnp.full((CLS, 1), -1, jnp.int32)
    for crop in range(6):
        first_rows = jnp.where(at == crop, starts[crop], first_rows)
    chosen = low((iota((CLS, b.rows), 1) == first_rows).astype(F32))
    r.cot_cls[...] = nn(chosen, r.cot[...])


def bring_in(b, r):
    r.stack[0 : b.columns, :] = r.rows[...].T
    r.stack[b.columns : 2 * b.columns, :] = r.cot[...].T

    def body(slot, carry):
        cols = slot_columns(b, slot)
        chosen = low((iota((b.rows, b.width), 0) == r.index[0:1, cols]).astype(F32))
        both = nn(r.stack[...], chosen)
        r.x[:, cols] = low(both[: b.columns])
        keep = r.index[2:3, cols] < 0
        r.cotT[:, cols] = low(jnp.where(keep, both[b.columns :], 0.0))
        return carry

    lax.fori_loop(0, b.slots, body, 0)


def slot_mask(b, slot):
    ends = [pick(slot, [e[min(i, len(e) - 1)] for e in b.bounds]) for i in range(3)]

    def segment(axis):
        at = iota((b.width, b.width), axis)
        total = jnp.zeros((b.width, b.width), jnp.int32)
        for end in ends:
            total = total + (at >= end).astype(jnp.int32)
        return total

    return jnp.where(segment(0) == segment(1), 0.0, NEGATIVE)


def forward_attention(b, r):
    columns, head, width = b.columns, b.head, b.width
    factor = float(head) ** (-0.5) * LOG2E

    def body(slot, carry):
        cols = slot_columns(b, slot)
        x = r.x[:, cols].astype(F32)
        unit, scale = norm(x, 0)
        a = low(unit * r.tabT[:, 0:1] + r.tabT[:, 5:6])
        r.a[0:columns, cols] = a
        nothing = jnp.zeros((columns, 1), F32)
        bias = jnp.concatenate([r.tabT[:, 6:7], nothing, r.tabT[:, 7:8]], 0)
        r.qkv[:, cols] = low(nn(r.w_inT[...], a) + bias)
        mask = slot_mask(b, slot)
        for h in range(HEADS):
            q = r.qkv[h * head : (h + 1) * head, cols]
            k = r.qkv[columns + h * head : columns + (h + 1) * head, cols]
            v = r.qkv[2 * columns + h * head : 2 * columns + (h + 1) * head, cols]
            scores = tn(k, q) * factor + mask
            highest = jnp.max(scores, 0, keepdims=True)
            powers = jnp.exp2(scores - highest)
            total = jnp.sum(powers, 0, keepdims=True)
            r.logs[h : h + 1, cols] = highest + jnp.log2(total)
            chances = low(powers * (1.0 / total))
            r.o[h * head : (h + 1) * head, cols] = low(nn(v, chances))
        y = x + nn(r.w_outT[...], r.o[0:columns, cols]) + r.tabT[:, 8:9]
        r.y[:, cols] = y
        unit, scale = norm(y, 0)
        r.c[0:columns, cols] = low(unit * r.tabT[:, 1:2] + r.tabT[:, 9:10])
        return carry

    lax.fori_loop(0, b.slots, body, 0)


def forward_mlp(b, r):
    chunk = LANES // 2
    r.cls[...] = jnp.zeros_like(r.cls)

    def body(slot, carry):
        cols = slot_columns(b, slot)
        c = r.c[0 : b.columns, cols]
        for at in range(0, b.hidden, chunk):
            hidden = nn(r.w_upT[at : at + chunk, :], c) + r.up_biasT[at % LANES : at % LANES + chunk, at // LANES : at // LANES + 1]
            active, slope = smooth_parts(hidden)
            r.u[at : at + chunk, cols] = low(active)
            r.g[at : at + chunk, cols] = low(slope)
        z = r.y[:, cols] + nn(r.w_downT[...], r.u[0 : b.hidden, cols]) + r.tabT[:, 10:11]
        r.z[:, cols] = z
        z_low = low(z)
        r.out[:, cols] = z_low
        chosen = low((iota((CLS, b.width), 0) == r.index[2:3, cols]).astype(F32))
        r.cls[...] += nt(chosen, z_low) + nt(chosen, low(z - z_low.astype(F32)))
        unit, scale = norm(z, 0)
        r.n[:, cols] = low(unit * r.tabT[:, 3:4] + r.tabT[:, 14:15])
        return carry

    lax.fori_loop(0, b.slots, body, 0)


def head_mask(columns):
    head = columns // HEADS
    at = iota((STACK, columns), 1)
    first = iota((STACK, columns), 0) // CLS * head
    return (at >= first) & (at < first + head)


def spread(values, mask):
    return jnp.where(mask, jnp.concatenate([values] * HEADS, 0), 0.0)


def gather_heads(values, mask):
    values = jnp.where(mask, values, 0.0)
    total = values[0:CLS]
    for h in range(1, HEADS):
        total = total + values[h * CLS : (h + 1) * CLS]
    return total


def column_sum(values):
    return jnp.sum(values, 0, keepdims=True)


def cross(b, r, o, ro, g):
    wide = o.columns
    factor = float(o.head) ** (-0.5)
    mask = head_mask(wide)
    og, ob = ro.gains, ro.shifts

    def row(table, at):
        return table[at : at + 1, :].astype(F32)

    xc = r.cls[...]
    unit2, scale2 = norm(xc, 1)
    lifted, slope2 = smooth_parts(unit2 * row(r.gains, 2) + row(r.shifts, 6))
    lifted = low(lifted)
    moved = nn(lifted, r.enter[...]) + row(ob, 8)
    unit3, scale3 = norm(moved, 1)
    query_norm = low(unit3 * row(og, 3) + row(ob, 9))
    q = low(nn(query_norm, ro.cross_in[:, 0:wide]) + row(ob, 10))
    own_k = low(nn(query_norm, ro.cross_in[:, wide : 2 * wide]))
    own_v = low(nn(query_norm, ro.cross_in[:, 2 * wide : 3 * wide]) + row(ob, 11))
    q_all = spread(q.astype(F32), mask)
    k_all = spread(own_k.astype(F32), mask)
    v_all = spread(own_v.astype(F32), mask)
    key_map = low(nt(low(q_all), ro.cross_in[:, wide : 2 * wide]))
    own_score = jnp.sum(q_all * k_all, 1, keepdims=True) * factor
    usable = ro.index[1:2, :] == iota((STACK, o.tokens), 0) % CLS
    scores = jnp.where(usable, nn(key_map, ro.n[...]) * factor, NEGATIVE)
    highest = jnp.maximum(own_score, jnp.max(scores, 1, keepdims=True))
    powers = jnp.exp(scores - highest)
    own_power = jnp.exp(own_score - highest)
    inverse = 1.0 / (own_power + jnp.sum(powers, 1, keepdims=True))
    chances = powers * inverse
    own_chance = own_power * inverse
    chances_low = low(chances)
    own_low = low(own_chance).astype(F32)
    ro.sp[STACK : 2 * STACK, :] = chances_low
    total = jnp.sum(chances_low.astype(F32), 1, keepdims=True)
    mean_row = low(nt(chances_low, ro.n[...]))
    value_bias = row(ob, 11)
    mixed = own_low * v_all + nn(mean_row, ro.cross_in[:, 2 * wide : 3 * wide]) + total * value_bias
    attended = low(gather_heads(mixed, mask))
    joined = moved + nn(attended, ro.cross_out[...]) + row(ob, 12)
    unit4, scale4 = norm(joined, 1)
    spread_out, slope4 = smooth_parts(unit4 * row(og, 4) + row(ob, 13))
    spread_out = low(spread_out)
    r.new_cls[...] = low(nn(spread_out, r.leave[...]) + row(r.shifts, 7))

    new_grad = r.cot_cls[...]
    new_low = low(new_grad)
    r.table[5 + 7 : 5 + 8, :] = column_sum(new_grad)
    g.leave(tn(spread_out, new_low))
    back = nt(new_low, r.leave[...]) * slope4
    ro.table[4:5, :] = column_sum(back * unit4)
    ro.table[5 + 13 : 5 + 14, :] = column_sum(back)
    joined_grad = norm_back(back * row(og, 4), unit4, scale4, 1)
    ro.table[5 + 12 : 5 + 13, :] = column_sum(joined_grad)
    joined_low = low(joined_grad)
    g.cross_out(tn(attended, joined_low))
    mixed_grad = low(nt(joined_low, ro.cross_out[...])).astype(F32)
    mixed_all = spread(mixed_grad, mask)
    mixed_all_low = low(mixed_all)
    own_v_grad = gather_heads(own_low * mixed_all, mask)
    own_chance_grad = jnp.sum(mixed_all * v_all, 1, keepdims=True)
    value_map = low(nt(mixed_all_low, ro.cross_in[:, 2 * wide : 3 * wide]))
    chance_grad = nn(value_map, ro.n[...]) + jnp.sum(mixed_all * value_bias, 1, keepdims=True)
    inner = own_chance_grad * own_chance + jnp.sum(chance_grad * chances, 1, keepdims=True)
    score_grad = low(chances * (chance_grad - inner) * factor)
    own_score_grad = low(own_chance * (own_chance_grad - inner) * factor).astype(F32)
    ro.sp[0:STACK, :] = score_grad
    mean_back = low(nt(score_grad, ro.n[...]))
    q_grad = gather_heads(
        own_score_grad * k_all + nn(mean_back, ro.cross_in[:, wide : 2 * wide]), mask
    )
    own_k_grad = gather_heads(own_score_grad * q_all, mask)
    ro.table[5 + 10 : 5 + 11, :] = column_sum(q_grad)
    ro.table[5 + 11 : 5 + 12, :] = column_sum(own_v_grad) + column_sum(total * mixed_all)
    q_low, k_low, v_low = low(q_grad), low(own_k_grad), low(own_v_grad)
    g.cross_in(
        0,
        tn(query_norm, q_low),
    )
    g.cross_in(
        1,
        tn(
            jnp.concatenate([query_norm, mean_back], 0),
            jnp.concatenate([k_low, low(q_all)], 0),
        ),
    )
    g.cross_in(
        2,
        tn(
            jnp.concatenate([query_norm, mean_row], 0),
            jnp.concatenate([v_low, mixed_all_low], 0),
        ),
    )
    back = (
        nt(q_low, ro.cross_in[:, 0:wide])
        + nt(k_low, ro.cross_in[:, wide : 2 * wide])
        + nt(v_low, ro.cross_in[:, 2 * wide : 3 * wide])
    )
    ro.table[3:4, :] = column_sum(back * unit3)
    ro.table[5 + 9 : 5 + 10, :] = column_sum(back)
    moved_grad = joined_grad + norm_back(back * row(og, 3), unit3, scale3, 1)
    ro.table[5 + 8 : 5 + 9, :] = column_sum(moved_grad)
    moved_low = low(moved_grad)
    g.enter(tn(lifted, moved_low))
    back = nt(moved_low, r.enter[...]) * slope2
    r.table[2:3, :] = column_sum(back * unit2)
    r.table[5 + 6 : 5 + 7, :] = column_sum(back)
    r.cls_grad[...] = norm_back(back * row(r.gains, 2), unit2, scale2, 1)
    ro.maps[0:STACK, :] = key_map
    ro.maps[STACK : 2 * STACK, :] = value_map


def backward_cross(b, r):
    r.sums[...] = jnp.zeros_like(r.sums)
    maps = r.maps[...].astype(F32).T.astype(BF16)
    cls_grad = r.cls_grad[...]
    high = low(cls_grad)
    pair = jnp.concatenate([high, low(cls_grad - high.astype(F32))], 0)

    def body(slot, carry):
        cols = slot_columns(b, slot)
        z = r.z[:, cols]
        unit, scale = norm(z, 0)
        grad = nn(maps, r.sp[:, cols])
        ones = jnp.ones((16, b.width), BF16)
        r.sums[0] += nt(ones, low(grad))
        r.sums[1] += nt(ones, low(grad * unit))
        chosen = low((iota((CLS, b.width), 0) == r.index[2:3, cols]).astype(F32))
        scatter = tn(pair, jnp.concatenate([chosen, chosen], 0))
        grad = norm_back(grad * r.tabT[:, 3:4], unit, scale, 0)
        r.z[:, cols] = r.cotT[:, cols].astype(F32) + scatter + grad
        return carry

    lax.fori_loop(0, b.slots, body, 0)
    r.table[3:4, :] += r.sums[1, 0:1, :]
    r.table[5 + 9 : 5 + 10, :] += r.sums[0, 0:1, :]


def put_out(b, r):
    def replace(slot, carry):
        cols = slot_columns(b, slot)
        cls = r.index[2:3, cols]
        chosen = low((iota((CLS, b.width), 0) == cls).astype(F32))
        new = low(tn(r.new_cls[...], chosen))
        r.out[:, cols] = jnp.where(cls >= 0, new.astype(F32), r.out[:, cols].astype(F32)).astype(BF16)
        return carry

    lax.fori_loop(0, b.slots, replace, 0)
    put_back(b, r, r.out, r.result, r.out_tiles)


def put_back(b, r, values, target, tiles):
    tile = tiles.shape[1]

    def body(step, carry):
        first = pl.multiple_of(step * tile, tile)
        chosen = low((iota((tile, b.tokens), 0) + first == r.index[0:1, :]).astype(F32))
        copy = pltpu.make_async_copy(tiles.at[0], target.at[pl.ds(first, tile), :], r.sem)
        tiles[0] = nt(chosen, values[...]).astype(target.dtype)
        copy.start()
        copy.wait()
        return carry

    lax.fori_loop(0, b.rows // tile, body, 0)


def backward_mlp(b, r):
    chunk = LANES // 2
    half = b.hidden // 2
    r.sums[...] = jnp.zeros_like(r.sums)

    def body(slot, carry):
        cols = slot_columns(b, slot)
        z_grad = r.z[:, cols]
        z_low = low(z_grad)
        r.zg[:, cols] = z_low
        for part in range(2):
            for at in range(0, half, chunk):
                here = part * half + at
                active = nn(r.down[part][at : at + chunk, :], z_low)
                r.g[here : here + chunk, cols] = low(
                    active * r.g[here : here + chunk, cols].astype(F32)
                )
        grad = nn(r.up[0][...], r.g[0:half, cols]) + nn(r.up[1][...], r.g[half:, cols])
        unit, scale = norm(r.y[:, cols], 0)
        ones = jnp.ones((16, b.width), BF16)
        r.sums[0] += nt(ones, low(grad))
        r.sums[1] += nt(ones, low(grad * unit))
        grad = z_grad + norm_back(grad * r.tabT[:, 1:2], unit, scale, 0)
        r.z[:, cols] = grad
        y_low = low(grad)
        r.yg[:, cols] = y_low
        r.og[:, cols] = low(nn(r.w_out[...], y_low))
        return carry

    lax.fori_loop(0, b.slots, body, 0)
    r.table[1:2, :] = r.sums[1, 0:1, :]
    r.table[5 + 4 : 5 + 5, :] = r.sums[0, 0:1, :]


def backward_attention(b, r):
    columns, head, width = b.columns, b.head, b.width
    factor = float(head) ** (-0.5)
    r.sums[...] = jnp.zeros_like(r.sums)

    def body(slot, carry):
        cols = slot_columns(b, slot)
        mask = slot_mask(b, slot)
        for h in range(HEADS):
            at_q = slice(h * head, (h + 1) * head)
            at_k = slice(columns + h * head, columns + (h + 1) * head)
            at_v = slice(2 * columns + h * head, 2 * columns + (h + 1) * head)
            q, k, v = r.qkv[at_q, cols], r.qkv[at_k, cols], r.qkv[at_v, cols]
            o_grad = r.og[at_q, cols]
            wide = jnp.exp2(tn(k, q) * (factor * LOG2E) + (mask - r.logs[h : h + 1, cols]))
            chances = low(wide)
            chance_grad = tn(v, o_grad)
            inner = jnp.sum(chance_grad * wide, 0, keepdims=True)
            score_grad = low(wide * ((chance_grad - inner) * factor))
            r.qkv[at_q, cols] = low(nn(k, score_grad))
            r.qkv[at_k, cols] = low(nt(q, score_grad))
            r.qkv[at_v, cols] = low(nt(o_grad, chances))
        grad = nn(r.w_in[...], r.qkv[:, cols])
        unit, scale = norm(r.x[:, cols].astype(F32), 0)
        ones = jnp.ones((16, b.width), BF16)
        r.sums[0] += nt(ones, low(grad))
        r.sums[1] += nt(ones, low(grad * unit))
        r.x[:, cols] = low(r.z[:, cols] + norm_back(grad * r.tabT[:, 0:1], unit, scale, 0))
        return carry

    lax.fori_loop(0, b.slots, body, 0)
    r.table[0:1, :] = r.sums[1, 0:1, :]
    r.table[5:6, :] = r.sums[0, 0:1, :]


def bit_of(value, place):
    return (value // (1 << place)) % 2


class Links:
    def __init__(self, dp_bits):
        self.bits = ["t"] + list(range(dp_bits))

    def bind(self):
        self.dp, self.tensor = lax.axis_index("dp"), lax.axis_index("tensor")

    def bit(self, name):
        return self.tensor if name == "t" else bit_of(self.dp, name)

    def partner(self, names):
        dp, tensor = self.dp, self.tensor
        for name in names:
            if name == "t":
                tensor = 1 - self.tensor
            else:
                dp = dp + (1 - 2 * bit_of(self.dp, name)) * (1 << name)
        return (dp, tensor)


def subsets(names):
    for number in range(1, 1 << len(names)):
        yield number, [name for at, name in enumerate(names) if number >> at & 1]


class Pool:
    def __init__(self):
        self.rows, self.copies, self.signals = 0, 0, 0

    def signal(self):
        self.signals += 1
        return self.signals - 1

    def take(self, rows, copies):
        at = (self.rows, self.copies)
        self.rows, self.copies = self.rows + rows, self.copies + copies
        return at


class Group:
    def __init__(self, pool, first, rows, phases, apart=None):
        self.first, self.rows, self.apart = first, rows, apart
        self.steps, size, bases = [], rows, 1 if apart is None else 2
        self.frees = {}
        phases = list(phases)
        while phases:
            names = phases.pop(0)
            count = 1 << len(names)
            if names == ["t"] and apart is not None:
                kind, bases = "merge", 1
                at = pool.take(size, 1)
                self.steps.append((kind, names, size, at, 1))
            elif size % (16 * count) == 0:
                at = pool.take(bases * (count - 1) * (size // count), 2 * bases * (count - 1))
                self.steps.append(("halve", names, size, at, bases))
                self.frees[len(self.steps) - 1] = pool.signal()
                size //= count
            elif len(names) > 1:
                phases = [[name] for name in names] + phases
            else:
                at = pool.take(bases * (count - 1) * size, bases * (count - 1))
                self.steps.append(("full", names, size, at, bases))
        self.plan = [("reduce", step, self.frees.get(at)) for at, step in enumerate(self.steps)]
        self.plan += [("gather",) + step[1:] for step in reversed(self.plan) if step[2] is not None]

    def bind(self, links, buffer, received, send, recv, free):
        self.links, self.buffer, self.received = links, buffer, received
        self.send, self.recv, self.free = send, recv, free
        self.lo, self.at, self.flight, self.offsets = 0, 0, [], {}
        return self

    def chunk(self, names, flipped):
        index = 0
        for place, name in enumerate(names):
            bit = self.links.bit(name)
            index = index + (1 - bit if name in flipped else bit) * (1 << place)
        return index

    def rows_at(self, base, first, size):
        return pl.ds(pl.multiple_of(base + first, 16), size)

    def copy(self, source, target, sem, partner):
        return pltpu.make_async_remote_copy(
            src_ref=source,
            dst_ref=target,
            send_sem=self.send.at[sem],
            recv_sem=self.recv.at[sem],
            device_id=partner,
            device_id_type=pl.DeviceIdType.MESH,
        )

    def bases(self, count):
        return (self.first, self.apart)[:count]

    def begin(self):
        if self.at == len(self.plan):
            return
        way, (kind, names, size, (row, sem), count), free = self.plan[self.at]
        flight = []
        if kind == "merge":
            source = self.buffer.at[self.rows_at(self.apart, self.lo, size), :]
            target = self.received.at[pl.ds(row, size), :]
            flight.append(self.copy(source, target, sem, self.links.partner(names)))
        elif way == "reduce":
            part = size // (1 << len(names)) if kind == "halve" else size
            for base in self.bases(count):
                for number, flipped in subsets(names):
                    first = self.lo
                    if kind == "halve":
                        first = first + self.chunk(names, flipped) * part
                    source = self.buffer.at[self.rows_at(base, first, part), :]
                    target = self.received.at[pl.ds(row, part), :]
                    flight.append(self.copy(source, target, sem, self.links.partner(flipped)))
                    row, sem = row + part, sem + 1
        else:
            part = size // (1 << len(names))
            before = self.offsets[(kind, tuple(names), size)]
            pl.semaphore_wait(self.free.at[free], (1 << len(names)) - 1)
            sem = sem + count * ((1 << len(names)) - 1)
            first = before + self.chunk(names, []) * part
            for number, flipped in subsets(names):
                mine = self.buffer.at[self.rows_at(self.first, first, part), :]
                flight.append(self.copy(mine, mine, sem, self.links.partner(flipped)))
                sem += 1
        for copy in flight:
            copy.start()
        self.flight = flight

    def end(self):
        if not self.flight:
            return
        way, (kind, names, size, (row, sem), count), free = self.plan[self.at]
        for copy in self.flight:
            copy.wait()
        self.flight = []
        self.at += 1
        if way == "gather":
            return
        if kind == "merge":
            self.add(self.first, self.lo, size, [row])
            return
        part = size
        parts = (1 << len(names)) - 1
        if kind == "halve":
            part = size // (parts + 1)
            self.offsets[(kind, tuple(names), size)] = self.lo
            self.lo = self.lo + self.chunk(names, []) * part
            for number, flipped in subsets(names):
                pl.semaphore_signal(
                    self.free.at[free],
                    inc=1,
                    device_id=self.links.partner(flipped),
                    device_id_type=pl.DeviceIdType.MESH,
                )
        for base in self.bases(count):
            self.add(base, self.lo, part, [row + i * part for i in range(parts)])
            row += parts * part

    def add(self, base, first, size, rows):
        block = 16
        for candidate in (32, 48, 64, 80, 96):
            if size % candidate == 0:
                block = candidate

        def body(step, carry):
            here = self.rows_at(base, first + step * block, block)
            terms = [self.buffer[here, :].astype(F32)]
            for row in rows:
                at = pl.ds(pl.multiple_of(row + step * block, 16), block)
                terms.append(self.received[at, :].astype(F32))
            while len(terms) > 1:
                terms = [a + b for a, b in zip(terms[0::2], terms[1::2])]
            self.buffer[here, :] = low(terms[0])
            return carry

        lax.fori_loop(0, size // block, body, 0)

    def advance(self):
        self.end()
        self.begin()

    @property
    def done(self):
        return self.at == len(self.plan)


def meet(links, partners):
    barrier = pltpu.get_barrier_semaphore()
    for names in partners:
        pl.semaphore_signal(
            barrier, inc=1, device_id=links.partner(names), device_id_type=pl.DeviceIdType.MESH
        )
    pl.semaphore_wait(barrier, len(partners))


class Swap:
    def __init__(self, links, pairs, sends, receives):
        self.links, self.pairs, self.sends, self.receives = links, pairs, sends, receives

    def copies(self, step):
        result = []
        for at, (mine, theirs) in enumerate(self.pairs):
            half = mine.shape[0] // 2
            rows = pl.ds(pl.multiple_of(self.links.bit(0) * half, 16), half)
            result.append(
                pltpu.make_async_remote_copy(
                    src_ref=(mine if step == 0 else theirs).at[rows, :],
                    dst_ref=theirs.at[rows, :],
                    send_sem=self.sends.at[step, at],
                    recv_sem=self.receives.at[step, at],
                    device_id=self.links.partner(["t"] if step == 0 else [0]),
                    device_id_type=pl.DeviceIdType.MESH,
                )
            )
        return result

    def start(self, step):
        for copy in self.copies(step):
            copy.start()

    def wait(self, step):
        for copy in self.copies(step):
            copy.wait()


class Place:
    def __init__(self, small, large):
        ds, dl = small.columns, large.columns
        self.first, self.size, at = {}, {}, 0
        for name, rows in (
            ("small_up", ds), ("small_down", ds), ("large_up", 2 * dl), ("large_down", 2 * dl),
            ("other", 2 * ds + 4 * dl),
            ("large_cross", 4 * dl), ("small_enter", ds), ("small_leave", ds),
            ("large_enter", ds), ("large_leave", ds), ("small_cross", 2 * ds),
            ("small_heads", 2 * ds), ("large_heads", 4 * dl), ("tables", 64),
        ):
            self.first[name], self.size[name] = at, rows
            at += rows
        self.total = at

    def rows(self, name, part=0, size=None):
        first = self.first[name] + part
        return slice(first, first + (self.size[name] if size is None else size))


class CrossGrads:
    def __init__(self, own, other, place, buffer):
        self.own, self.other, self.place, self.buffer = own, other, place, buffer
        self.kept = {}

    def put(self, name, part, values):
        first = self.place.first[name] + part
        self.buffer[first : first + values.shape[0], :] = low(values)

    def cross_in(self, third, values):
        if self.other.index == 1:
            self.put("large_cross", third * self.other.columns, values)
            return
        self.kept[third] = values
        if third == 1:
            self.put("small_cross", 0, jnp.concatenate([self.kept[0], values], 1))
        if third == 2:
            self.put(
                "small_cross", self.other.columns, jnp.concatenate([values, self.kept["out"]], 1)
            )

    def cross_out(self, values):
        if self.other.index == 1:
            self.put("large_cross", 3 * self.other.columns, values)
        else:
            self.kept["out"] = values

    def enter(self, values):
        if self.own.index == 0:
            self.put("small_enter", 0, values)
        else:
            self.put("large_enter", 0, side_by_side(values))

    def leave(self, values):
        if self.own.index == 1:
            self.put("large_leave", 0, values)
        else:
            self.put("small_leave", 0, side_by_side(values))


def side_by_side(values):
    half = values.shape[0] // 2
    return jnp.concatenate([values[:half], values[half:]], 1)


def mlp_grads(b, r, place, buffer):
    half, columns = b.hidden // 2, b.columns
    name = ("small", "large")[b.index]
    r.table[5 + 5 : 5 + 6, :] = nt(r.u[b.hidden : b.hidden + 16, :], r.zg[...])[0:1]
    for part in range(2):
        base = place.first["other"] * part
        mine = slice(part * half, (part + 1) * half)
        up = nt(r.c[...], r.g[mine, :])
        first = base + place.first[name + "_up"]
        for at in range(0, half, LANES):
            buffer[first : first + columns, :] = low(up[0:columns, at : at + LANES])
            first += columns
        bias = up[columns : columns + 1, :]
        first = base + place.first[name + "_down"]
        down = nt(r.u[mine, :], r.zg[...])
        if b.index == 0:
            buffer[first : first + columns, :] = low(side_by_side(down))
            r.bias_rows[part, 0:1, :] = bias
        else:
            buffer[first : first + half, :] = low(down)
            r.bias_rows[part, 1:2, :] = bias[:, 0:LANES]
            r.bias_rows[part, 2:3, :] = bias[:, LANES:]


def head_grads(b, r, place, buffer):
    columns = b.columns
    w_in = nt(r.a[...], r.qkv[...])
    w_out = nt(r.o[...], r.yg[...])
    r.table[5 + 1 : 5 + 2, :] = w_in[columns : columns + 1, 0:columns]
    r.table[5 + 2 : 5 + 3, :] = w_in[columns : columns + 1, 2 * columns : 3 * columns]
    r.table[5 + 3 : 5 + 4, :] = w_out[columns : columns + 1, :]
    if b.index == 1:
        first = place.first["large_heads"]
        for third in range(3):
            buffer[first : first + columns, :] = low(
                w_in[0:columns, third * columns : (third + 1) * columns]
            )
            first += columns
        buffer[first : first + columns, :] = low(w_out[0:columns])
    else:
        first = place.first["small_heads"]
        buffer[first : first + columns, :] = low(w_in[0:columns, 0:LANES])
        buffer[first + columns : first + 2 * columns, :] = low(
            jnp.concatenate([w_in[0:columns, LANES:], w_out[0:columns]], 1)
        )


NAMES = (
    "counts", "small_rows", "large_rows", "small_cot", "large_cot",
    "small_in", "small_out", "small_up", "small_down",
    "large_in", "large_out", "large_up", "large_down",
    "small_enter", "large_cross_in", "large_cross_out", "small_leave",
    "large_enter", "small_cross_in", "small_cross_out", "large_leave",
    "small_gains", "small_shifts", "large_gains", "large_shifts", "up_biases",
)
OUTS = (
    "small_out", "large_out", "small_rows", "large_rows",
    "small_heads_in", "small_heads_out", "small_up", "small_up_bias", "small_down",
    "large_heads_in", "large_heads_out", "large_up", "large_up_bias", "large_down",
    "small_enter", "large_cross_in", "large_cross_out", "small_leave",
    "large_enter", "small_cross_in", "small_cross_out", "large_leave",
    "small_gains", "small_shifts", "large_gains", "large_shifts",
)
BY_COPY = frozenset((
    "small_out", "large_out", "small_rows", "large_rows", "large_heads_in", "large_heads_out", "large_up", "large_down",
    "large_cross_in", "large_cross_out", "small_enter", "large_leave", "small_up",
    "small_leave", "large_enter", "small_down",
))


def scratch_of(b):
    d, t, h = b.columns, b.tokens, b.hidden
    return dict(
        logs=pltpu.VMEM((8, t), F32),
        out_tiles=pltpu.VMEM((1, 256, d), BF16),
        grad_tiles=pltpu.VMEM((1, 256, d), F32),
        sem=pltpu.SemaphoreType.DMA(()),
        index=pltpu.VMEM((8, t), jnp.int32),
        x=pltpu.VMEM((d, t), BF16),
        cotT=pltpu.VMEM((d, t), BF16),
        a=pltpu.VMEM((d + 16, t), BF16),
        qkv=pltpu.VMEM((3 * d, t), BF16),
        o=pltpu.VMEM((d + 16, t), BF16),
        y=pltpu.VMEM((d, t), F32),
        c=pltpu.VMEM((d + 16, t), BF16),
        u=pltpu.VMEM((h + 16, t), BF16),
        g=pltpu.VMEM((h, t), BF16),
        z=pltpu.VMEM((d, t), F32),
        n=pltpu.VMEM((d, t), BF16),
        og=pltpu.VMEM((d, t), BF16),
        sp=pltpu.VMEM((2 * STACK, t), BF16),
        maps=pltpu.VMEM((2 * STACK, d), BF16),
        cls=pltpu.VMEM((CLS, d), F32),
        cot_cls=pltpu.VMEM((CLS, d), F32),
        new_cls=pltpu.VMEM((CLS, d), BF16),
        cls_grad=pltpu.VMEM((CLS, d), F32),
        sums=pltpu.VMEM((2, 16, d), F32),
        table=pltpu.VMEM((24, d), F32),
        tabT=pltpu.VMEM((d, 128), F32),
        up_biasT=pltpu.VMEM((LANES, 128), F32),
        w_inT=pltpu.VMEM((3 * d, d), BF16),
        w_outT=pltpu.VMEM((d, d), BF16),
        w_upT=pltpu.VMEM((h, d), BF16),
        w_downT=pltpu.VMEM((d, h), BF16),
        other_up=pltpu.VMEM((d, h // 2), BF16),
        other_down=pltpu.VMEM((h // 2, d), BF16),
    )


def columns_of(rows):
    rows = rows.astype(F32)
    return jnp.concatenate([rows, jnp.zeros((128 - rows.shape[0], rows.shape[1]), F32)], 0).T


def prepare(b, r):
    r.tabT[...] = columns_of(jnp.concatenate([r.gains[...].astype(F32), r.shifts[...].astype(F32)], 0))
    r.w_inT[...] = r.w_in[...].T
    r.w_outT[...] = r.w_out[...].T
    r.a[b.columns : b.columns + 16, :] = jnp.ones((16, b.tokens), BF16)
    r.o[b.columns : b.columns + 16, :] = jnp.ones((16, b.tokens), BF16)
    r.c[b.columns : b.columns + 16, :] = jnp.ones((16, b.tokens), BF16)
    r.u[b.hidden : b.hidden + 16, :] = jnp.ones((16, b.tokens), BF16)
    r.table[...] = jnp.zeros_like(r.table)


def prepare_mlp(b, r):
    half = b.hidden // 2
    for part in range(2):
        biases = columns_of(r.up_bias[part][0:16, :])
        for at in range(0, half, LANES):
            place = b.index + at // LANES
            first = part * half + at
            r.up_biasT[:, first // LANES : first // LANES + 1] = biases[:, place : place + 1]
        r.w_upT[part * half : (part + 1) * half, :] = r.up[part][...].T
        r.w_downT[:, part * half : (part + 1) * half] = r.down[part][...].T


class Refs:
    pass


class Plan:
    def __init__(self, place, small, large, dp):
        ds, dl, first = small.columns, large.columns, place.first
        self.dp_bits = dp.bit_length() - 1
        assert dp == 1 << self.dp_bits
        far = [list(range(at, min(at + 2, self.dp_bits))) for at in range(2, self.dp_bits, 2)]
        pool = Pool()
        other = first["other"]
        cross = 2560
        both = [[0], ["t", 1]] + far
        self.large_mlp = Group(
            pool, first["large_up"], 4 * dl, [[0], ["t"], [1]] + far, other + first["large_up"]
        )
        self.small_mlp = Group(
            pool, first["small_up"], 2 * ds, [[0], ["t"], [1]] + far, other + first["small_up"]
        )
        begin = first["large_cross"]
        self.cross_a = Group(pool, begin, cross // 2, [[0], [1], ["t"]] + far)
        self.cross_b = Group(pool, begin + cross // 2, cross // 2, [[0], ["t"], [1]] + far)
        self.large_heads = Group(pool, first["large_heads"], 4 * dl, both)
        tail = begin + cross
        self.small_heads = Group(pool, tail, first["large_heads"] - tail, both)
        self.tables = Group(pool, first["tables"], 64, both)
        self.pool = pool
        self.groups = (
            self.large_mlp, self.small_mlp, self.cross_a, self.cross_b, self.large_heads, self.small_heads, self.tables,
        )
        met = [[0], ["t"], [1]]
        for phase in [["t", 1]] + far:
            met += [flipped for number, flipped in subsets(phase)]
        self.met = []
        for names in met:
            if names not in self.met:
                self.met.append(names)


def drain(groups):
    while any(not group.done for group in groups):
        for group in groups:
            group.end()
            group.begin()


def layer_kernel(small, large, place, plan, keys, *refs):
    ins = dict(zip(NAMES, refs))
    refs = refs[len(NAMES) :]
    outs = dict(zip(OUTS, refs))
    refs = refs[len(OUTS) :]
    groups = []
    links = Links(plan.dp_bits)
    links.bind()
    for b, name in ((small, "small"), (large, "large")):
        r = Refs()
        for key in keys:
            setattr(r, key, refs[0])
            refs = refs[1:]
        r.rows, r.cot = ins[name + "_rows"], ins[name + "_cot"]
        r.w_in, r.w_out = ins[name + "_in"], ins[name + "_out"]
        r.up = (ins[name + "_up"], r.other_up)
        r.down = (ins[name + "_down"], r.other_down)
        r.gains, r.shifts = ins[name + "_gains"], ins[name + "_shifts"]
        r.enter, r.leave = ins[name + "_enter"], ins[name + "_leave"]
        r.cross_in, r.cross_out = ins[name + "_cross_in"], ins[name + "_cross_out"]
        r.result, r.grad = outs[name + "_out"], outs[name + "_rows"]
        r.stack = r.g.at[0 : 2 * b.columns, 0 : b.rows]
        r.out, r.zg, r.yg = r.og, r.n, r.cotT
        groups.append((b, r))
    biases, other_biases, buffer, received, send, recv, free, swap_send, swap_recv, narrow, out_sem, in_sem = refs
    (bs, rs), (bl, rl) = groups
    for b, r in groups:
        r.bias_rows = biases
        r.up_bias = (ins["up_biases"], other_biases)
    biases[...] = jnp.zeros_like(biases)
    for group in plan.groups:
        group.bind(links, buffer, received, send, recv, free)
    swap = Swap(
        links,
        (
            (ins["large_up"], rl.other_up),
            (ins["large_down"], rl.other_down),
            (ins["small_up"], rs.other_up),
            (ins["small_down"], rs.other_down),
            (ins["up_biases"], other_biases),
        ),
        swap_send,
        swap_recv,
    )
    arrivals = []
    for at, name in enumerate(("large_rows", "large_cot")):
        target = rl.u.at[0 : bl.rows, at * bl.columns : (at + 1) * bl.columns]
        arrivals.append(pltpu.make_async_copy(ins[name], target, in_sem.at[at]))
        arrivals[-1].start()
    rl.rows = rl.u.at[0 : bl.rows, 0 : bl.columns]
    rl.cot = rl.u.at[0 : bl.rows, bl.columns : 2 * bl.columns]
    meet(links, plan.met)
    swap.start(0)
    for b, r in groups:
        prepare(b, r)
        if b is bl:
            for copy in arrivals:
                copy.wait()
        lay_out(b, r, ins["counts"])
        bring_in(b, r)
    forward_attention(bl, rl)
    swap.wait(0)
    swap.start(1)
    forward_attention(bs, rs)
    swap.wait(1)
    for b, r in groups:
        prepare_mlp(b, r)
    for b, r in groups:
        forward_mlp(b, r)
    cross(bs, rs, bl, rl, CrossGrads(bs, bl, place, buffer))
    cross(bl, rl, bs, rs, CrossGrads(bl, bs, place, buffer))
    for b, r in groups:
        backward_cross(b, r)
        put_out(b, r)
    for b, r in groups:
        backward_mlp(b, r)
        mlp_grads(b, r, place, buffer)
    for b, r in reversed(groups):
        backward_attention(b, r)
        head_grads(b, r, place, buffer)
        put_back(b, r, r.x, r.grad, r.grad_tiles)
    put_tables(links, place, buffer, rs, rl, biases)
    drain(plan.groups)
    emit(links, place, buffer, outs, rs, rl, narrow, out_sem)


def put_tables(links, place, buffer, rs, rl, biases):
    ds = rs.table.shape[1]
    own, other = biases[0, 0:8, :], biases[1, 0:8, :]
    first = links.tensor == 0
    rows = [
        rl.table[...],
        jnp.concatenate([rs.table[...], jnp.zeros((24, LANES - ds), F32)], 1),
        jnp.where(first, own, other),
        jnp.where(first, other, own),
    ]
    buffer[place.rows("tables"), :] = low(jnp.concatenate(rows, 0))


def unstacked(values):
    half = values.shape[1] // 2
    return jnp.concatenate([values[:, :half], values[:, half:]], 0)


def emit(links, place, buffer, outs, rs, rl, narrow, sems):
    ds, dl = rs.table.shape[1], rl.table.shape[1]

    def read(name, part, rows):
        first = place.first[name] + part
        return buffer[first : first + rows, :].astype(F32)

    flights = {}

    def send(at, pairs):
        flights[at] = []
        for number, (source, target) in enumerate(pairs):
            copy = pltpu.make_async_copy(source, target, sems.at[at, number])
            copy.start()
            flights[at].append(copy)

    def wait(at):
        for copy in flights[at]:
            copy.wait()

    for at, stage, name in ((0, rl.y, "large_cross"), (1, rl.z, "large_heads")):
        for third in range(3):
            stage[:, third * dl : (third + 1) * dl] = read(name, third * dl, dl)
        send(at, [(stage, outs[name + "_in"])])
    for at, name in enumerate(("small_enter", "large_leave", "small_up")):
        rs.y[:, at * LANES : (at + 1) * LANES] = read(name, 0, ds)
    send(
        2,
        [
            (rs.y.at[:, at * LANES : (at + 1) * LANES], outs[name])
            for at, name in enumerate(("small_enter", "large_leave", "small_up"))
        ],
    )
    for name in ("small_heads", "small_cross"):
        second = read(name, ds, ds)
        outs[name + "_in"][:, 0:LANES] = read(name, 0, ds)
        outs[name + "_in"][:, LANES:] = second[:, 0:ds]
        outs[name + "_out"][...] = second[:, ds:]
    for at, name in enumerate(("small_leave", "large_enter", "small_down")):
        if at:
            wait(3)
        narrow[...] = unstacked(read(name, 0, ds))
        send(3, [(narrow, outs[name])])
    wait(0)
    for third in range(2):
        rl.y[:, third * dl : (third + 1) * dl] = read("large_up", third * dl, dl)
    rl.y[:, 2 * dl :] = read("large_cross", 3 * dl, dl)
    send(
        0,
        [
            (rl.y.at[:, 0 : 2 * dl], outs["large_up"]),
            (rl.y.at[:, 2 * dl :], outs["large_cross_out"]),
        ],
    )
    wait(1)
    rl.z[:, 0:dl] = read("large_heads", 3 * dl, dl)
    for part in range(2):
        rl.z[:, (part + 1) * dl : (part + 2) * dl] = read("large_down", part * dl, dl)
    send(
        1,
        [
            (rl.z.at[:, 0:dl], outs["large_heads_out"]),
            (rl.z.at[:, dl : 2 * dl], outs["large_down"].at[0:dl, :]),
            (rl.z.at[:, 2 * dl :], outs["large_down"].at[dl:, :]),
        ],
    )
    tables = buffer[place.rows("tables"), :].astype(F32)
    outs["large_gains"][...] = tables[0:5]
    outs["large_shifts"][...] = tables[5:19]
    outs["small_gains"][...] = tables[24:29, 0:ds]
    outs["small_shifts"][...] = tables[29:43, 0:ds]
    mine = jnp.where(links.tensor == 0, tables[48:56], tables[56:64])
    outs["small_up_bias"][...] = mine[0:1]
    outs["large_up_bias"][...] = jnp.concatenate([mine[1:2], mine[2:3]], 1)
    for at in range(4):
        wait(at)


def run_layer(args, dp):
    (
        small_rows, large_rows, counts, small_cot, large_cot,
        small_in, small_out, small_up, small_up_bias, small_down,
        large_in, large_out, large_up, large_up_bias, large_down,
    ) = args[:15]
    ds, dl = small_rows.shape[1], large_rows.shape[1]
    small = Branch(0, small_rows.shape[0], ds, 2 * small_up.shape[1], 256, ((0, 4), (1, 5), (2,), (3,), (6,)))
    large = Branch(1, large_rows.shape[0], dl, 2 * large_up.shape[1], 384, ((0, 1, 4), (2, 3, 5), (6,)))
    place = Place(small, large)
    plan = Plan(place, small, large, dp)
    biases = jnp.concatenate([small_up_bias, large_up_bias]).reshape(-1, LANES)
    biases = jnp.pad(biases, ((0, 32 - biases.shape[0]), (0, 0)))
    inputs = (
        counts, small_rows, large_rows, small_cot, large_cot,
        small_in, small_out, small_up, small_down,
        large_in, large_out, large_up, large_down,
    ) + args[15:] + (biases,)
    keys = tuple(scratch_of(small))
    scratch = [s for b in (small, large) for s in scratch_of(b).values()]
    scratch += [
        pltpu.VMEM((2, 16, LANES), F32),
        pltpu.VMEM((32, LANES), BF16),
        pltpu.VMEM((place.total, LANES), BF16),
        pltpu.VMEM((plan.pool.rows, LANES), BF16),
        pltpu.SemaphoreType.DMA((plan.pool.copies,)),
        pltpu.SemaphoreType.DMA((plan.pool.copies,)),
        pltpu.SemaphoreType.REGULAR((plan.pool.signals,)),
        pltpu.SemaphoreType.DMA((2, 5)),
        pltpu.SemaphoreType.DMA((2, 5)),
        pltpu.VMEM((2 * ds, ds), F32),
        pltpu.SemaphoreType.DMA((4, 3)),
        pltpu.SemaphoreType.DMA((2,)),
    ]
    shape = jax.ShapeDtypeStruct
    shapes = dict(
        small_out=shape(small_rows.shape, BF16),
        large_out=shape(large_rows.shape, BF16),
        small_rows=shape(small_rows.shape, F32),
        large_rows=shape(large_rows.shape, F32),
        small_up_bias=shape((1, small_up_bias.shape[0]), F32),
        large_up_bias=shape((1, large_up_bias.shape[0]), F32),
    )
    order = OUTS[4:]
    for name, value in zip(order, args[5:]):
        shapes.setdefault(name, shape(value.shape, F32))
    vmem, hbm = pl.BlockSpec(memory_space=pltpu.VMEM), pl.BlockSpec(memory_space=pl.ANY)
    results = pl.pallas_call(
        functools.partial(layer_kernel, small, large, place, plan, keys),
        out_shape=tuple(shapes[name] for name in OUTS),
        in_specs=[pl.BlockSpec(memory_space=pltpu.SMEM)]
        + [hbm if name in ("large_rows", "large_cot") else vmem for name in NAMES[1:]],
        out_specs=tuple(hbm if name in BY_COPY else vmem for name in OUTS),
        scratch_shapes=scratch,
        compiler_params=pltpu.CompilerParams(
            vmem_limit_bytes=VMEM_LIMIT, collective_id=0, has_side_effects=True
        ),
        name="layer",
    )(*inputs)
    return tuple(
        value.reshape(-1) if name.endswith("_bias") else value for name, value in zip(OUTS, results)
    )


def solution(mesh):
    both = ("dp", "tensor")
    rows = P(both, None)
    mlp = (P(None, "tensor"), P("tensor"), P("tensor", None))

    def shards(*args):
        return run_layer(args, mesh.shape["dp"])

    return jax.shard_map(
        shards,
        mesh=mesh,
        in_specs=(rows, rows, P(None, both), rows, rows)
        + ((P(), P()) + mlp) * 2
        + (P(),) * 12,
        out_specs=(rows,) * 4 + ((P(), P()) + mlp) * 2 + (P(),) * 12,
        check_vma=False,
    )
```

```python
import functools
import collections
import jax
import jax.numpy as jnp
from jax import lax
from jax.experimental import pallas as pl
from jax.experimental.pallas import tpu as pltpu
from jax.sharding import PartitionSpec as P

HEADS = 6
VMEM_LIMIT = 64 * 1024 * 1024
NEGATIVE = -1e30
EPSILON = 1e-06
F32, BF16 = jnp.float32, jnp.bfloat16
LANES = 384
CLS = 16
STACK = HEADS * CLS

GLOBAL_ROWS, LOCAL_ROWS = (197, 145), (37, 65)
BLOCK = 32
LOG2E = 1.4426950408889634


def low(values):
    return values.astype(BF16)


def dot(left, right, left_axis, right_axis):
    return lax.dot_general(
        left, right, (((left_axis,), (right_axis,)), ((), ())), preferred_element_type=F32
    )


def nn(left, right):
    return dot(left, right, 1, 0)


def nt(left, right):
    return dot(left, right, 1, 1)


def tn(left, right):
    return dot(left, right, 0, 0)


class Branch:
    def __init__(self, index, rows, columns, hidden, width, layout):
        self.index, self.rows, self.columns, self.hidden = index, rows, columns, hidden
        self.head = columns // HEADS
        self.width, self.slots = width, len(layout)
        self.tokens = width * self.slots
        self.pieces = []
        self.bounds = []
        g_rows, l_rows = GLOBAL_ROWS[index], LOCAL_ROWS[index]
        for slot, crops in enumerate(layout):
            lane, ends = 0, []
            for crop in crops:
                length = g_rows if crop < 4 else l_rows if crop < 6 else rows - 4 * g_rows - 2 * l_rows
                self.pieces.append((slot * width + lane, length, crop))
                lane += length
                ends.append(lane)
            assert lane <= width
            self.bounds.append(ends)


def norm(values, axis):
    center = values - jnp.mean(values, axis, keepdims=True)
    scale = lax.rsqrt(jnp.mean(center * center, axis, keepdims=True) + EPSILON)
    return center * scale, scale


def fold(values):
    total = values[0:8]
    for at in range(8, values.shape[0], 8):
        total = total + values[at : at + 8]
    return total


def fold_lanes(values):
    total = values[:, 0:128]
    for at in range(128, values.shape[1], 128):
        total = total + values[:, at : at + 128]
    return total


def chunks(columns):
    return [slice(at, at + BLOCK) for at in range(0, columns, BLOCK)]


def norm_columns(load, columns, keep):
    total = sum(fold(load(rows)) for rows in chunks(columns))
    mean = jnp.sum(total, 0, keepdims=True) * (1.0 / columns)
    spread = 0.0
    for rows in chunks(columns):
        center = load(rows) - mean
        spread = spread + fold(center * center)
    spread = jnp.sum(spread, 0, keepdims=True) * (1.0 / columns)
    scale = lax.rsqrt(spread + EPSILON)
    keep(mean, scale)
    return mean, scale


def norm_columns_back(load, grad, columns, mean, scale, gain, sums, store):
    first = second = 0.0
    for rows in chunks(columns):
        unit = (load(rows) - mean) * scale
        back = grad(rows)
        both = back * unit
        sums[0, rows, :] += fold_lanes(back)
        sums[1, rows, :] += fold_lanes(both)
        first = first + fold(back * gain(rows))
        second = second + fold(both * gain(rows))
    first = jnp.sum(first, 0, keepdims=True) * (1.0 / columns)
    second = jnp.sum(second, 0, keepdims=True) * (1.0 / columns)
    for rows in chunks(columns):
        unit = (load(rows) - mean) * scale
        store(rows, scale * (grad(rows) * gain(rows) - first - unit * second))


def norm_back(grad, unit, scale, axis):
    return scale * (
        grad
        - jnp.mean(grad, axis, keepdims=True)
        - unit * jnp.mean(grad * unit, axis, keepdims=True)
    )


def smooth_parts(values):
    chance = 0.5 + 0.5 * lax.erf(values * (0.5**0.5))
    slope = chance + values * (jnp.exp(values * values * -0.5) * 0.3989422804014327)
    return values * chance, slope


def pick(at, values):
    if isinstance(at, int):
        return values[at]
    result = values[-1]
    for place in range(len(values) - 2, -1, -1):
        result = jnp.where(at == place, values[place], result)
    return result


def iota(shape, axis):
    return lax.broadcasted_iota(jnp.int32, shape, axis)


def each_slot(branch, body, between=None):
    if between is None:
        lax.fori_loop(0, branch.slots, lambda slot, carry: body(slot) or carry, 0)
        return
    for slot in range(branch.slots):
        body(slot)
        between(slot)


def slot_columns(branch, slot):
    if isinstance(slot, int):
        return slice(slot * branch.width, (slot + 1) * branch.width)
    return pl.ds(pl.multiple_of(slot * branch.width, branch.width), branch.width)


def places(counts, b):
    starts = [jnp.int32(0)] * 7
    begin, globals_seen, locals_seen = jnp.int32(0), jnp.int32(0), jnp.int32(0)
    for crop in range(6):
        rows = counts[b.index, crop]
        is_global = counts[0, crop] == GLOBAL_ROWS[0]
        for k in range(4):
            starts[k] = jnp.where(is_global & (globals_seen == k), begin, starts[k])
        for k in range(2):
            starts[4 + k] = jnp.where((~is_global) & (locals_seen == k), begin, starts[4 + k])
        begin = begin + rows
        globals_seen = globals_seen + jnp.where(is_global, 1, 0)
        locals_seen = locals_seen + jnp.where(is_global, 0, 1)
    starts[6] = begin
    return starts


def lay_out(b, r, counts):
    starts = places(counts, b)
    lane = iota((1, b.tokens), 1)
    source = jnp.full((1, b.tokens), -1, jnp.int32)
    patch = jnp.full((1, b.tokens), -1, jnp.int32)
    cls = jnp.full((1, b.tokens), -1, jnp.int32)
    for first, length, crop in b.pieces:
        inside = (lane >= first) & (lane < first + length)
        source = jnp.where(inside, lane - first + starts[crop], source)
        if crop < 6:
            patch = jnp.where(inside & (lane > first), crop, patch)
            cls = jnp.where(lane == first, crop, cls)
    r.index[0:1, :] = source
    r.index[1:2, :] = patch
    r.index[2:3, :] = cls
    at = iota((CLS, 1), 0)
    first_rows = jnp.full((CLS, 1), -1, jnp.int32)
    for crop in range(6):
        first_rows = jnp.where(at == crop, starts[crop], first_rows)
    chosen = low((iota((CLS, b.rows), 1) == first_rows).astype(F32))
    r.cot_cls[...] = nt(chosen, r.cot[...])


def bring_in(b, r):
    def body(slot):
        cols = slot_columns(b, slot)
        chosen = low((iota((b.rows, b.width), 0) == r.index[0:1, cols]).astype(F32))
        r.x[:, cols] = low(nn(r.rows[...], chosen))
        keep = r.index[2:3, cols] < 0
        r.cotT[:, cols] = low(jnp.where(keep, nn(r.cot[...], chosen), 0.0))

    each_slot(b, body)


def slot_mask(b, slot):
    ends = [pick(slot, [e[min(i, len(e) - 1)] for e in b.bounds]) for i in range(3)]

    def segment(axis):
        at = iota((b.width, b.width), axis)
        total = jnp.zeros((b.width, b.width), jnp.int32)
        for end in ends[: max(len(e) for e in b.bounds)]:
            total = total + (at >= end).astype(jnp.int32)
        return total

    return jnp.where(segment(0) == segment(1), 0.0, NEGATIVE)


def squares(b, refs):
    result = []
    for ref in refs:
        for row in range(0, ref.shape[0] - b.width + 1, b.width):
            for lane in range(0, ref.shape[1] - b.width + 1, b.width):
                result.append(ref.at[row : row + b.width, lane : lane + b.width])
    return result


def parts_of(b, h):
    first = [part * b.columns + h * b.head for part in range(3)]
    return [slice(at, at + b.head) for at in first]


def forward_attention(b, r, wide_work, low_work, between=None):
    columns, width = b.columns, b.width
    factor = float(b.head) ** (-0.5) * LOG2E
    wide, lows = squares(b, wide_work), squares(b, low_work)
    many = min(len(wide), len(lows), HEADS)
    mask_ref = r.mask.at[0:width, 0:width]

    def body(slot):
        cols = slot_columns(b, slot)

        def tokens(rows):
            return r.x[rows, cols].astype(F32)

        def keep(at):
            def put(mean, scale):
                r.stats[at : at + 1, cols] = mean
                r.stats[at + 1 : at + 2, cols] = scale

            return put

        mean, scale = norm_columns(tokens, columns, keep(0))
        for rows in chunks(columns):
            unit = (tokens(rows) - mean) * scale
            r.a[rows, cols] = low(unit * r.tabT[rows, 0:1] + r.tabT[rows, 5:6])
        a = r.a[0:columns, cols]
        for third, bias in ((0, 6), (1, None), (2, 7)):
            rows = slice(third * columns, (third + 1) * columns)
            product = nn(r.w_inT[rows, :], a)
            r.qkv[rows, cols] = low(product if bias is None else product + r.tabT[:, bias : bias + 1])
        mask_ref[...] = slot_mask(b, slot)
        for begin in range(0, HEADS, many):
            heads = range(begin, min(begin + many, HEADS))
            for h in heads:
                q, k, v = parts_of(b, h)
                wide[h - begin][...] = tn(r.qkv[k, cols], r.qkv[q, cols])
            for h in heads:
                scores = wide[h - begin][...] * factor + mask_ref[...]
                highest = jnp.max(scores, 0, keepdims=True)
                powers = jnp.exp2(scores - highest)
                total = jnp.sum(powers, 0, keepdims=True)
                r.logs[h : h + 1, cols] = highest + jnp.log2(total)
                lows[h - begin][...] = low(powers * (1.0 / total))
            for h in heads:
                q, k, v = parts_of(b, h)
                r.o[q, cols] = low(nn(r.qkv[v, cols], lows[h - begin][...]))
        r.y[:, cols] = (
            r.x[:, cols].astype(F32) + nn(r.w_outT[...], r.o[0:columns, cols]) + r.tabT[:, 8:9]
        )
        mean, scale = norm_columns(lambda rows: r.y[rows, cols], columns, keep(2))
        for rows in chunks(columns):
            unit = (r.y[rows, cols] - mean) * scale
            r.c[rows, cols] = low(unit * r.tabT[rows, 1:2] + r.tabT[rows, 9:10])

    each_slot(b, body, between)


def forward_mlp(b, r, between=None):
    chunk = LANES // 2
    columns = b.columns
    r.cls[...] = jnp.zeros_like(r.cls)

    def body(slot):
        cols = slot_columns(b, slot)
        c = r.c[0:columns, cols]
        for at in range(0, b.hidden, chunk):
            bias = r.tabT[at % columns : at % columns + chunk, 19 + at // columns : 20 + at // columns]
            active, slope = smooth_parts(nn(r.w_upT[at : at + chunk, :], c) + bias)
            r.u[at : at + chunk, cols] = low(active)
            r.g[at : at + chunk, cols] = low(slope)
        r.z[:, cols] = r.y[:, cols] + nn(r.w_downT[...], r.u[0 : b.hidden, cols]) + r.tabT[:, 10:11]

        def keep(mean, scale):
            r.stats[4:5, cols] = mean
            r.stats[5:6, cols] = scale

        mean, scale = norm_columns(lambda rows: r.z[rows, cols], columns, keep)
        for rows in chunks(columns):
            z = r.z[rows, cols]
            r.out[rows, cols] = low(z)
            r.n[rows, cols] = low((z - mean) * scale * r.tabT[rows, 3:4] + r.tabT[rows, 14:15])
        chosen = low((iota((CLS, b.width), 0) == r.index[2:3, cols]).astype(F32))
        rest = low(r.z[:, cols] - r.out[:, cols].astype(F32))
        r.cls[...] += nt(chosen, r.out[:, cols]) + nt(chosen, rest)

    each_slot(b, body, between)


def backward_cross(b, r, work, between=None):
    columns, width = b.columns, b.width
    r.sums[...] = jnp.zeros_like(r.sums)
    cls_grad = r.cls_grad[...]
    high = low(cls_grad)
    pair = jnp.concatenate([high, low(cls_grad - high.astype(F32))], 0)
    maps, pair = r.maps[...].T, pair.T

    def body(slot):
        cols = slot_columns(b, slot)
        work[0:columns, 0:width] = nn(maps, r.sp[:, cols])
        chosen = low((iota((CLS, width), 0) == r.index[2:3, cols]).astype(F32))
        work[0:columns, width : 2 * width] = nn(pair, jnp.concatenate([chosen, chosen], 0))

        def store(rows, back):
            r.z[rows, cols] = r.cotT[rows, cols].astype(F32) + work[rows, width : 2 * width] + back

        norm_columns_back(
            lambda rows: r.z[rows, cols],
            lambda rows: work[rows, 0:width],
            columns,
            r.stats[4:5, cols],
            r.stats[5:6, cols],
            lambda rows: r.tabT[rows, 3:4],
            r.sums.at[:, 0:columns, :],
            store,
        )

    each_slot(b, body, between)
    r.table[3:4, :] += row_sum(r.sums[1, 0:columns, :])
    r.table[5 + 9 : 5 + 10, :] += row_sum(r.sums[0, 0:columns, :])


def row_sum(values):
    return jnp.sum(values.T, 0, keepdims=True)


def put_out(b, r):
    def replace(slot):
        cols = slot_columns(b, slot)
        cls = r.index[2:3, cols]
        chosen = low((iota((CLS, b.width), 0) == cls).astype(F32))
        new = tn(r.new_cls[...], chosen)
        r.out[:, cols] = jnp.where(cls >= 0, new, r.out[:, cols].astype(F32)).astype(BF16)

    each_slot(b, replace)
    put_back(b, r, r.out)


def put_back(b, r, values):
    tile = 256

    def body(step, carry):
        first = pl.multiple_of(step * tile, tile)
        chosen = low((iota((tile, b.tokens), 0) + first == r.index[0:1, :]).astype(F32))
        if b.index == 0:
            r.staged[:, pl.ds(first, tile)] = low(nt(values[...], chosen))
        else:
            r.staged[pl.ds(first, tile), :] = low(nt(chosen, values[...]))
        return carry

    lax.fori_loop(0, b.rows // tile, body, 0)


def backward_mlp(b, r, work, between=None):
    half, columns, width = b.hidden // 2, b.columns, b.width
    r.sums[...] = jnp.zeros_like(r.sums)

    def body(slot):
        cols = slot_columns(b, slot)
        r.zg[:, cols] = low(r.z[:, cols])
        z_low = r.zg[:, cols]
        for part in range(2):
            mine = slice(part * half, (part + 1) * half)
            r.g[mine, cols] = low(r.down_times(part, z_low) * r.g[mine, cols].astype(F32))
        work[0:columns, 0:width] = nn(r.up[0][...], r.g[0:half, cols]) + nn(
            r.up[1][...], r.g[half:, cols]
        )

        def store(rows, back):
            grad = r.z[rows, cols] + back
            r.z[rows, cols] = grad
            r.yg[rows, cols] = low(grad)

        norm_columns_back(
            lambda rows: r.y[rows, cols],
            lambda rows: work[rows, 0:width],
            columns,
            r.stats[2:3, cols],
            r.stats[3:4, cols],
            lambda rows: r.tabT[rows, 1:2],
            r.sums.at[:, 0:columns, :],
            store,
        )
        r.og_rows(slot, slice(0, columns))[...] = low(nn(r.w_out[...], r.yg[:, cols]))

    each_slot(b, body, between)
    r.table[1:2, :] = row_sum(r.sums[1, 0:columns, :])
    r.table[5 + 4 : 5 + 5, :] = row_sum(r.sums[0, 0:columns, :])


def backward_attention(b, r, wide_work, low_work, more_work, between=None):
    columns, width = b.columns, b.width
    factor = float(b.head) ** (-0.5)
    wide, lows, more = squares(b, wide_work), squares(b, low_work), squares(b, more_work)
    many = min(len(wide) // 2, len(lows), len(more), HEADS)
    mask_ref = r.mask.at[0:width, 0:width]

    def body(slot):
        cols = slot_columns(b, slot)
        mask_ref[...] = slot_mask(b, slot)
        for begin in range(0, HEADS, many):
            heads = range(begin, min(begin + many, HEADS))
            for h in heads:
                q, k, v = parts_of(b, h)
                wide[h - begin][...] = tn(r.qkv[k, cols], r.qkv[q, cols])
            for h in heads:
                q, k, v = parts_of(b, h)
                wide[many + h - begin][...] = tn(r.qkv[v, cols], r.og_rows(slot, q)[...])
            for h in heads:
                chances = jnp.exp2(
                    wide[h - begin][...] * (factor * LOG2E)
                    + (mask_ref[...] - r.logs[h : h + 1, cols])
                )
                lows[h - begin][...] = low(chances)
                chance_grad = wide[many + h - begin][...]
                inner = jnp.sum(chance_grad * chances, 0, keepdims=True)
                more[h - begin][...] = low(chances * ((chance_grad - inner) * factor))
            for h in heads:
                q, k, v = parts_of(b, h)
                q_low, k_low = r.qkv[q, cols], r.qkv[k, cols]
                score_grad = more[h - begin][...]
                r.qkv[q, cols] = low(nn(k_low, score_grad))
                r.qkv[k, cols] = low(nt(q_low, score_grad))
                r.qkv[v, cols] = low(nt(r.og_rows(slot, q)[...], lows[h - begin][...]))

    each_slot(b, body, between)


def backward_first_norm(b, r, work):
    columns, width = b.columns, b.width
    r.sums[...] = jnp.zeros_like(r.sums)

    def body(slot):
        cols = slot_columns(b, slot)
        work[0:columns, 0:width] = nn(r.w_in[...], r.qkv[:, cols])

        def store(rows, back):
            r.x[rows, cols] = low(r.z[rows, cols] + back)

        norm_columns_back(
            lambda rows: r.x[rows, cols].astype(F32),
            lambda rows: work[rows, 0:width],
            columns,
            r.stats[0:1, cols],
            r.stats[1:2, cols],
            lambda rows: r.tabT[rows, 0:1],
            r.sums.at[:, 0:columns, :],
            store,
        )

    each_slot(b, body)
    r.table[0:1, :] = row_sum(r.sums[1, 0:columns, :])
    r.table[5:6, :] = row_sum(r.sums[0, 0:columns, :])
def head_mask(columns):
    head = columns // HEADS
    at = iota((STACK, columns), 1)
    first = iota((STACK, columns), 0) // CLS * head
    return (at >= first) & (at < first + head)


def spread(values, mask):
    return jnp.where(mask, jnp.concatenate([values] * HEADS, 0), 0.0)


def gather_heads(values, mask):
    values = jnp.where(mask, values, 0.0)
    total = values[0:CLS]
    for h in range(1, HEADS):
        total = total + values[h * CLS : (h + 1) * CLS]
    return total


def column_sum(values):
    return jnp.sum(values, 0, keepdims=True)


def cross(b, r, o, ro, g):
    wide = o.columns
    factor = float(o.head) ** (-0.5)
    mask = head_mask(wide)
    og, ob = ro.gains, ro.shifts

    def row(table, at):
        return table[at : at + 1, :].astype(F32)

    enter_on, enter_back, leave_on, leave_back = (nn, nt, nt, nn) if b.index == 0 else (nt, nn, nn, nt)

    xc = r.cls[...]
    yield
    unit2, scale2 = norm(xc, 1)
    lifted, slope2 = smooth_parts(unit2 * row(r.gains, 2) + row(r.shifts, 6))
    lifted = low(lifted)
    yield
    moved = enter_on(lifted, r.enter[...]) + row(ob, 8)
    yield
    unit3, scale3 = norm(moved, 1)
    query_norm = low(unit3 * row(og, 3) + row(ob, 9))
    yield
    q = low(nn(query_norm, ro.cross_in[:, 0:wide]) + row(ob, 10))
    own_k = low(nn(query_norm, ro.cross_in[:, wide : 2 * wide]))
    own_v = low(nn(query_norm, ro.cross_in[:, 2 * wide : 3 * wide]) + row(ob, 11))
    q_all = spread(q.astype(F32), mask)
    k_all = spread(own_k.astype(F32), mask)
    v_all = spread(own_v.astype(F32), mask)
    yield
    key_map = low(nt(low(q_all), ro.cross_in[:, wide : 2 * wide]))
    yield
    own_score = jnp.sum(q_all * k_all, 1, keepdims=True) * factor
    usable = ro.index[1:2, :] == iota((STACK, o.tokens), 0) % CLS
    yield
    scores = jnp.where(usable, nn(key_map, ro.n[...]) * factor, NEGATIVE)
    yield
    highest = jnp.maximum(own_score, jnp.max(scores, 1, keepdims=True))
    powers = jnp.exp(scores - highest)
    own_power = jnp.exp(own_score - highest)
    yield
    inverse = 1.0 / (own_power + jnp.sum(powers, 1, keepdims=True))
    chances = powers * inverse
    own_chance = own_power * inverse
    chances_low = low(chances)
    own_low = low(own_chance).astype(F32)
    ro.sp[STACK : 2 * STACK, :] = chances_low
    total = jnp.sum(chances_low.astype(F32), 1, keepdims=True)
    yield
    mean_row = low(nt(chances_low, ro.n[...]))
    value_bias = row(ob, 11)
    yield
    mixed = own_low * v_all + nn(mean_row, ro.cross_in[:, 2 * wide : 3 * wide]) + total * value_bias
    attended = low(gather_heads(mixed, mask))
    yield
    joined = moved + nn(attended, ro.cross_out[...]) + row(ob, 12)
    yield
    unit4, scale4 = norm(joined, 1)
    spread_out, slope4 = smooth_parts(unit4 * row(og, 4) + row(ob, 13))
    spread_out = low(spread_out)
    r.new_cls[...] = low(leave_on(spread_out, r.leave[...]) + row(r.shifts, 7))

    yield
    new_grad = r.cot_cls[...]
    new_low = low(new_grad)
    r.table[5 + 7 : 5 + 8, :] = column_sum(new_grad)
    yield
    g.leave(tn(new_low, spread_out) if b.index == 0 else tn(spread_out, new_low))
    yield
    back = leave_back(new_low, r.leave[...]) * slope4
    ro.table[4:5, :] = column_sum(back * unit4)
    ro.table[5 + 13 : 5 + 14, :] = column_sum(back)
    yield
    joined_grad = norm_back(back * row(og, 4), unit4, scale4, 1)
    ro.table[5 + 12 : 5 + 13, :] = column_sum(joined_grad)
    joined_low = low(joined_grad)
    yield
    g.cross_out(tn(attended, joined_low))
    yield
    mixed_grad = low(nt(joined_low, ro.cross_out[...])).astype(F32)
    yield
    mixed_all = spread(mixed_grad, mask)
    mixed_all_low = low(mixed_all)
    own_v_grad = gather_heads(own_low * mixed_all, mask)
    own_chance_grad = jnp.sum(mixed_all * v_all, 1, keepdims=True)
    yield
    value_map = low(nt(mixed_all_low, ro.cross_in[:, 2 * wide : 3 * wide]))
    yield
    chance_grad = nn(value_map, ro.n[...]) + jnp.sum(mixed_all * value_bias, 1, keepdims=True)
    yield
    inner = own_chance_grad * own_chance + jnp.sum(chance_grad * chances, 1, keepdims=True)
    score_grad = low(chances * (chance_grad - inner) * factor)
    own_score_grad = low(own_chance * (own_chance_grad - inner) * factor).astype(F32)
    ro.sp[0:STACK, :] = score_grad
    yield
    mean_back = low(nt(score_grad, ro.n[...]))
    yield
    q_grad = gather_heads(
        own_score_grad * k_all + nn(mean_back, ro.cross_in[:, wide : 2 * wide]), mask
    )
    own_k_grad = gather_heads(own_score_grad * q_all, mask)
    ro.table[5 + 10 : 5 + 11, :] = column_sum(q_grad)
    ro.table[5 + 11 : 5 + 12, :] = column_sum(own_v_grad) + column_sum(total * mixed_all)
    q_low, k_low, v_low = low(q_grad), low(own_k_grad), low(own_v_grad)
    yield
    g.cross_in(
        0,
        tn(query_norm, q_low),
    )
    yield
    g.cross_in(
        1,
        tn(
            jnp.concatenate([query_norm, mean_back], 0),
            jnp.concatenate([k_low, low(q_all)], 0),
        ),
    )
    yield
    g.cross_in(
        2,
        tn(
            jnp.concatenate([query_norm, mean_row], 0),
            jnp.concatenate([v_low, mixed_all_low], 0),
        ),
    )
    yield
    back = (
        nt(q_low, ro.cross_in[:, 0:wide])
        + nt(k_low, ro.cross_in[:, wide : 2 * wide])
        + nt(v_low, ro.cross_in[:, 2 * wide : 3 * wide])
    )
    ro.table[3:4, :] = column_sum(back * unit3)
    ro.table[5 + 9 : 5 + 10, :] = column_sum(back)
    yield
    moved_grad = joined_grad + norm_back(back * row(og, 3), unit3, scale3, 1)
    ro.table[5 + 8 : 5 + 9, :] = column_sum(moved_grad)
    moved_low = low(moved_grad)
    yield
    g.enter(tn(lifted, moved_low) if b.index == 0 else tn(moved_low, lifted))
    yield
    back = enter_back(moved_low, r.enter[...]) * slope2
    r.table[2:3, :] = column_sum(back * unit2)
    r.table[5 + 6 : 5 + 7, :] = column_sum(back)
    r.cls_grad[...] = norm_back(back * row(r.gains, 2), unit2, scale2, 1)
    ro.maps[0:STACK, :] = key_map
    ro.maps[STACK : 2 * STACK, :] = value_map


def bit_of(value, place):
    return (value // (1 << place)) % 2


class Links:
    def __init__(self, dp_bits):
        self.bits = ["t"] + list(range(dp_bits))

    def bind(self, solo=None):
        self.dp = self.tensor = 0
        if solo is None:
            self.dp, self.tensor = lax.axis_index("dp"), lax.axis_index("tensor")

    def bit(self, name):
        return self.tensor if name == "t" else bit_of(self.dp, name)

    def partner(self, names):
        dp, tensor = self.dp, self.tensor
        for name in names:
            if name == "t":
                tensor = 1 - self.tensor
            else:
                dp = dp + (1 - 2 * bit_of(self.dp, name)) * (1 << name)
        return (dp, tensor)


def subsets(names):
    for number in range(1, 1 << len(names)):
        yield number, [name for at, name in enumerate(names) if number >> at & 1]


class Pool:
    def __init__(self):
        self.rows, self.copies, self.signals = 0, 0, 0

    def signal(self):
        self.signals += 1
        return self.signals - 1

    def take(self, rows, copies):
        at = (self.rows, self.copies)
        self.rows, self.copies = self.rows + rows, self.copies + copies
        return at


class Group:
    def __init__(self, pool, first, rows, phases, apart=None):
        self.first, self.rows, self.apart = first, rows, apart
        self.steps, size, bases = [], rows, 1 if apart is None else 2
        self.frees = {}
        phases = list(phases)
        while phases:
            names = phases.pop(0)
            count = 1 << len(names)
            if names == ["t"] and apart is not None:
                kind, bases = "merge", 1
                at = pool.take(size, 1)
                self.steps.append((kind, names, size, at, 1))
            elif size % (16 * count) == 0:
                at = pool.take(bases * (count - 1) * (size // count), 2 * bases * (count - 1))
                self.steps.append(("halve", names, size, at, bases))
                self.frees[len(self.steps) - 1] = pool.signal()
                size //= count
            elif len(names) > 1:
                phases = [[name] for name in names] + phases
            else:
                at = pool.take(bases * (count - 1) * size, bases * (count - 1))
                self.steps.append(("full", names, size, at, bases))
        self.plan = [("reduce", step, self.frees.get(at)) for at, step in enumerate(self.steps)]
        self.plan += [("gather",) + step[1:] for step in reversed(self.plan) if step[2] is not None]

    def bind(self, links, buffer, received, send, recv, free):
        self.links, self.buffer, self.received = links, buffer, received
        self.send, self.recv, self.free = send, recv, free
        self.lo, self.at, self.flight, self.offsets = 0, 0, [], {}
        return self

    def chunk(self, names, flipped):
        index = 0
        for place, name in enumerate(names):
            bit = self.links.bit(name)
            index = index + (1 - bit if name in flipped else bit) * (1 << place)
        return index

    def rows_at(self, base, first, size):
        return pl.ds(pl.multiple_of(base + first, 16), size)

    def copy(self, source, target, sem, partner):
        return pltpu.make_async_remote_copy(
            src_ref=source,
            dst_ref=target,
            send_sem=self.send.at[sem],
            recv_sem=self.recv.at[sem],
            device_id=partner,
            device_id_type=pl.DeviceIdType.MESH,
        )

    def bases(self, count):
        return (self.first, self.apart)[:count]

    def begin(self):
        if self.at == len(self.plan):
            return
        way, (kind, names, size, (row, sem), count), free = self.plan[self.at]
        flight = []
        if kind == "merge":
            source = self.buffer.at[self.rows_at(self.apart, self.lo, size), :]
            target = self.received.at[pl.ds(row, size), :]
            flight.append(self.copy(source, target, sem, self.links.partner(names)))
        elif way == "reduce":
            part = size // (1 << len(names)) if kind == "halve" else size
            for base in self.bases(count):
                for number, flipped in subsets(names):
                    first = self.lo
                    if kind == "halve":
                        first = first + self.chunk(names, flipped) * part
                    source = self.buffer.at[self.rows_at(base, first, part), :]
                    target = self.received.at[pl.ds(row, part), :]
                    flight.append(self.copy(source, target, sem, self.links.partner(flipped)))
                    row, sem = row + part, sem + 1
        else:
            part = size // (1 << len(names))
            before = self.offsets[(kind, tuple(names), size)]
            pl.semaphore_wait(self.free.at[free], (1 << len(names)) - 1)
            sem = sem + count * ((1 << len(names)) - 1)
            first = before + self.chunk(names, []) * part
            for number, flipped in subsets(names):
                mine = self.buffer.at[self.rows_at(self.first, first, part), :]
                flight.append(self.copy(mine, mine, sem, self.links.partner(flipped)))
                sem += 1
        for copy in flight:
            copy.start()
        self.flight = flight

    def end(self):
        if not self.flight:
            return
        way, (kind, names, size, (row, sem), count), free = self.plan[self.at]
        for copy in self.flight:
            copy.wait()
        self.flight = []
        self.at += 1
        if way == "gather":
            return
        if kind == "merge":
            self.add(self.first, self.lo, size, [row])
            return
        part = size
        parts = (1 << len(names)) - 1
        if kind == "halve":
            part = size // (parts + 1)
            self.offsets[(kind, tuple(names), size)] = self.lo
            self.lo = self.lo + self.chunk(names, []) * part
            for number, flipped in subsets(names):
                pl.semaphore_signal(
                    self.free.at[free],
                    inc=1,
                    device_id=self.links.partner(flipped),
                    device_id_type=pl.DeviceIdType.MESH,
                )
        for base in self.bases(count):
            self.add(base, self.lo, part, [row + i * part for i in range(parts)])
            row += parts * part

    def add(self, base, first, size, rows):
        block = 16
        for candidate in (32, 48, 64, 80, 96):
            if size % candidate == 0:
                block = candidate

        def body(step, carry):
            here = self.rows_at(base, first + step * block, block)
            terms = [self.buffer[here, :].astype(F32)]
            for row in rows:
                at = pl.ds(pl.multiple_of(row + step * block, 16), block)
                terms.append(self.received[at, :].astype(F32))
            while len(terms) > 1:
                terms = [a + b for a, b in zip(terms[0::2], terms[1::2])]
            self.buffer[here, :] = low(terms[0])
            return carry

        lax.fori_loop(0, size // block, body, 0)

    def advance(self):
        self.end()
        self.begin()

    @property
    def done(self):
        return self.at == len(self.plan)


def meet(links, partners):
    barrier = pltpu.get_barrier_semaphore()
    for names in partners:
        pl.semaphore_signal(
            barrier, inc=1, device_id=links.partner(names), device_id_type=pl.DeviceIdType.MESH
        )
    pl.semaphore_wait(barrier, len(partners))


class Swap:
    def __init__(self, links, pairs, sends, receives):
        self.links, self.pairs, self.sends, self.receives = links, pairs, sends, receives

    def copies(self, step):
        result = []
        for at, (mine, theirs) in enumerate(self.pairs):
            half = mine.shape[0] // 2
            rows = pl.ds(pl.multiple_of(self.links.bit(0) * half, 16), half)
            result.append(
                pltpu.make_async_remote_copy(
                    src_ref=(mine if step == 0 else theirs).at[rows, :],
                    dst_ref=theirs.at[rows, :],
                    send_sem=self.sends.at[step, at],
                    recv_sem=self.receives.at[step, at],
                    device_id=self.links.partner(["t"] if step == 0 else [0]),
                    device_id_type=pl.DeviceIdType.MESH,
                )
            )
        return result

    def start(self, step):
        for copy in self.copies(step):
            copy.start()

    def wait(self, step):
        for copy in self.copies(step):
            copy.wait()


class Place:
    def __init__(self, small, large):
        ds, dl = small.columns, large.columns
        self.first, self.size, at = {}, {}, 0
        for name, rows in (
            ("small_up", ds), ("small_down", ds), ("large_up", 2 * dl), ("large_down", 2 * dl),
            ("other", 2 * ds + 4 * dl),
            ("large_cross", 4 * dl), ("small_enter", ds), ("small_leave", ds),
            ("large_enter", ds), ("large_leave", ds), ("small_cross", 2 * ds),
            ("small_heads", 2 * ds), ("large_heads", 4 * dl), ("tables", 64),
        ):
            self.first[name], self.size[name] = at, rows
            at += rows
        self.total = at

    def rows(self, name, part=0, size=None):
        first = self.first[name] + part
        return slice(first, first + (self.size[name] if size is None else size))


class CrossGrads:
    def __init__(self, own, other, place, buffer):
        self.own, self.other, self.place, self.buffer = own, other, place, buffer
        self.kept = {}

    def put(self, name, part, values):
        first = self.place.first[name] + part
        self.buffer[first : first + values.shape[0], :] = low(values)

    def cross_in(self, third, values):
        if self.other.index == 1:
            self.put("large_cross", third * self.other.columns, values)
            return
        self.kept[third] = values
        if third == 1:
            self.put("small_cross", 0, jnp.concatenate([self.kept[0], values], 1))
        if third == 2:
            self.put(
                "small_cross", self.other.columns, jnp.concatenate([values, self.kept["out"]], 1)
            )

    def cross_out(self, values):
        if self.other.index == 1:
            self.put("large_cross", 3 * self.other.columns, values)
        else:
            self.kept["out"] = values

    def enter(self, values):
        if self.own.index == 0:
            self.put("small_enter", 0, values)
        else:
            self.put("large_enter", 0, values)

    def leave(self, values):
        if self.own.index == 1:
            self.put("large_leave", 0, values)
        else:
            self.put("small_leave", 0, values)


def mlp_grads(b, r, place, buffer):
    half, columns = b.hidden // 2, b.columns
    name = ("small", "large")[b.index]
    r.table[5 + 5 : 5 + 6, :] = nt(r.u[b.hidden : b.hidden + 16, :], r.zg[...])[0:1]
    for part in range(2):
        base = place.first["other"] * part
        mine = slice(part * half, (part + 1) * half)
        up = nt(r.c[...], r.g[mine, :])
        first = base + place.first[name + "_up"]
        for at in range(0, half, LANES):
            buffer[first : first + columns, :] = low(up[0:columns, at : at + LANES])
            first += columns
        bias = up[columns : columns + 1, :]
        first = base + place.first[name + "_down"]
        if b.index == 0:
            buffer[first : first + columns, :] = low(nt(r.zg[...], r.u[mine, :]))
            r.bias_rows[part, 0:1, :] = bias
        else:
            buffer[first : first + half, :] = low(nt(r.u[mine, :], r.zg[...]))
            r.bias_rows[part, 1:2, :] = bias[:, 0:LANES]
            r.bias_rows[part, 2:3, :] = bias[:, LANES:]


def head_grads(b, r, place, buffer):
    columns = b.columns
    w_in = nt(r.a[...], r.qkv[...])
    w_out = nt(r.o[...], r.yg[...])
    r.table[5 + 1 : 5 + 2, :] = w_in[columns : columns + 1, 0:columns]
    r.table[5 + 2 : 5 + 3, :] = w_in[columns : columns + 1, 2 * columns : 3 * columns]
    r.table[5 + 3 : 5 + 4, :] = w_out[columns : columns + 1, :]
    if b.index == 1:
        first = place.first["large_heads"]
        for third in range(3):
            buffer[first : first + columns, :] = low(
                w_in[0:columns, third * columns : (third + 1) * columns]
            )
            first += columns
        buffer[first : first + columns, :] = low(w_out[0:columns])
    else:
        first = place.first["small_heads"]
        buffer[first : first + columns, :] = low(w_in[0:columns, 0:LANES])
        buffer[first + columns : first + 2 * columns, :] = low(
            jnp.concatenate([w_in[0:columns, LANES:], w_out[0:columns]], 1)
        )


NAMES = (
    "counts", "small_rows", "large_rows", "small_cot", "large_cot",
    "small_in", "small_out", "small_up", "small_down",
    "large_in", "large_out", "large_up", "large_down",
    "small_enter", "large_cross_in", "large_cross_out", "small_leave",
    "large_enter", "small_cross_in", "small_cross_out", "large_leave",
    "small_gains", "small_shifts", "large_gains", "large_shifts", "up_biases",
)
OUTS = (
    "small_out", "large_out", "small_rows", "large_rows",
    "small_heads_in", "small_heads_out", "small_up", "small_up_bias", "small_down",
    "large_heads_in", "large_heads_out", "large_up", "large_up_bias", "large_down",
    "small_enter", "large_cross_in", "large_cross_out", "small_leave",
    "large_enter", "small_cross_in", "small_cross_out", "large_leave",
    "small_gains", "small_shifts", "large_gains", "large_shifts",
)
def scratch_of(b):
    d, t, h = b.columns, b.tokens, b.hidden
    scratch = dict(
        logs=pltpu.VMEM((8, t), F32),
        stats=pltpu.VMEM((8, t), F32),
        index=pltpu.VMEM((8, t), jnp.int32),
        x=pltpu.VMEM((d, t), BF16),
        cotT=pltpu.VMEM((d, t), BF16),
        a=pltpu.VMEM((d + 16, t), BF16),
        qkv=pltpu.VMEM((3 * d, t), BF16),
        o=pltpu.VMEM((d + 16, t), BF16),
        y=pltpu.VMEM((d, t), F32),
        c=pltpu.VMEM((d + 16, t), BF16),
        u=pltpu.VMEM((h + 16, t), BF16),
        g=pltpu.VMEM((h, t), BF16),
        z=pltpu.VMEM((d, t), F32),
        n=pltpu.VMEM((d, t), BF16),
        out=pltpu.VMEM((d, t), BF16),
        sp=pltpu.VMEM((2 * STACK, t), BF16),
        maps=pltpu.VMEM((2 * STACK, d), BF16),
        cls=pltpu.VMEM((CLS, d), F32),
        cot_cls=pltpu.VMEM((CLS, d), F32),
        new_cls=pltpu.VMEM((CLS, d), BF16),
        cls_grad=pltpu.VMEM((CLS, d), F32),
        table=pltpu.VMEM((24, d), F32),
        tabT=pltpu.VMEM((d, 128), F32),
        w_inT=pltpu.VMEM((3 * d, d), BF16),
        w_outT=pltpu.VMEM((d, d), BF16),
        w_upT=pltpu.VMEM((h, d), BF16),
        w_downT=pltpu.VMEM((d, h), BF16),
        other_up=pltpu.VMEM((d, h // 2), BF16),
    )
    if b.index == 0:
        scratch.update(og=pltpu.VMEM((d, t), BF16), other_down=pltpu.VMEM((d, h // 2), BF16))
    else:
        scratch.update(other_down=pltpu.VMEM((h // 2, d), BF16))
    return scratch


def columns_of(rows):
    rows = rows.astype(F32)
    return jnp.concatenate([rows, jnp.zeros((128 - rows.shape[0], rows.shape[1]), F32)], 0).T


def prepare(b, r):
    r.tabT[...] = columns_of(jnp.concatenate([r.gains[...].astype(F32), r.shifts[...].astype(F32)], 0))
    r.w_inT[...] = r.w_in[...].T
    r.w_outT[...] = r.w_out[...].T
    r.a[b.columns : b.columns + 16, :] = jnp.ones((16, b.tokens), BF16)
    r.o[b.columns : b.columns + 16, :] = jnp.ones((16, b.tokens), BF16)
    r.c[b.columns : b.columns + 16, :] = jnp.ones((16, b.tokens), BF16)
    r.u[b.hidden : b.hidden + 16, :] = jnp.ones((16, b.tokens), BF16)
    r.table[...] = jnp.zeros_like(r.table)


def prepare_mlp(b, r):
    half, columns = b.hidden // 2, b.columns
    for part in range(2):
        mine = slice(part * half, (part + 1) * half)
        biases = columns_of(r.up_bias[part][0:16, :])
        for at in range(0, half, columns):
            place = b.index + at // LANES
            column = 19 + (part * half + at) // columns
            r.tabT[:, column : column + 1] = biases[at % LANES : at % LANES + columns, place : place + 1]
        r.w_upT[mine, :] = r.up[part][...].T
        r.w_downT[:, mine] = r.down[part][...].T if b.index else r.down[part][...]


class Refs:
    pass


class Plan:
    def __init__(self, place, small, large, dp):
        ds, dl, first = small.columns, large.columns, place.first
        self.dp_bits = dp.bit_length() - 1
        assert dp == 1 << self.dp_bits
        far = [list(range(at, min(at + 2, self.dp_bits))) for at in range(2, self.dp_bits, 2)]
        pool = Pool()
        other = first["other"]
        cross = 2560
        both = [[0], ["t", 1]] + far
        self.large_mlp = Group(
            pool, first["large_up"], 4 * dl, [[0], ["t"], [1]] + far, other + first["large_up"]
        )
        self.small_mlp = Group(
            pool, first["small_up"], 2 * ds, [[0], ["t"], [1]] + far, other + first["small_up"]
        )
        begin = first["large_cross"]
        self.cross_a = Group(pool, begin, cross // 2, [[0], [1], ["t"]] + far)
        self.cross_b = Group(pool, begin + cross // 2, cross // 2, [[0], ["t"], [1]] + far)
        self.large_heads = Group(pool, first["large_heads"], 4 * dl, both)
        tail = begin + cross
        self.small_heads = Group(pool, tail, first["large_heads"] - tail, both)
        self.tables = Group(pool, first["tables"], 64, both)
        self.pool = pool
        self.groups = (
            self.large_mlp, self.small_mlp, self.cross_a, self.cross_b, self.large_heads, self.small_heads, self.tables,
        )
        met = [[0], ["t"], [1]]
        for phase in [["t", 1]] + far:
            met += [flipped for number, flipped in subsets(phase)]
        self.met = []
        for names in met:
            if names not in self.met:
                self.met.append(names)


def drain(groups):
    while any(not group.done for group in groups):
        for group in groups:
            group.end()
            group.begin()


def layer_kernel(small, large, place, plan, keys, solo, *refs):
    ins = dict(zip(NAMES, refs))
    refs = refs[len(NAMES) :]
    packed, small_out, large_out, small_grad, large_grad = refs[:5]
    refs = refs[5:]
    groups = []
    links = Links(plan.dp_bits)
    links.bind(solo)
    for b, name in ((small, "small"), (large, "large")):
        r = Refs()
        for key in keys[b.index]:
            setattr(r, key, refs[0])
            refs = refs[1:]
        r.w_in, r.w_out = ins[name + "_in"], ins[name + "_out"]
        r.up = (ins[name + "_up"], r.other_up)
        r.down = (ins[name + "_down"], r.other_down)
        r.gains, r.shifts = ins[name + "_gains"], ins[name + "_shifts"]
        r.enter, r.leave = ins[name + "_enter"], ins[name + "_leave"]
        r.cross_in, r.cross_out = ins[name + "_cross_in"], ins[name + "_cross_out"]
        r.zg, r.yg = r.n, r.cotT
        groups.append((b, r))
    (bs, rs), (bl, rl) = groups
    work, mask, sums = refs[:3]
    biases, other_biases, buffer, received, send, recv, free, swap_send, swap_recv, out_sem, in_sem = refs[3:]
    for b, r in groups:
        r.bias_rows, r.mask, r.sums = biases, mask, sums
        r.up_bias = (ins["up_biases"], other_biases)
    half_s = bs.hidden // 2
    rs.down_times = lambda part, z: tn(rs.w_downT[:, part * half_s : (part + 1) * half_s], z)
    rl.down_times = lambda part, z: nn(rl.down[part][...], z)
    rs.og_rows = lambda slot, rows: rs.og.at[rows, slot_columns(bs, slot)]

    def large_og(slot, rows):
        size = rows.stop - rows.start
        if isinstance(slot, int):
            return rl.w_upT.at[slot * bl.columns + rows.start : slot * bl.columns + rows.stop, :]
        return rl.w_upT.at[pl.ds(pl.multiple_of(slot * bl.columns + rows.start, 64), size), :]

    rl.og_rows = large_og
    rs.staged = rs.sp.at[:, 0 : bs.rows]
    rl.staged = rl.w_inT.at[0 : bl.rows, :]
    biases[...] = jnp.zeros_like(biases)
    for group in plan.groups:
        group.bind(links, buffer, received, send, recv, free)
    swap = Swap(
        links,
        (
            (ins["large_up"], rl.other_up),
            (ins["large_down"], rl.other_down),
            (ins["small_up"], rs.other_up),
            (ins["small_down"], rs.other_down),
            (ins["up_biases"], other_biases),
        ),
        swap_send,
        swap_recv,
    )
    arrivals = []
    for at, name in enumerate(("large_rows", "large_cot")):
        target = rl.u.at[0 : bl.rows, at * bl.columns : (at + 1) * bl.columns]
        arrivals.append(pltpu.make_async_copy(ins[name], target, in_sem.at[at]))
        arrivals[-1].start()
    rs.rows, rs.cot = ins["small_rows"], ins["small_cot"]
    rl.rows = rl.g.at[0 : bl.columns, 0 : bl.rows]
    rl.cot = rl.g.at[bl.columns : 2 * bl.columns, 0 : bl.rows]

    def go(*names):
        if solo is None:
            for name in names:
                getattr(plan, name).advance()

    out_copies = {}

    def write_out(name, source, target):
        copy = pltpu.make_async_copy(source, target, out_sem.at[len(out_copies)])
        copy.start()
        out_copies[name] = copy

    def write_group(name):
        group = getattr(plan, name)
        if solo is None:
            while not group.done:
                group.advance()
        rows = slice(group.first, group.first + group.rows)
        write_out(name, buffer.at[rows, :], packed.at[rows, :])

    if solo is None:
        meet(links, plan.met)
        swap.start(0)
    else:
        for mine, theirs in swap.pairs:
            theirs[...] = mine[...]
    prepare(bs, rs)
    lay_out(bs, rs, ins["counts"])
    bring_in(bs, rs)
    prepare(bl, rl)
    for at, copy in enumerate(arrivals):
        copy.wait()
        (rl.rows, rl.cot)[at][...] = rl.u[0 : bl.rows, at * bl.columns : (at + 1) * bl.columns].T
    lay_out(bl, rl, ins["counts"])
    bring_in(bl, rl)
    forward_attention(bl, rl, [rl.z], [rl.w_downT])
    if solo is None:
        swap.wait(0)
        swap.start(1)
    forward_attention(bs, rs, [rl.z, work], [rl.w_downT])
    if solo is None:
        swap.wait(1)
    prepare_mlp(bl, rl)
    prepare_mlp(bs, rs)
    forward_mlp(bl, rl)
    forward_mlp(bs, rs)
    both = [
        cross(bs, rs, bl, rl, CrossGrads(bs, bl, place, buffer)),
        cross(bl, rl, bs, rs, CrossGrads(bl, bs, place, buffer)),
    ]
    while both:
        both = [one for one in both if next(one, both) is None]
    go("cross_a", "cross_b")
    backward_cross(bl, rl, work)
    go("cross_a", "cross_b")
    backward_mlp(bl, rl, work)
    go("cross_a", "cross_b")
    mlp_grads(bl, rl, place, buffer)
    go("large_mlp")
    backward_cross(bs, rs, work)
    go("large_mlp", "cross_a", "cross_b")
    backward_mlp(bs, rs, work)
    go("cross_a", "cross_b")
    mlp_grads(bs, rs, place, buffer)
    go("small_mlp")

    def during_large(slot):
        if slot == 0:
            go("large_mlp", "cross_a", "cross_b", "small_mlp")
        if slot == 1:
            go("cross_a", "cross_b", "small_mlp")
        if slot == 2:
            go("large_mlp", "cross_a", "cross_b", "small_mlp")

    backward_attention(bl, rl, [rl.y, work], [rl.w_downT], [rl.w_inT], during_large)
    head_grads(bl, rl, place, buffer)
    go("large_heads", "large_mlp", "cross_a", "cross_b", "small_mlp")
    backward_first_norm(bl, rl, work)
    go("large_heads", "cross_a", "cross_b")

    def during_small(slot):
        if slot in (1, 3):
            go("large_mlp", "small_mlp", "large_heads")

    backward_attention(bs, rs, [rl.y, work, rl.z], [rl.w_downT], [rl.qkv], during_small)
    head_grads(bs, rs, place, buffer)
    go("small_heads", "large_heads", "large_mlp")
    write_group("cross_a")
    write_group("cross_b")
    backward_first_norm(bs, rs, work)
    put_tables(links, place, buffer, rs, rl, biases)
    go("small_heads", "tables")
    go("large_heads", "small_mlp")
    put_out(bl, rl)
    write_out("large_out", rl.staged, large_out)
    go("small_heads", "tables")
    go("large_heads")
    put_out(bs, rs)
    write_out("small_out", rs.staged, small_out)
    go("small_heads", "tables")
    write_group("small_mlp")
    write_group("large_mlp")
    out_copies["large_out"].wait()
    put_back(bl, rl, rl.x)
    write_out("large_grad", rl.staged, large_grad)
    go("small_heads", "tables")
    go("large_heads")
    out_copies["small_out"].wait()
    put_back(bs, rs, rs.x)
    write_out("small_grad", rs.staged, small_grad)
    go("small_heads", "tables")
    go("large_heads")
    write_group("large_heads")
    write_group("small_heads")
    write_group("tables")
    for name, copy in out_copies.items():
        if name not in ("large_out", "small_out"):
            copy.wait()


def put_tables(links, place, buffer, rs, rl, biases):
    ds = rs.table.shape[1]
    own, other = biases[0, 0:8, :], biases[1, 0:8, :]
    first = links.tensor == 0
    rows = [
        rl.table[...],
        jnp.concatenate([rs.table[...], jnp.zeros((24, LANES - ds), F32)], 1),
        jnp.where(first, own, other),
        jnp.where(first, other, own),
    ]
    buffer[place.rows("tables"), :] = low(jnp.concatenate(rows, 0))


def unpack_kernel(place, ds, dl, parts, *refs):
    (packed, small_out, large_out, small_grad, large_grad), refs = refs[:5], refs[5:]
    outs, refs = dict(zip(OUTS, refs)), refs[len(OUTS) :]
    got, got_small, got_large, out_small, out_large = refs[:5]
    refs = refs[5:]
    stages, refs = dict(zip(OUTS[2:], refs)), refs[len(OUTS) - 2 :]
    in_sem, out_sem = refs
    copies, arriving = [], {}

    def bring(name, source, target):
        arriving[name] = pltpu.make_async_copy(source, target, in_sem.at[len(arriving)])
        arriving[name].start()

    def leave(source, target):
        copies.append(pltpu.make_async_copy(source, target, out_sem.at[len(copies)]))
        copies[-1].start()

    for name, first, rows in parts:
        bring(name, packed.at[first : first + rows, :], got.at[first : first + rows, :])
    bring("small_rows", small_grad, got_small)
    bring("large_rows", large_grad, got_large)
    bring("small_out", small_out, out_small)
    bring("large_out", large_out, out_large)

    def read(name, part, rows):
        first = place.first[name] + part
        return got[first : first + rows, :].astype(F32)

    def done(*names):
        for name in names:
            leave(stages[name], outs[name])

    arriving["mlp"].wait()
    for part in range(2):
        stages["large_up"][:, part * dl : (part + 1) * dl] = read("large_up", part * dl, dl)
    done("large_up")
    stages["large_down"][...] = read("large_down", 0, 2 * dl)
    stages["small_up"][...] = read("small_up", 0, ds)
    stages["small_down"][...] = read("small_down", 0, ds)
    done("large_down", "small_up", "small_down")
    for name in ("cross", "heads"):
        arriving[name].wait()
        for third in range(3):
            stages["large_" + name + "_in"][:, third * dl : (third + 1) * dl] = read(
                "large_" + name, third * dl, dl
            )
        stages["large_" + name + "_out"][...] = read("large_" + name, 3 * dl, dl)
        second = read("small_" + name, ds, ds)
        stages["small_" + name + "_in"][:, 0:LANES] = read("small_" + name, 0, ds)
        stages["small_" + name + "_in"][:, LANES:] = second[:, 0:ds]
        stages["small_" + name + "_out"][...] = second[:, ds:]
        done("large_" + name + "_in", "large_" + name + "_out", "small_" + name + "_in", "small_" + name + "_out")
        if name == "cross":
            for key in ("small_enter", "small_leave", "large_enter", "large_leave"):
                stages[key][...] = read(key, 0, ds)
                done(key)
    for name, ref in (("small_rows", got_small), ("large_rows", got_large)):
        arriving[name].wait()
        stages[name][...] = ref[...].astype(F32)
        done(name)
    for name, ref in (("small_out", out_small), ("large_out", out_large)):
        arriving[name].wait()
        leave(ref, outs[name])
    arriving["tables"].wait()
    first = place.first["tables"]
    tables = got[first : first + 64, :].astype(F32)
    stages["large_gains"][...] = tables[0:5]
    stages["large_shifts"][...] = tables[5:19]
    stages["small_gains"][...] = tables[24:29, 0:ds]
    stages["small_shifts"][...] = tables[29:43, 0:ds]
    mine = jnp.where(lax.axis_index("tensor") == 0, tables[48:56], tables[56:64])
    stages["small_up_bias"][...] = mine[0:1]
    stages["large_up_bias"][...] = jnp.concatenate([mine[1:2], mine[2:3]], 1)
    done("large_gains", "large_shifts", "small_gains", "small_shifts", "small_up_bias", "large_up_bias")
    for copy in copies:
        copy.wait()


TURNED = ("small_out", "small_rows", "small_down", "small_leave", "large_enter")


def run_layer(args, dp, solo=None):
    (
        small_rows, large_rows, counts, small_cot, large_cot,
        small_in, small_out, small_up, small_up_bias, small_down,
        large_in, large_out, large_up, large_up_bias, large_down,
        small_enter, large_cross_in, large_cross_out, small_leave, large_enter,
    ) = args[:20]
    ds, dl = small_rows.shape[1], large_rows.shape[1]
    small = Branch(0, small_rows.shape[0], ds, 2 * small_up.shape[1], 256, ((0, 4), (1, 5), (2,), (3,), (6,)))
    large = Branch(1, large_rows.shape[0], dl, 2 * large_up.shape[1], 384, ((0, 1, 4), (2, 3, 5), (6,)))
    place = Place(small, large)
    plan = Plan(place, small, large, dp)
    biases = jnp.concatenate([small_up_bias, large_up_bias]).reshape(-1, LANES)
    biases = jnp.pad(biases, ((0, 32 - biases.shape[0]), (0, 0)))
    inputs = (
        counts, small_rows.T, large_rows, small_cot.T, large_cot,
        small_in, small_out, small_up, small_down.T,
        large_in, large_out, large_up, large_down,
        small_enter, large_cross_in, large_cross_out, small_leave.T, large_enter.T,
    ) + args[20:] + (biases,)
    keys = tuple(tuple(scratch_of(b)) for b in (small, large))
    scratch = [s for b in (small, large) for s in scratch_of(b).values()]
    copies = pltpu.SemaphoreType.DMA
    scratch += [
        pltpu.VMEM((dl, large.tokens), F32),
        pltpu.VMEM((large.width, large.width), F32),
        pltpu.VMEM((2, dl, 128), F32),
        pltpu.VMEM((2, 16, LANES), F32),
        pltpu.VMEM((32, LANES), BF16),
        pltpu.VMEM((place.total, LANES), BF16),
        pltpu.VMEM((plan.pool.rows, LANES), BF16),
        copies((plan.pool.copies,)),
        copies((plan.pool.copies,)),
        pltpu.SemaphoreType.REGULAR((plan.pool.signals,)),
        copies((2, 5)),
        copies((2, 5)),
        copies((16,)),
        copies((2,)),
    ]
    shape = jax.ShapeDtypeStruct
    vmem, hbm = pl.BlockSpec(memory_space=pltpu.VMEM), pl.BlockSpec(memory_space=pl.ANY)
    middle = (
        shape((place.total, LANES), BF16),
        shape((ds, small.rows), BF16),
        shape((large.rows, dl), BF16),
        shape((ds, small.rows), BF16),
        shape((large.rows, dl), BF16),
    )
    values = pl.pallas_call(
        functools.partial(layer_kernel, small, large, place, plan, keys, solo),
        out_shape=middle,
        in_specs=[pl.BlockSpec(memory_space=pltpu.SMEM)]
        + [hbm if name in ("large_rows", "large_cot") else vmem for name in NAMES[1:]],
        out_specs=(hbm,) * 5,
        scratch_shapes=scratch,
        compiler_params=pltpu.CompilerParams(
            vmem_limit_bytes=VMEM_LIMIT,
            collective_id=0 if solo is None else None,
            has_side_effects=True,
        ),
        name="layer",
    )(*inputs)
    shapes = dict(
        small_out=shape((ds, small.rows), BF16),
        large_out=shape(large_rows.shape, BF16),
        small_rows=shape((ds, small.rows), F32),
        large_rows=shape(large_rows.shape, F32),
        small_up_bias=shape((1, small_up_bias.shape[0]), F32),
        large_up_bias=shape((1, large_up_bias.shape[0]), F32),
    )
    for name, value in zip(OUTS[4:], args[5:]):
        turned = value.shape[::-1] if name in TURNED else value.shape
        shapes.setdefault(name, shape(turned, F32))
    first = place.first
    cross_first = first["large_cross"]
    parts = (
        ("mlp", 0, first["other"]),
        ("cross", cross_first, first["small_heads"] - cross_first),
        ("heads", first["small_heads"], first["tables"] - first["small_heads"]),
        ("tables", first["tables"], 64),
    )
    results = pl.pallas_call(
        functools.partial(unpack_kernel, place, ds, dl, parts),
        out_shape=tuple(shapes[name] for name in OUTS),
        in_specs=(hbm,) * 5,
        out_specs=(hbm,) * len(OUTS),
        scratch_shapes=[
            pltpu.VMEM((place.total, LANES), BF16),
        ]
        + [pltpu.VMEM((ds, small.rows), BF16), pltpu.VMEM(large_rows.shape, BF16)] * 2
        + [pltpu.VMEM(shapes[name].shape, F32) for name in OUTS[2:]]
        + [copies((8,)), copies((len(OUTS),))],
        compiler_params=pltpu.CompilerParams(vmem_limit_bytes=VMEM_LIMIT),
        name="unpack",
    )(*values)

    def restore(name, value):
        if name.endswith("_bias"):
            return value.reshape(-1)
        return value.T if name in TURNED else value

    return tuple(restore(name, value) for name, value in zip(OUTS, results))


def solution(mesh):
    both = ("dp", "tensor")
    rows = P(both, None)
    mlp = (P(None, "tensor"), P("tensor"), P("tensor", None))

    def shards(*args):
        return run_layer(args, mesh.shape["dp"])

    return jax.shard_map(
        shards,
        mesh=mesh,
        in_specs=(rows, rows, P(None, both), rows, rows)
        + ((P(), P()) + mlp) * 2
        + (P(),) * 12,
        out_specs=(rows,) * 4 + ((P(), P()) + mlp) * 2 + (P(),) * 12,
        check_vma=False,
    )
```

```python
import functools
import collections
import jax
import jax.numpy as jnp
from jax import lax
from jax.experimental import pallas as pl
from jax.experimental.pallas import tpu as pltpu
from jax.sharding import PartitionSpec as P

HEADS = 6
VMEM_LIMIT = 64 * 1024 * 1024
NEGATIVE = -1e30
EPSILON = 1e-06
F32, BF16 = jnp.float32, jnp.bfloat16
LANES = 384
CLS = 16
STACK = HEADS * CLS

GLOBAL_ROWS, LOCAL_ROWS = (197, 145), (37, 65)
BLOCK = 32
LOG2E = 1.4426950408889634


def low(values):
    return values.astype(BF16)


def dot(left, right, left_axis, right_axis):
    return lax.dot_general(
        left, right, (((left_axis,), (right_axis,)), ((), ())), preferred_element_type=F32
    )


def nn(left, right):
    return dot(left, right, 1, 0)


def nt(left, right):
    return dot(left, right, 1, 1)


def tn(left, right):
    return dot(left, right, 0, 0)


class Branch:
    def __init__(self, index, rows, columns, hidden, width, layout):
        self.index, self.rows, self.columns, self.hidden = index, rows, columns, hidden
        self.head = columns // HEADS
        self.width, self.slots = width, len(layout)
        self.tokens = width * self.slots
        self.pieces = []
        self.bounds = []
        g_rows, l_rows = GLOBAL_ROWS[index], LOCAL_ROWS[index]
        for slot, crops in enumerate(layout):
            lane, ends = 0, []
            for crop in crops:
                length = g_rows if crop < 4 else l_rows if crop < 6 else rows - 4 * g_rows - 2 * l_rows
                self.pieces.append((slot * width + lane, length, crop))
                lane += length
                ends.append(lane)
            assert lane <= width
            self.bounds.append(ends)


def norm(values, axis):
    center = values - jnp.mean(values, axis, keepdims=True)
    scale = lax.rsqrt(jnp.mean(center * center, axis, keepdims=True) + EPSILON)
    return center * scale, scale


def fold(values):
    total = values[0:8]
    for at in range(8, values.shape[0], 8):
        total = total + values[at : at + 8]
    return total


def fold_lanes(values):
    total = values[:, 0:128]
    for at in range(128, values.shape[1], 128):
        total = total + values[:, at : at + 128]
    return total


def chunks(columns):
    return [slice(at, at + BLOCK) for at in range(0, columns, BLOCK)]


def norm_columns(load, columns, keep):
    total = sum(fold(load(rows)) for rows in chunks(columns))
    mean = jnp.sum(total, 0, keepdims=True) * (1.0 / columns)
    spread = 0.0
    for rows in chunks(columns):
        center = load(rows) - mean
        spread = spread + fold(center * center)
    spread = jnp.sum(spread, 0, keepdims=True) * (1.0 / columns)
    scale = lax.rsqrt(spread + EPSILON)
    keep(mean, scale)
    return mean, scale


def norm_columns_back(load, grad, columns, mean, scale, gain, sums, store):
    first = second = 0.0
    for rows in chunks(columns):
        unit = (load(rows) - mean) * scale
        back = grad(rows)
        both = back * unit
        sums[0, rows, :] += fold_lanes(back)
        sums[1, rows, :] += fold_lanes(both)
        first = first + fold(back * gain(rows))
        second = second + fold(both * gain(rows))
    first = jnp.sum(first, 0, keepdims=True) * (1.0 / columns)
    second = jnp.sum(second, 0, keepdims=True) * (1.0 / columns)
    for rows in chunks(columns):
        unit = (load(rows) - mean) * scale
        store(rows, scale * (grad(rows) * gain(rows) - first - unit * second))


def norm_back(grad, unit, scale, axis):
    return scale * (
        grad
        - jnp.mean(grad, axis, keepdims=True)
        - unit * jnp.mean(grad * unit, axis, keepdims=True)
    )


def smooth_parts(values):
    chance = 0.5 + 0.5 * lax.erf(values * (0.5**0.5))
    slope = chance + values * (jnp.exp(values * values * -0.5) * 0.3989422804014327)
    return values * chance, slope


def pick(at, values):
    if isinstance(at, int):
        return values[at]
    result = values[-1]
    for place in range(len(values) - 2, -1, -1):
        result = jnp.where(at == place, values[place], result)
    return result


def iota(shape, axis):
    return lax.broadcasted_iota(jnp.int32, shape, axis)


def each_slot(branch, body, between=None):
    if between is None:
        lax.fori_loop(0, branch.slots, lambda slot, carry: body(slot) or carry, 0)
        return
    for slot in range(branch.slots):
        body(slot)
        between(slot)


def slot_columns(branch, slot):
    if isinstance(slot, int):
        return slice(slot * branch.width, (slot + 1) * branch.width)
    return pl.ds(pl.multiple_of(slot * branch.width, branch.width), branch.width)


def places(counts, b):
    starts = [jnp.int32(0)] * 7
    begin, globals_seen, locals_seen = jnp.int32(0), jnp.int32(0), jnp.int32(0)
    for crop in range(6):
        rows = counts[b.index, crop]
        is_global = counts[0, crop] == GLOBAL_ROWS[0]
        for k in range(4):
            starts[k] = jnp.where(is_global & (globals_seen == k), begin, starts[k])
        for k in range(2):
            starts[4 + k] = jnp.where((~is_global) & (locals_seen == k), begin, starts[4 + k])
        begin = begin + rows
        globals_seen = globals_seen + jnp.where(is_global, 1, 0)
        locals_seen = locals_seen + jnp.where(is_global, 0, 1)
    starts[6] = begin
    return starts


def lay_out(b, r, counts):
    starts = places(counts, b)
    lane = iota((1, b.tokens), 1)
    source = jnp.full((1, b.tokens), -1, jnp.int32)
    patch = jnp.full((1, b.tokens), -1, jnp.int32)
    cls = jnp.full((1, b.tokens), -1, jnp.int32)
    for first, length, crop in b.pieces:
        inside = (lane >= first) & (lane < first + length)
        source = jnp.where(inside, lane - first + starts[crop], source)
        if crop < 6:
            patch = jnp.where(inside & (lane > first), crop, patch)
            cls = jnp.where(lane == first, crop, cls)
    r.index[0:1, :] = source
    r.index[1:2, :] = patch
    r.index[2:3, :] = cls
    at = iota((CLS, 1), 0)
    first_rows = jnp.full((CLS, 1), -1, jnp.int32)
    for crop in range(6):
        first_rows = jnp.where(at == crop, starts[crop], first_rows)
    chosen = low((iota((CLS, b.rows), 1) == first_rows).astype(F32))
    r.cot_cls[...] = nt(chosen, r.cot[...])


def bring_in(b, r):
    def body(slot):
        cols = slot_columns(b, slot)
        chosen = low((iota((b.rows, b.width), 0) == r.index[0:1, cols]).astype(F32))
        r.x[:, cols] = low(nn(r.rows[...], chosen))
        keep = r.index[2:3, cols] < 0
        r.cotT[:, cols] = low(jnp.where(keep, nn(r.cot[...], chosen), 0.0))

    each_slot(b, body)


def slot_mask(b, slot):
    ends = [pick(slot, [e[min(i, len(e) - 1)] for e in b.bounds]) for i in range(3)]

    def segment(axis):
        at = iota((b.width, b.width), axis)
        total = jnp.zeros((b.width, b.width), jnp.int32)
        for end in ends[: max(len(e) for e in b.bounds)]:
            total = total + (at >= end).astype(jnp.int32)
        return total

    return jnp.where(segment(0) == segment(1), 0.0, NEGATIVE)


def squares(b, refs):
    result = []
    for ref in refs:
        for row in range(0, ref.shape[0] - b.width + 1, b.width):
            for lane in range(0, ref.shape[1] - b.width + 1, b.width):
                result.append(ref.at[row : row + b.width, lane : lane + b.width])
    return result


def parts_of(b, h):
    first = [part * b.columns + h * b.head for part in range(3)]
    return [slice(at, at + b.head) for at in first]


def forward_attention(b, r, wide_work, low_work, between=None):
    columns, width = b.columns, b.width
    factor = float(b.head) ** (-0.5) * LOG2E
    wide, lows = squares(b, wide_work), squares(b, low_work)
    many = min(len(wide), len(lows), HEADS)
    mask_ref = r.mask.at[0:width, 0:width]

    def body(slot):
        cols = slot_columns(b, slot)

        def tokens(rows):
            return r.x[rows, cols].astype(F32)

        def keep(at):
            def put(mean, scale):
                r.stats[at : at + 1, cols] = mean
                r.stats[at + 1 : at + 2, cols] = scale

            return put

        mean, scale = norm_columns(tokens, columns, keep(0))
        for rows in chunks(columns):
            unit = (tokens(rows) - mean) * scale
            r.a[rows, cols] = low(unit * r.tabT[rows, 0:1] + r.tabT[rows, 5:6])
        a = r.a[0:columns, cols]
        for third, bias in ((0, 6), (1, None), (2, 7)):
            rows = slice(third * columns, (third + 1) * columns)
            product = nn(r.w_inT[rows, :], a)
            r.qkv[rows, cols] = low(product if bias is None else product + r.tabT[:, bias : bias + 1])
        mask_ref[...] = slot_mask(b, slot)
        for begin in range(0, HEADS, many):
            heads = range(begin, min(begin + many, HEADS))
            for h in heads:
                q, k, v = parts_of(b, h)
                wide[h - begin][...] = tn(r.qkv[k, cols], r.qkv[q, cols])
            for h in heads:
                scores = wide[h - begin][...] * factor + mask_ref[...]
                highest = jnp.max(scores, 0, keepdims=True)
                powers = jnp.exp2(scores - highest)
                total = jnp.sum(powers, 0, keepdims=True)
                r.logs[h : h + 1, cols] = highest + jnp.log2(total)
                lows[h - begin][...] = low(powers * (1.0 / total))
            for h in heads:
                q, k, v = parts_of(b, h)
                r.o[q, cols] = low(nn(r.qkv[v, cols], lows[h - begin][...]))
        r.y[:, cols] = (
            r.x[:, cols].astype(F32) + tn(r.w_out[...], r.o[0:columns, cols]) + r.tabT[:, 8:9]
        )
        mean, scale = norm_columns(lambda rows: r.y[rows, cols], columns, keep(2))
        for rows in chunks(columns):
            unit = (r.y[rows, cols] - mean) * scale
            r.c[rows, cols] = low(unit * r.tabT[rows, 1:2] + r.tabT[rows, 9:10])

    each_slot(b, body, between)


def forward_mlp(b, r, between=None):
    chunk = LANES // 2
    columns = b.columns
    r.cls[...] = jnp.zeros_like(r.cls)

    def body(slot):
        cols = slot_columns(b, slot)
        c = r.c[0:columns, cols]
        for at in range(0, b.hidden, chunk):
            bias = r.tabT[at % columns : at % columns + chunk, 19 + at // columns : 20 + at // columns]
            active, slope = smooth_parts(nn(r.w_upT[at : at + chunk, :], c) + bias)
            r.u[at : at + chunk, cols] = low(active)
            r.g[at : at + chunk, cols] = low(slope)
        r.z[:, cols] = r.y[:, cols] + nn(r.w_downT[...], r.u[0 : b.hidden, cols]) + r.tabT[:, 10:11]

        def keep(mean, scale):
            r.stats[4:5, cols] = mean
            r.stats[5:6, cols] = scale

        mean, scale = norm_columns(lambda rows: r.z[rows, cols], columns, keep)
        for rows in chunks(columns):
            z = r.z[rows, cols]
            r.out[rows, cols] = low(z)
            r.n[rows, cols] = low((z - mean) * scale * r.tabT[rows, 3:4] + r.tabT[rows, 14:15])
        chosen = low((iota((CLS, b.width), 0) == r.index[2:3, cols]).astype(F32))
        rest = low(r.z[:, cols] - r.out[:, cols].astype(F32))
        r.cls[...] += nt(chosen, r.out[:, cols]) + nt(chosen, rest)

    each_slot(b, body, between)


def backward_cross(b, r, work, between=None):
    columns, width = b.columns, b.width
    r.sums[...] = jnp.zeros_like(r.sums)
    cls_grad = r.cls_grad[...]
    high = low(cls_grad)
    pair = jnp.concatenate([high, low(cls_grad - high.astype(F32))], 0)
    maps, pair = r.maps[...].T, pair.T

    def body(slot):
        cols = slot_columns(b, slot)
        work[0:columns, 0:width] = nn(maps, r.sp[:, cols])
        chosen = low((iota((CLS, width), 0) == r.index[2:3, cols]).astype(F32))
        work[0:columns, width : 2 * width] = nn(pair, jnp.concatenate([chosen, chosen], 0))

        def store(rows, back):
            r.z[rows, cols] = r.cotT[rows, cols].astype(F32) + work[rows, width : 2 * width] + back

        norm_columns_back(
            lambda rows: r.z[rows, cols],
            lambda rows: work[rows, 0:width],
            columns,
            r.stats[4:5, cols],
            r.stats[5:6, cols],
            lambda rows: r.tabT[rows, 3:4],
            r.sums.at[:, 0:columns, :],
            store,
        )

    each_slot(b, body, between)
    r.table[3:4, :] += row_sum(r.sums[1, 0:columns, :])
    r.table[5 + 9 : 5 + 10, :] += row_sum(r.sums[0, 0:columns, :])


def row_sum(values):
    return jnp.sum(values.T, 0, keepdims=True)


def put_out(b, r, between=None):
    def replace(slot):
        cols = slot_columns(b, slot)
        cls = r.index[2:3, cols]
        chosen = low((iota((CLS, b.width), 0) == cls).astype(F32))
        new = tn(r.new_cls[...], chosen)
        r.out[:, cols] = jnp.where(cls >= 0, new, r.out[:, cols].astype(F32)).astype(BF16)

    each_slot(b, replace)
    put_back(b, r, r.out, between)


def put_back(b, r, values, between=None):
    tile = b.rows // 4

    def part(step):
        first = step * tile if isinstance(step, int) else pl.multiple_of(step * tile, tile)
        chosen = low((iota((tile, b.tokens), 0) + first == r.index[0:1, :]).astype(F32))
        if b.index == 0:
            r.staged[:, pl.ds(first, tile)] = low(nt(values[...], chosen))
        else:
            r.staged[pl.ds(first, tile), :] = low(nt(chosen, values[...]))

    if between is None:
        lax.fori_loop(0, 4, lambda step, carry: part(step) or carry, 0)
        return
    for step in range(4):
        part(step)
        between(step)


def backward_mlp(b, r, work, between=None):
    half, columns, width = b.hidden // 2, b.columns, b.width
    r.sums[...] = jnp.zeros_like(r.sums)

    def body(slot):
        cols = slot_columns(b, slot)
        r.zg[:, cols] = low(r.z[:, cols])
        z_low = r.zg[:, cols]
        for part in range(2):
            mine = slice(part * half, (part + 1) * half)
            r.g[mine, cols] = low(r.down_times(part, z_low) * r.g[mine, cols].astype(F32))
        work[0:columns, 0:width] = nn(r.up[0][...], r.g[0:half, cols]) + nn(
            r.up[1][...], r.g[half:, cols]
        )

        def store(rows, back):
            grad = r.z[rows, cols] + back
            r.z[rows, cols] = grad
            r.yg[rows, cols] = low(grad)

        norm_columns_back(
            lambda rows: r.y[rows, cols],
            lambda rows: work[rows, 0:width],
            columns,
            r.stats[2:3, cols],
            r.stats[3:4, cols],
            lambda rows: r.tabT[rows, 1:2],
            r.sums.at[:, 0:columns, :],
            store,
        )
        r.og_rows(slot, slice(0, columns))[...] = low(nn(r.w_out[...], r.yg[:, cols]))

    each_slot(b, body, between)
    r.table[1:2, :] = row_sum(r.sums[1, 0:columns, :])
    r.table[5 + 4 : 5 + 5, :] = row_sum(r.sums[0, 0:columns, :])


def backward_attention(b, r, wide_work, low_work, more_work, between=None):
    columns, width = b.columns, b.width
    factor = float(b.head) ** (-0.5)
    wide, lows, more = squares(b, wide_work), squares(b, low_work), squares(b, more_work)
    many = min(len(wide) // 2, len(lows), len(more), HEADS)
    mask_ref = r.mask.at[0:width, 0:width]

    def body(slot):
        cols = slot_columns(b, slot)
        mask_ref[...] = slot_mask(b, slot)
        for begin in range(0, HEADS, many):
            heads = range(begin, min(begin + many, HEADS))
            for h in heads:
                q, k, v = parts_of(b, h)
                wide[h - begin][...] = tn(r.qkv[k, cols], r.qkv[q, cols])
            for h in heads:
                q, k, v = parts_of(b, h)
                wide[many + h - begin][...] = tn(r.qkv[v, cols], r.og_rows(slot, q)[...])
            for h in heads:
                chances = jnp.exp2(
                    wide[h - begin][...] * (factor * LOG2E)
                    + (mask_ref[...] - r.logs[h : h + 1, cols])
                )
                lows[h - begin][...] = low(chances)
                chance_grad = wide[many + h - begin][...]
                inner = jnp.sum(chance_grad * chances, 0, keepdims=True)
                more[h - begin][...] = low(chances * ((chance_grad - inner) * factor))
            for h in heads:
                q, k, v = parts_of(b, h)
                q_low, k_low = r.qkv[q, cols], r.qkv[k, cols]
                score_grad = more[h - begin][...]
                r.qkv[q, cols] = low(nn(k_low, score_grad))
                r.qkv[k, cols] = low(nt(q_low, score_grad))
                r.qkv[v, cols] = low(nt(r.og_rows(slot, q)[...], lows[h - begin][...]))

    each_slot(b, body, between)


def backward_first_norm(b, r, work, between=None):
    columns, width = b.columns, b.width
    r.sums[...] = jnp.zeros_like(r.sums)

    def body(slot):
        cols = slot_columns(b, slot)
        work[0:columns, 0:width] = nn(r.w_in[...], r.qkv[:, cols])

        def store(rows, back):
            r.x[rows, cols] = low(r.z[rows, cols] + back)

        norm_columns_back(
            lambda rows: r.x[rows, cols].astype(F32),
            lambda rows: work[rows, 0:width],
            columns,
            r.stats[0:1, cols],
            r.stats[1:2, cols],
            lambda rows: r.tabT[rows, 0:1],
            r.sums.at[:, 0:columns, :],
            store,
        )
    each_slot(b, body, between)
    r.table[0:1, :] = row_sum(r.sums[1, 0:columns, :])
    r.table[5:6, :] = row_sum(r.sums[0, 0:columns, :])
def head_mask(columns):
    head = columns // HEADS
    at = iota((STACK, columns), 1)
    first = iota((STACK, columns), 0) // CLS * head
    return (at >= first) & (at < first + head)


def spread(values, mask):
    return jnp.where(mask, jnp.concatenate([values] * HEADS, 0), 0.0)


def gather_heads(values, mask):
    values = jnp.where(mask, values, 0.0)
    total = values[0:CLS]
    for h in range(1, HEADS):
        total = total + values[h * CLS : (h + 1) * CLS]
    return total


def column_sum(values):
    return jnp.sum(values, 0, keepdims=True)


def cross(b, r, o, ro, g):
    wide = o.columns
    factor = float(o.head) ** (-0.5)
    mask = head_mask(wide)
    og, ob = ro.gains, ro.shifts

    def row(table, at):
        return table[at : at + 1, :].astype(F32)

    enter_on, enter_back, leave_on, leave_back = (nn, nt, nt, nn) if b.index == 0 else (nt, nn, nn, nt)

    xc = r.cls[...]
    yield
    unit2, scale2 = norm(xc, 1)
    lifted, slope2 = smooth_parts(unit2 * row(r.gains, 2) + row(r.shifts, 6))
    lifted = low(lifted)
    yield
    moved = enter_on(lifted, r.enter[...]) + row(ob, 8)
    yield
    unit3, scale3 = norm(moved, 1)
    query_norm = low(unit3 * row(og, 3) + row(ob, 9))
    yield
    q = low(nn(query_norm, ro.cross_in[:, 0:wide]) + row(ob, 10))
    own_k = low(nn(query_norm, ro.cross_in[:, wide : 2 * wide]))
    own_v = low(nn(query_norm, ro.cross_in[:, 2 * wide : 3 * wide]) + row(ob, 11))
    q_all = spread(q.astype(F32), mask)
    k_all = spread(own_k.astype(F32), mask)
    v_all = spread(own_v.astype(F32), mask)
    yield
    key_map = low(nt(low(q_all), ro.cross_in[:, wide : 2 * wide]))
    yield
    own_score = jnp.sum(q_all * k_all, 1, keepdims=True) * factor
    usable = ro.index[1:2, :] == iota((STACK, o.tokens), 0) % CLS
    yield
    scores = jnp.where(usable, nn(key_map, ro.n[...]) * factor, NEGATIVE)
    yield
    highest = jnp.maximum(own_score, jnp.max(scores, 1, keepdims=True))
    powers = jnp.exp(scores - highest)
    own_power = jnp.exp(own_score - highest)
    yield
    inverse = 1.0 / (own_power + jnp.sum(powers, 1, keepdims=True))
    chances = powers * inverse
    own_chance = own_power * inverse
    chances_low = low(chances)
    own_low = low(own_chance).astype(F32)
    ro.sp[STACK : 2 * STACK, :] = chances_low
    total = jnp.sum(chances_low.astype(F32), 1, keepdims=True)
    yield
    mean_row = low(nt(chances_low, ro.n[...]))
    value_bias = row(ob, 11)
    yield
    mixed = own_low * v_all + nn(mean_row, ro.cross_in[:, 2 * wide : 3 * wide]) + total * value_bias
    attended = low(gather_heads(mixed, mask))
    yield
    joined = moved + nn(attended, ro.cross_out[...]) + row(ob, 12)
    yield
    unit4, scale4 = norm(joined, 1)
    spread_out, slope4 = smooth_parts(unit4 * row(og, 4) + row(ob, 13))
    spread_out = low(spread_out)
    r.new_cls[...] = low(leave_on(spread_out, r.leave[...]) + row(r.shifts, 7))

    yield
    new_grad = r.cot_cls[...]
    new_low = low(new_grad)
    r.table[5 + 7 : 5 + 8, :] = column_sum(new_grad)
    yield
    g.leave(tn(new_low, spread_out) if b.index == 0 else tn(spread_out, new_low))
    yield
    back = leave_back(new_low, r.leave[...]) * slope4
    ro.table[4:5, :] = column_sum(back * unit4)
    ro.table[5 + 13 : 5 + 14, :] = column_sum(back)
    yield
    joined_grad = norm_back(back * row(og, 4), unit4, scale4, 1)
    ro.table[5 + 12 : 5 + 13, :] = column_sum(joined_grad)
    joined_low = low(joined_grad)
    yield
    g.cross_out(tn(attended, joined_low))
    yield
    mixed_grad = low(nt(joined_low, ro.cross_out[...])).astype(F32)
    yield
    mixed_all = spread(mixed_grad, mask)
    mixed_all_low = low(mixed_all)
    own_v_grad = gather_heads(own_low * mixed_all, mask)
    own_chance_grad = jnp.sum(mixed_all * v_all, 1, keepdims=True)
    yield
    value_map = low(nt(mixed_all_low, ro.cross_in[:, 2 * wide : 3 * wide]))
    yield
    chance_grad = nn(value_map, ro.n[...]) + jnp.sum(mixed_all * value_bias, 1, keepdims=True)
    yield
    inner = own_chance_grad * own_chance + jnp.sum(chance_grad * chances, 1, keepdims=True)
    score_grad = low(chances * (chance_grad - inner) * factor)
    own_score_grad = low(own_chance * (own_chance_grad - inner) * factor).astype(F32)
    ro.sp[0:STACK, :] = score_grad
    yield
    mean_back = low(nt(score_grad, ro.n[...]))
    yield
    q_grad = gather_heads(
        own_score_grad * k_all + nn(mean_back, ro.cross_in[:, wide : 2 * wide]), mask
    )
    own_k_grad = gather_heads(own_score_grad * q_all, mask)
    ro.table[5 + 10 : 5 + 11, :] = column_sum(q_grad)
    ro.table[5 + 11 : 5 + 12, :] = column_sum(own_v_grad) + column_sum(total * mixed_all)
    q_low, k_low, v_low = low(q_grad), low(own_k_grad), low(own_v_grad)
    yield
    g.cross_in(
        0,
        tn(query_norm, q_low),
    )
    yield
    g.cross_in(
        1,
        tn(
            jnp.concatenate([query_norm, mean_back], 0),
            jnp.concatenate([k_low, low(q_all)], 0),
        ),
    )
    yield
    g.cross_in(
        2,
        tn(
            jnp.concatenate([query_norm, mean_row], 0),
            jnp.concatenate([v_low, mixed_all_low], 0),
        ),
    )
    yield
    back = (
        nt(q_low, ro.cross_in[:, 0:wide])
        + nt(k_low, ro.cross_in[:, wide : 2 * wide])
        + nt(v_low, ro.cross_in[:, 2 * wide : 3 * wide])
    )
    ro.table[3:4, :] = column_sum(back * unit3)
    ro.table[5 + 9 : 5 + 10, :] = column_sum(back)
    yield
    moved_grad = joined_grad + norm_back(back * row(og, 3), unit3, scale3, 1)
    ro.table[5 + 8 : 5 + 9, :] = column_sum(moved_grad)
    moved_low = low(moved_grad)
    yield
    g.enter(tn(lifted, moved_low) if b.index == 0 else tn(moved_low, lifted))
    yield
    back = enter_back(moved_low, r.enter[...]) * slope2
    r.table[2:3, :] = column_sum(back * unit2)
    r.table[5 + 6 : 5 + 7, :] = column_sum(back)
    r.cls_grad[...] = norm_back(back * row(r.gains, 2), unit2, scale2, 1)
    ro.maps[0:STACK, :] = key_map
    ro.maps[STACK : 2 * STACK, :] = value_map


def bit_of(value, place):
    return (value // (1 << place)) % 2


class Links:
    def __init__(self, dp_bits):
        self.bits = ["t"] + list(range(dp_bits))

    def bind(self, solo=None):
        self.dp = self.tensor = 0
        if solo is None:
            self.dp, self.tensor = lax.axis_index("dp"), lax.axis_index("tensor")

    def bit(self, name):
        return self.tensor if name == "t" else bit_of(self.dp, name)

    def partner(self, names):
        dp, tensor = self.dp, self.tensor
        for name in names:
            if name == "t":
                tensor = 1 - self.tensor
            else:
                dp = dp + (1 - 2 * bit_of(self.dp, name)) * (1 << name)
        return (dp, tensor)


def subsets(names):
    for number in range(1, 1 << len(names)):
        yield number, [name for at, name in enumerate(names) if number >> at & 1]


class Pool:
    def __init__(self):
        self.rows, self.copies, self.signals = 0, 0, 0

    def signal(self):
        self.signals += 1
        return self.signals - 1

    def take(self, rows, copies):
        at = (self.rows, self.copies)
        self.rows, self.copies = self.rows + rows, self.copies + copies
        return at


class Group:
    def __init__(self, pool, first, rows, phases, apart=None):
        self.first, self.rows, self.apart = first, rows, apart
        self.steps, size, bases = [], rows, 1 if apart is None else 2
        self.frees = {}
        phases = list(phases)
        while phases:
            names, kind = phases.pop(0)
            count = 1 << len(names)
            if kind == "halve" and size % (16 * count):
                kind = "full"
                if len(names) > 1:
                    phases = [((name,), "halve") for name in names] + phases
                    continue
            if kind == "merge":
                bases = 1
                self.steps.append((kind, names, size, pool.take(size, 1), 1))
            elif kind == "halve":
                at = pool.take(bases * (count - 1) * (size // count), 2 * bases * (count - 1))
                self.steps.append((kind, names, size, at, bases))
                self.frees[len(self.steps) - 1] = pool.signal()
                size //= count
            else:
                at = pool.take(bases * (count - 1) * size, bases * (count - 1))
                self.steps.append((kind, names, size, at, bases))
        self.plan = [("reduce", step, self.frees.get(at)) for at, step in enumerate(self.steps)]
        self.plan += [("gather",) + step[1:] for step in reversed(self.plan) if step[2] is not None]

    def bind(self, links, buffer, received, send, recv, free):
        self.links, self.buffer, self.received = links, buffer, received
        self.send, self.recv, self.free = send, recv, free
        self.lo, self.at, self.flight, self.offsets = 0, 0, [], {}
        return self

    def chunk(self, names, flipped):
        index = 0
        for place, name in enumerate(names):
            bit = self.links.bit(name)
            index = index + (1 - bit if name in flipped else bit) * (1 << place)
        return index

    def rows_at(self, base, first, size):
        return pl.ds(pl.multiple_of(base + first, 16), size)

    def copy(self, source, target, sem, partner):
        return pltpu.make_async_remote_copy(
            src_ref=source,
            dst_ref=target,
            send_sem=self.send.at[sem],
            recv_sem=self.recv.at[sem],
            device_id=partner,
            device_id_type=pl.DeviceIdType.MESH,
        )

    def bases(self, count):
        return (self.first, self.apart)[:count]

    def begin(self):
        if self.at == len(self.plan):
            return
        way, (kind, names, size, (row, sem), count), free = self.plan[self.at]
        flight = []
        if kind == "merge":
            source = self.buffer.at[self.rows_at(self.apart, self.lo, size), :]
            target = self.received.at[pl.ds(row, size), :]
            flight.append(self.copy(source, target, sem, self.links.partner(names)))
        elif way == "reduce":
            part = size // (1 << len(names)) if kind == "halve" else size
            for base in self.bases(count):
                for number, flipped in subsets(names):
                    first = self.lo
                    if kind == "halve":
                        first = first + self.chunk(names, flipped) * part
                    source = self.buffer.at[self.rows_at(base, first, part), :]
                    target = self.received.at[pl.ds(row, part), :]
                    flight.append(self.copy(source, target, sem, self.links.partner(flipped)))
                    row, sem = row + part, sem + 1
        else:
            part = size // (1 << len(names))
            before = self.offsets[(kind, tuple(names), size)]
            pl.semaphore_wait(self.free.at[free], (1 << len(names)) - 1)
            sem = sem + count * ((1 << len(names)) - 1)
            first = before + self.chunk(names, []) * part
            for number, flipped in subsets(names):
                mine = self.buffer.at[self.rows_at(self.first, first, part), :]
                flight.append(self.copy(mine, mine, sem, self.links.partner(flipped)))
                sem += 1
        for copy in flight:
            copy.start()
        self.flight = flight

    def end(self):
        if not self.flight:
            return
        way, (kind, names, size, (row, sem), count), free = self.plan[self.at]
        for copy in self.flight:
            copy.wait()
        self.flight = []
        self.at += 1
        if way == "gather":
            return
        if kind == "merge":
            self.add(self.first, self.lo, size, [row])
            return
        part = size
        parts = (1 << len(names)) - 1
        if kind == "halve":
            part = size // (parts + 1)
            self.offsets[(kind, tuple(names), size)] = self.lo
            self.lo = self.lo + self.chunk(names, []) * part
            for number, flipped in subsets(names):
                pl.semaphore_signal(
                    self.free.at[free],
                    inc=1,
                    device_id=self.links.partner(flipped),
                    device_id_type=pl.DeviceIdType.MESH,
                )
        for base in self.bases(count):
            self.add(base, self.lo, part, [row + i * part for i in range(parts)])
            row += parts * part

    def add(self, base, first, size, rows):
        block = 16
        for candidate in (32, 48, 64, 80, 96):
            if size % candidate == 0:
                block = candidate

        def body(step, carry):
            here = self.rows_at(base, first + step * block, block)
            terms = [self.buffer[here, :].astype(F32)]
            for row in rows:
                at = pl.ds(pl.multiple_of(row + step * block, 16), block)
                terms.append(self.received[at, :].astype(F32))
            while len(terms) > 1:
                terms = [a + b for a, b in zip(terms[0::2], terms[1::2])]
            self.buffer[here, :] = low(terms[0])
            return carry

        lax.fori_loop(0, size // block, body, 0)

    def advance(self):
        self.end()
        self.begin()

    @property
    def done(self):
        return self.at == len(self.plan)


def meet(links, partners):
    barrier = pltpu.get_barrier_semaphore()
    for names in partners:
        pl.semaphore_signal(
            barrier, inc=1, device_id=links.partner(names), device_id_type=pl.DeviceIdType.MESH
        )
    pl.semaphore_wait(barrier, len(partners))


class Swap:
    def __init__(self, links, pairs, sends, receives):
        self.links, self.pairs, self.sends, self.receives = links, pairs, sends, receives

    def copies(self, step):
        result = []
        for at, (mine, theirs) in enumerate(self.pairs):
            half = mine.shape[0] // 2
            rows = pl.ds(pl.multiple_of(self.links.bit(0) * half, 16), half)
            result.append(
                pltpu.make_async_remote_copy(
                    src_ref=(mine if step == 0 else theirs).at[rows, :],
                    dst_ref=theirs.at[rows, :],
                    send_sem=self.sends.at[step, at],
                    recv_sem=self.receives.at[step, at],
                    device_id=self.links.partner(["t"] if step == 0 else [0]),
                    device_id_type=pl.DeviceIdType.MESH,
                )
            )
        return result

    def start(self, step):
        for copy in self.copies(step):
            copy.start()

    def wait(self, step):
        for copy in self.copies(step):
            copy.wait()


class Place:
    def __init__(self, small, large):
        ds, dl = small.columns, large.columns
        self.first, self.size, at = {}, {}, 0
        for name, rows in (
            ("small_up", ds), ("small_down", ds), ("large_up", 2 * dl), ("large_down", 2 * dl),
            ("other", 2 * ds + 4 * dl),
            ("large_cross", 4 * dl), ("small_enter", ds), ("small_leave", ds),
            ("large_enter", ds), ("large_leave", ds), ("small_cross", 2 * ds),
            ("large_out", dl), ("large_in", 3 * dl), ("small_heads", 2 * ds), ("tables", 64),
        ):
            self.first[name], self.size[name] = at, rows
            at += rows
        self.total = at

    def rows(self, name, part=0, size=None):
        first = self.first[name] + part
        return slice(first, first + (self.size[name] if size is None else size))


class CrossGrads:
    def __init__(self, own, other, place, buffer):
        self.own, self.other, self.place, self.buffer = own, other, place, buffer
        self.kept = {}

    def put(self, name, part, values):
        first = self.place.first[name] + part
        self.buffer[first : first + values.shape[0], :] = low(values)

    def cross_in(self, third, values):
        if self.other.index == 1:
            self.put("large_cross", third * self.other.columns, values)
            return
        self.kept[third] = values
        if third == 1:
            self.put("small_cross", 0, jnp.concatenate([self.kept[0], values], 1))
        if third == 2:
            self.put(
                "small_cross", self.other.columns, jnp.concatenate([values, self.kept["out"]], 1)
            )

    def cross_out(self, values):
        if self.other.index == 1:
            self.put("large_cross", 3 * self.other.columns, values)
        else:
            self.kept["out"] = values

    def enter(self, values):
        if self.own.index == 0:
            self.put("small_enter", 0, values)
        else:
            self.put("large_enter", 0, values)

    def leave(self, values):
        if self.own.index == 1:
            self.put("large_leave", 0, values)
        else:
            self.put("small_leave", 0, values)


def mlp_grads(b, r, place, buffer, tick):
    half, columns = b.hidden // 2, b.columns
    name = ("small", "large")[b.index]
    for part in range(2):
        first = place.first["other"] * part + place.first[name + "_up"]
        for at in range(0, half, LANES):
            up = nt(r.c[...], r.g[part * half + at : part * half + at + LANES, :])
            buffer[first : first + columns, :] = low(up[0:columns])
            first += columns
            row = b.index + at // LANES
            r.bias_rows[part, row : row + 1, :] = up[columns : columns + 1]
        tick(part)
    r.table[5 + 5 : 5 + 6, :] = nt(r.u[b.hidden : b.hidden + 16, :], r.zg[...])[0:1]
    for part in range(2):
        mine = slice(part * half, (part + 1) * half)
        first = place.first["other"] * part + place.first[name + "_down"]
        if b.index == 0:
            buffer[first : first + columns, :] = low(nt(r.zg[...], r.u[mine, :]))
        else:
            buffer[first : first + half, :] = low(nt(r.u[mine, :], r.zg[...]))
        tick(2 + part)


def out_grads(b, r):
    w_out = nt(r.o[...], r.yg[...])
    r.table[5 + 3 : 5 + 4, :] = w_out[b.columns : b.columns + 1, :]
    return w_out[0 : b.columns]


def in_grads(b, r, third):
    columns = b.columns
    w_in = nt(r.a[...], r.qkv[third * columns : (third + 1) * columns, :])
    if third != 1:
        row = 5 + 1 + third // 2
        r.table[row : row + 1, :] = w_in[columns : columns + 1, :]
    return w_in[0:columns]


def large_in_grads(b, r, place, buffer):
    for third in range(3):
        first = place.first["large_in"] + third * b.columns
        buffer[first : first + b.columns, :] = low(in_grads(b, r, third))


def small_head_grads(b, r, place, buffer):
    columns, first = b.columns, place.first["small_heads"]
    thirds = [in_grads(b, r, third) for third in range(3)] + [out_grads(b, r)]
    for half in range(2):
        at = first + half * columns
        buffer[at : at + columns, :] = low(jnp.concatenate(thirds[2 * half : 2 * half + 2], 1))


NAMES = (
    "counts", "small_rows", "large_rows", "small_cot", "large_cot",
    "small_in", "small_out", "small_up", "small_down",
    "large_in", "large_out", "large_up", "large_down",
    "small_enter", "large_cross_in", "large_cross_out", "small_leave",
    "large_enter", "small_cross_in", "small_cross_out", "large_leave",
    "small_gains", "small_shifts", "large_gains", "large_shifts", "small_up_bias", "large_up_bias",
)
OUTS = (
    "small_out", "large_out", "small_rows", "large_rows",
    "small_heads_in", "small_heads_out", "small_up", "small_up_bias", "small_down",
    "large_heads_in", "large_heads_out", "large_up", "large_up_bias", "large_down",
    "small_enter", "large_cross_in", "large_cross_out", "small_leave",
    "large_enter", "small_cross_in", "small_cross_out", "large_leave",
    "small_gains", "small_shifts", "large_gains", "large_shifts",
)
def scratch_of(b):
    d, t, h = b.columns, b.tokens, b.hidden
    scratch = dict(
        logs=pltpu.VMEM((8, t), F32),
        stats=pltpu.VMEM((8, t), F32),
        index=pltpu.VMEM((8, t), jnp.int32),
        x=pltpu.VMEM((d, t), BF16),
        cotT=pltpu.VMEM((d, t), BF16),
        a=pltpu.VMEM((d + 16, t), BF16),
        qkv=pltpu.VMEM((3 * d, t), BF16),
        o=pltpu.VMEM((d + 16, t), BF16),
        y=pltpu.VMEM((d, t), F32),
        c=pltpu.VMEM((d + 16, t), BF16),
        u=pltpu.VMEM((h + 16, t), BF16),
        g=pltpu.VMEM((h, t), BF16),
        z=pltpu.VMEM((d, t), F32),
        n=pltpu.VMEM((d, t), BF16),
        out=pltpu.VMEM((d, t), BF16),
        sp=pltpu.VMEM((2 * STACK, t), BF16),
        maps=pltpu.VMEM((2 * STACK, d), BF16),
        cls=pltpu.VMEM((CLS, d), F32),
        cot_cls=pltpu.VMEM((CLS, d), F32),
        new_cls=pltpu.VMEM((CLS, d), BF16),
        cls_grad=pltpu.VMEM((CLS, d), F32),
        table=pltpu.VMEM((24, d), F32),
        tabT=pltpu.VMEM((d, 128), F32),
        w_inT=pltpu.VMEM((3 * d, d), BF16),
        w_upT=pltpu.VMEM((h, d), BF16),
        w_downT=pltpu.VMEM((d, h), BF16),
        other_up=pltpu.VMEM((d, h // 2), BF16),
    )
    if b.index == 0:
        scratch.update(og=pltpu.VMEM((d, t), BF16), other_down=pltpu.VMEM((d, h // 2), BF16))
    else:
        scratch.update(other_down=pltpu.VMEM((h // 2, d), BF16))
    return scratch


def columns_of(rows):
    rows = rows.astype(F32)
    return jnp.concatenate([rows, jnp.zeros((128 - rows.shape[0], rows.shape[1]), F32)], 0).T


def prepare(b, r):
    r.tabT[...] = columns_of(jnp.concatenate([r.gains[...].astype(F32), r.shifts[...].astype(F32)], 0))
    r.w_inT[...] = r.w_in[...].T
    r.a[b.columns : b.columns + 16, :] = jnp.ones((16, b.tokens), BF16)
    r.o[b.columns : b.columns + 16, :] = jnp.ones((16, b.tokens), BF16)
    r.c[b.columns : b.columns + 16, :] = jnp.ones((16, b.tokens), BF16)
    r.u[b.hidden : b.hidden + 16, :] = jnp.ones((16, b.tokens), BF16)
    r.table[...] = jnp.zeros_like(r.table)


def prepare_mlp(b, r):
    half, columns = b.hidden // 2, b.columns
    for part in range(2):
        mine = slice(part * half, (part + 1) * half)
        biases = columns_of(r.up_bias[part][0:16, :])
        for at in range(0, half, columns):
            place = b.index + at // LANES
            column = 19 + (part * half + at) // columns
            r.tabT[:, column : column + 1] = biases[at % LANES : at % LANES + columns, place : place + 1]
        r.w_upT[mine, :] = r.up[part][...].T
        r.w_downT[:, mine] = r.down[part][...].T if b.index else r.down[part][...]


class Refs:
    pass


PHASES = {
    "large_in": (((0,), "halve"), (("t", 1,), "halve"), ((2,), "halve"), ((3,), "halve")),
    "tail": (((0,), "halve"), (("t", 1,), "halve"), ((2, 3,), "full")),
    "mixed": (((0,), "halve"), (("t",), "halve"), ((1,), "full"), ((2, 3,), "halve")),
    "large_down": (((0,), "halve"), ((1,), "halve"), ((2,), "halve"), (("t",), "merge"), ((3,), "full")),
    "cross_d": (((0,), "halve"), ((1,), "halve"), (("t",), "halve"), ((2, 3,), "halve")),
    "tables": (((0,), "full"), (("t", 1,), "full"), ((2, 3,), "full")),
    "cross_a": (((0,), "halve"), (("t", 1,), "halve"), ((2, 3,), "full")),
    "small_mlp": (((0,), "halve"), ((1,), "halve"), (("t",), "merge"), ((2,), "full"), ((3,), "full")),
    "large_up": (((0,), "halve"), ((1,), "halve"), ((2,), "halve"), (("t",), "merge"), ((3,), "full")),
}
TICKS = {
    "crossend": ("cross_d", "cross_a",),
    "bcross_l2": ("cross_d", "cross_a",),
    "gmlp_l1": ("large_up",),
    "gmlp_l3": ("cross_a", "large_up", "large_down",),
    "gol": ("cross_d", "mixed",),
    "batt_l0": ("mixed", "large_down",),
    "batt_l1": ("cross_d",),
    "batt_l2": ("mixed", "cross_a", "large_up",),
    "ghead_l": ("large_in",),
    "bcross_s2": ("cross_d",),
    "bcross_s4": ("large_in",),
    "bmlp_s0": ("large_down",),
    "bmlp_s1": ("large_up",),
    "bmlp_s2": ("mixed",),
    "gmlp_s3": ("cross_d", "small_mlp",),
    "batt_s0": ("small_mlp", "large_up",),
    "batt_s1": ("large_in", "large_down", "cross_a",),
    "batt_s2": ("mixed", "cross_d", "cross_a",),
    "batt_s3": ("large_in", "large_down", "small_mlp", "large_up",),
    "ghead_s": ("tail",),
    "bnorm_l1": ("tail", "small_mlp",),
    "bnorm_l2": ("large_in", "mixed",),
    "bnorm_s4": ("large_up",),
    "tables": ("large_down", "tables",),
    "out_l0": ("cross_d",),
    "out_l1": ("large_in", "tables", "small_mlp",),
    "out_l2": ("tail", "cross_d",),
    "out_l3": ("mixed",),
    "out_s0": ("large_down",),
    "out_s1": ("mixed",),
    "out_s3": ("large_up",),
    "back_l0": ("large_in",),
    "back_l1": ("large_up",),
    "back_l2": ("tables",),
    "back_s0": ("small_mlp",),
    "back_s3": ("large_down",),
}
REST = (
    "tail", "large_down", "small_mlp", "large_in", "small_mlp", "tables", "large_in", "tail", "tail",
)


class Plan:
    def __init__(self, place, small, large, dp):
        ds, dl, first = small.columns, large.columns, place.first
        self.dp_bits = dp.bit_length() - 1
        assert dp == 1 << self.dp_bits
        more = [(tuple(range(at, min(at + 2, self.dp_bits))), "halve") for at in range(4, self.dp_bits, 2)]
        self.pool = Pool()
        other, cross, heads = first["other"], first["large_cross"], first["large_in"]
        tail = heads + 1024
        places = {
            "large_up": (first["large_up"], 2 * dl, other + first["large_up"]),
            "large_down": (first["large_down"], 2 * dl, other + first["large_down"]),
            "small_mlp": (first["small_up"], 2 * ds, other + first["small_up"]),
            "cross_d": (cross + 0, 1536, None),
            "cross_a": (cross + 1536, 1024, None),
            "mixed": (cross + 2560, first["large_in"] - cross - 2560, None),
            "large_in": (heads, 1024, None),
            "tail": (tail, first["tables"] - tail, None),
            "tables": (first["tables"], 64, None),
        }
        self.groups, self.met = {}, []
        for name, (begin, rows, apart) in places.items():
            group = Group(self.pool, begin, rows, list(PHASES[name]) + more, apart)
            self.groups[name] = group
            for step in group.steps:
                for number, flipped in subsets(step[1]):
                    if flipped not in self.met:
                        self.met.append(flipped)


def layer_kernel(small, large, place, plan, keys, solo, *refs):
    ins = dict(zip(NAMES, refs))
    refs = refs[len(NAMES) :]
    packed, small_out, large_out, small_grad, large_grad = refs[:5]
    refs = refs[5:]
    groups = []
    links = Links(plan.dp_bits)
    links.bind(solo)
    for b, name in ((small, "small"), (large, "large")):
        r = Refs()
        for key in keys[b.index]:
            setattr(r, key, refs[0])
            refs = refs[1:]
        r.w_in, r.w_out = ins[name + "_in"], ins[name + "_out"]
        r.up = (ins[name + "_up"], r.other_up)
        r.down = (ins[name + "_down"], r.other_down)
        r.gains, r.shifts = ins[name + "_gains"], ins[name + "_shifts"]
        r.enter, r.leave = ins[name + "_enter"], ins[name + "_leave"]
        r.cross_in, r.cross_out = ins[name + "_cross_in"], ins[name + "_cross_out"]
        r.zg, r.yg = r.n, r.cotT
        groups.append((b, r))
    (bs, rs), (bl, rl) = groups
    work, mask, sums, own_biases = refs[:4]
    biases, other_biases, buffer, received, send, recv, free, swap_send, swap_recv, out_sem, in_sem = refs[4:]
    for b, r in groups:
        r.bias_rows, r.mask, r.sums = biases, mask, sums
        r.up_bias = (own_biases, other_biases)
    half_s = bs.hidden // 2
    rs.down_times = lambda part, z: tn(rs.w_downT[:, part * half_s : (part + 1) * half_s], z)
    rl.down_times = lambda part, z: nn(rl.down[part][...], z)
    rs.og_rows = lambda slot, rows: rs.og.at[rows, slot_columns(bs, slot)]

    def large_og(slot, rows):
        size = rows.stop - rows.start
        if isinstance(slot, int):
            return rl.w_upT.at[slot * bl.columns + rows.start : slot * bl.columns + rows.stop, :]
        return rl.w_upT.at[pl.ds(pl.multiple_of(slot * bl.columns + rows.start, 64), size), :]

    rl.og_rows = large_og
    rs.staged = rs.sp.at[:, 0 : bs.rows]
    rl.staged = rl.w_inT.at[0 : bl.rows, :]
    biases[...] = jnp.zeros_like(biases)
    bias = [ins["small_up_bias"][...]]
    bias += [ins["large_up_bias"][at : at + LANES] for at in range(0, bl.hidden // 2, LANES)]
    bias = [value.astype(F32).reshape(1, LANES) for value in bias]
    own_biases[...] = low(jnp.concatenate(bias + [jnp.zeros((32 - len(bias), LANES), F32)], 0))
    for group in plan.groups.values():
        group.bind(links, buffer, received, send, recv, free)
    swap = Swap(
        links,
        (
            (ins["large_up"], rl.other_up),
            (ins["large_down"], rl.other_down),
            (ins["small_up"], rs.other_up),
            (ins["small_down"], rs.other_down),
            (own_biases, other_biases),
        ),
        swap_send,
        swap_recv,
    )
    arrivals = []
    for at, name in enumerate(("large_rows", "large_cot")):
        target = rl.u.at[0 : bl.rows, at * bl.columns : (at + 1) * bl.columns]
        arrivals.append(pltpu.make_async_copy(ins[name], target, in_sem.at[at]))
        arrivals[-1].start()
    rs.rows, rs.cot = ins["small_rows"], ins["small_cot"]
    rl.rows = rl.g.at[0 : bl.columns, 0 : bl.rows]
    rl.cot = rl.g.at[bl.columns : 2 * bl.columns, 0 : bl.rows]

    out_copies = {}

    def write_out(name, source, target):
        copy = pltpu.make_async_copy(source, target, out_sem.at[len(out_copies)])
        copy.start()
        out_copies[name] = copy

    def step(name):
        group = plan.groups[name]
        if solo is None and not group.done:
            group.advance()
            if group.done:
                rows = slice(group.first, group.first + group.rows)
                write_out(name, buffer.at[rows, :], packed.at[rows, :])

    def tick(label):
        for name in TICKS.get(label, ()):
            step(name)

    def ticks(stage, count):
        if any(stage + str(part) in TICKS for part in range(count)):
            return lambda part: tick(stage + str(part))
        return None

    def always(stage):
        return lambda part: tick(stage + str(part))

    if solo is None:
        meet(links, plan.met)
        swap.start(0)
    else:
        for mine, theirs in swap.pairs:
            theirs[...] = mine[...]
    prepare(bs, rs)
    lay_out(bs, rs, ins["counts"])
    bring_in(bs, rs)
    prepare(bl, rl)
    for at, copy in enumerate(arrivals):
        copy.wait()
        (rl.rows, rl.cot)[at][...] = rl.u[0 : bl.rows, at * bl.columns : (at + 1) * bl.columns].T
    lay_out(bl, rl, ins["counts"])
    bring_in(bl, rl)
    forward_attention(bl, rl, [rl.z], [rl.w_downT])
    if solo is None:
        swap.wait(0)
        swap.start(1)
    forward_attention(bs, rs, [rl.z, work], [rl.w_downT])
    if solo is None:
        swap.wait(1)
    prepare_mlp(bl, rl)
    prepare_mlp(bs, rs)
    forward_mlp(bl, rl)
    forward_mlp(bs, rs)
    both = [
        cross(bs, rs, bl, rl, CrossGrads(bs, bl, place, buffer)),
        cross(bl, rl, bs, rs, CrossGrads(bl, bs, place, buffer)),
    ]
    while both:
        both = [one for one in both if next(one, both) is None]
    def large_block():
        backward_cross(bl, rl, work, ticks("bcross_l", bl.slots))
        backward_mlp(bl, rl, work, ticks("bmlp_l", bl.slots))
        mlp_grads(bl, rl, place, buffer, always("gmlp_l"))
        first = place.first["large_out"]
        buffer[first : first + bl.columns, :] = low(out_grads(bl, rl))
        tick("gol")

    def large_attention():
        wide = [rl.y, work]
        backward_attention(bl, rl, wide, [rl.w_downT], [rl.w_inT], ticks("batt_l", bl.slots))
        large_in_grads(bl, rl, place, buffer)
        tick("ghead_l")

    def small_block():
        backward_cross(bs, rs, work, ticks("bcross_s", bs.slots))
        backward_mlp(bs, rs, work, ticks("bmlp_s", bs.slots))
        mlp_grads(bs, rs, place, buffer, always("gmlp_s"))

    def small_attention():
        wide = [rl.y, work]
        backward_attention(bs, rs, wide, [rl.w_downT], [rl.g], ticks("batt_s", bs.slots))
        small_head_grads(bs, rs, place, buffer)
        tick("ghead_s")

    def norms():
        backward_first_norm(bl, rl, work, ticks("bnorm_l", bl.slots))
        backward_first_norm(bs, rs, work, ticks("bnorm_s", bs.slots))
        put_tables(links, place, buffer, rs, rl, biases)
        tick("tables")

    def outputs():
        put_out(bl, rl, ticks("out_l", 4))
        write_out("large_out", rl.staged, large_out)
        put_out(bs, rs, ticks("out_s", 4))
        write_out("small_out", rs.staged, small_out)
        out_copies["large_out"].wait()
        put_back(bl, rl, rl.x, ticks("back_l", 4))
        write_out("large_grad", rl.staged, large_grad)
        out_copies["small_out"].wait()
        put_back(bs, rs, rs.x, ticks("back_s", 4))
        write_out("small_grad", rs.staged, small_grad)

    tick("crossend")
    large_block()
    large_attention()
    small_block()
    small_attention()
    norms()
    outputs()
    for name in REST:
        step(name)
    while any(not group.done for group in plan.groups.values()) and solo is None:
        for name in plan.groups:
            step(name)
    for name, copy in out_copies.items():
        if name not in ("large_out", "small_out"):
            copy.wait()


def put_tables(links, place, buffer, rs, rl, biases):
    ds = rs.table.shape[1]
    own, other = biases[0, 0:8, :], biases[1, 0:8, :]
    first = links.tensor == 0
    rows = [
        rl.table[...],
        jnp.concatenate([rs.table[...], jnp.zeros((24, LANES - ds), F32)], 1),
        jnp.where(first, own, other),
        jnp.where(first, other, own),
    ]
    buffer[place.rows("tables"), :] = low(jnp.concatenate(rows, 0))


def unpack_kernel(place, ds, dl, parts, *refs):
    (packed, small_out, large_out, small_grad, large_grad), refs = refs[:5], refs[5:]
    outs, refs = dict(zip(OUTS, refs)), refs[len(OUTS) :]
    got, got_small, got_large, out_small, out_large = refs[:5]
    refs = refs[5:]
    stages, refs = dict(zip(OUTS[2:], refs)), refs[len(OUTS) - 2 :]
    in_sem, out_sem = refs
    copies, arriving = [], {}

    def bring(name, source, target):
        arriving[name] = pltpu.make_async_copy(source, target, in_sem.at[len(arriving)])
        arriving[name].start()

    def leave(source, target):
        copies.append(pltpu.make_async_copy(source, target, out_sem.at[len(copies)]))
        copies[-1].start()

    for name, first, rows in parts:
        bring(name, packed.at[first : first + rows, :], got.at[first : first + rows, :])
    bring("small_rows", small_grad, got_small)
    bring("large_rows", large_grad, got_large)
    bring("small_out", small_out, out_small)
    bring("large_out", large_out, out_large)

    def read(name, part, rows):
        first = place.first[name] + part
        return got[first : first + rows, :].astype(F32)

    def done(*names):
        for name in names:
            leave(stages[name], outs[name])

    arriving["mlp"].wait()
    for part in range(2):
        stages["large_up"][:, part * dl : (part + 1) * dl] = read("large_up", part * dl, dl)
    done("large_up")
    stages["large_down"][...] = read("large_down", 0, 2 * dl)
    stages["small_up"][...] = read("small_up", 0, ds)
    stages["small_down"][...] = read("small_down", 0, ds)
    done("large_down", "small_up", "small_down")
    for name, into, out, at in (("cross", "large_cross", "large_cross", 3), ("heads", "large_in", "large_out", 0)):
        arriving[name].wait()
        for third in range(3):
            stages["large_" + name + "_in"][:, third * dl : (third + 1) * dl] = read(
                into, third * dl, dl
            )
        stages["large_" + name + "_out"][...] = read(out, at * dl, dl)
        second = read("small_" + name, ds, ds)
        stages["small_" + name + "_in"][:, 0:LANES] = read("small_" + name, 0, ds)
        stages["small_" + name + "_in"][:, LANES:] = second[:, 0:ds]
        stages["small_" + name + "_out"][...] = second[:, ds:]
        done("large_" + name + "_in", "large_" + name + "_out", "small_" + name + "_in", "small_" + name + "_out")
        if name == "cross":
            for key in ("small_enter", "small_leave", "large_enter", "large_leave"):
                stages[key][...] = read(key, 0, ds)
                done(key)
    for name, ref in (("small_rows", got_small), ("large_rows", got_large)):
        arriving[name].wait()
        stages[name][...] = ref[...].astype(F32)
        done(name)
    for name, ref in (("small_out", out_small), ("large_out", out_large)):
        arriving[name].wait()
        leave(ref, outs[name])
    arriving["tables"].wait()
    first = place.first["tables"]
    tables = got[first : first + 64, :].astype(F32)
    stages["large_gains"][...] = tables[0:5]
    stages["large_shifts"][...] = tables[5:19]
    stages["small_gains"][...] = tables[24:29, 0:ds]
    stages["small_shifts"][...] = tables[29:43, 0:ds]
    mine = jnp.where(lax.axis_index("tensor") == 0, tables[48:56], tables[56:64])
    stages["small_up_bias"][...] = mine[0]
    stages["large_up_bias"][0:LANES] = mine[1]
    stages["large_up_bias"][LANES:] = mine[2]
    done("large_gains", "large_shifts", "small_gains", "small_shifts", "small_up_bias", "large_up_bias")
    for copy in copies:
        copy.wait()


TURNED = ("small_out", "small_rows", "small_down", "small_leave", "large_enter")


def run_layer(args, dp, solo=None):
    (
        small_rows, large_rows, counts, small_cot, large_cot,
        small_in, small_out, small_up, small_up_bias, small_down,
        large_in, large_out, large_up, large_up_bias, large_down,
        small_enter, large_cross_in, large_cross_out, small_leave, large_enter,
    ) = args[:20]
    ds, dl = small_rows.shape[1], large_rows.shape[1]
    small = Branch(0, small_rows.shape[0], ds, 2 * small_up.shape[1], 256, ((0, 4), (1, 5), (2,), (3,), (6,)))
    large = Branch(1, large_rows.shape[0], dl, 2 * large_up.shape[1], 384, ((0, 1, 4), (2, 3, 5), (6,)))
    place = Place(small, large)
    plan = Plan(place, small, large, dp)
    inputs = (
        counts, small_rows.T, large_rows, small_cot.T, large_cot,
        small_in, small_out, small_up, small_down.T,
        large_in, large_out, large_up, large_down,
        small_enter, large_cross_in, large_cross_out, small_leave.T, large_enter.T,
    ) + args[20:] + (small_up_bias, large_up_bias)
    keys = tuple(tuple(scratch_of(b)) for b in (small, large))
    scratch = [s for b in (small, large) for s in scratch_of(b).values()]
    copies = pltpu.SemaphoreType.DMA
    scratch += [
        pltpu.VMEM((dl, large.tokens), F32),
        pltpu.VMEM((large.width, large.width), F32),
        pltpu.VMEM((2, dl, 128), F32),
        pltpu.VMEM((32, LANES), BF16),
        pltpu.VMEM((2, 16, LANES), F32),
        pltpu.VMEM((32, LANES), BF16),
        pltpu.VMEM((place.total, LANES), BF16),
        pltpu.VMEM((plan.pool.rows, LANES), BF16),
        copies((plan.pool.copies,)),
        copies((plan.pool.copies,)),
        pltpu.SemaphoreType.REGULAR((plan.pool.signals,)),
        copies((2, 5)),
        copies((2, 5)),
        copies((20,)),
        copies((2,)),
    ]
    shape = jax.ShapeDtypeStruct
    vmem, hbm = pl.BlockSpec(memory_space=pltpu.VMEM), pl.BlockSpec(memory_space=pl.ANY)
    middle = (
        shape((place.total, LANES), BF16),
        shape((ds, small.rows), BF16),
        shape((large.rows, dl), BF16),
        shape((ds, small.rows), BF16),
        shape((large.rows, dl), BF16),
    )
    values = pl.pallas_call(
        functools.partial(layer_kernel, small, large, place, plan, keys, solo),
        out_shape=middle,
        in_specs=[pl.BlockSpec(memory_space=pltpu.SMEM)]
        + [hbm if name in ("large_rows", "large_cot") else vmem for name in NAMES[1:]],
        out_specs=(hbm,) * 5,
        scratch_shapes=scratch,
        compiler_params=pltpu.CompilerParams(
            vmem_limit_bytes=VMEM_LIMIT,
            collective_id=0 if solo is None else None,
            has_side_effects=True,
        ),
        name="layer",
    )(*inputs)
    shapes = dict(
        small_out=shape((ds, small.rows), BF16),
        large_out=shape(large_rows.shape, BF16),
        small_rows=shape((ds, small.rows), F32),
        large_rows=shape(large_rows.shape, F32),
        small_up_bias=shape(small_up_bias.shape, F32),
        large_up_bias=shape(large_up_bias.shape, F32),
    )
    for name, value in zip(OUTS[4:], args[5:]):
        turned = value.shape[::-1] if name in TURNED else value.shape
        shapes.setdefault(name, shape(turned, F32))
    first = place.first
    cross_first = first["large_cross"]
    parts = (
        ("mlp", 0, first["other"]),
        ("cross", cross_first, first["large_out"] - cross_first),
        ("heads", first["large_out"], first["tables"] - first["large_out"]),
        ("tables", first["tables"], 64),
    )
    results = pl.pallas_call(
        functools.partial(unpack_kernel, place, ds, dl, parts),
        out_shape=tuple(shapes[name] for name in OUTS),
        in_specs=(hbm,) * 5,
        out_specs=(hbm,) * len(OUTS),
        scratch_shapes=[
            pltpu.VMEM((place.total, LANES), BF16),
        ]
        + [pltpu.VMEM((ds, small.rows), BF16), pltpu.VMEM(large_rows.shape, BF16)] * 2
        + [pltpu.VMEM(shapes[name].shape, F32) for name in OUTS[2:]]
        + [copies((8,)), copies((len(OUTS),))],
        compiler_params=pltpu.CompilerParams(vmem_limit_bytes=VMEM_LIMIT),
        name="unpack",
    )(*values)

    def restore(name, value):
        return value.T if name in TURNED else value

    return tuple(restore(name, value) for name, value in zip(OUTS, results))


def solution(mesh):
    both = ("dp", "tensor")
    rows = P(both, None)
    mlp = (P(None, "tensor"), P("tensor"), P("tensor", None))

    def shards(*args):
        return run_layer(args, mesh.shape["dp"])

    return jax.shard_map(
        shards,
        mesh=mesh,
        in_specs=(rows, rows, P(None, both), rows, rows)
        + ((P(), P()) + mlp) * 2
        + (P(),) * 12,
        out_specs=(rows,) * 4 + ((P(), P()) + mlp) * 2 + (P(),) * 12,
        check_vma=False,
    )
```

```python
import functools
import collections
import jax
import jax.numpy as jnp
from jax import lax
from jax.experimental import pallas as pl
from jax.experimental.pallas import tpu as pltpu
from jax.sharding import PartitionSpec as P

HEADS = 6
VMEM_LIMIT = 64 * 1024 * 1024
NEGATIVE = -1e30
EPSILON = 1e-06
F32, BF16 = jnp.float32, jnp.bfloat16
LANES = 384
CLS = 16
STACK = HEADS * CLS

GLOBAL_ROWS, LOCAL_ROWS = (197, 145), (37, 65)
BLOCK = 32
LOG2E = 1.4426950408889634


def low(values):
    return values.astype(BF16)


def dot(left, right, left_axis, right_axis):
    return lax.dot_general(
        left, right, (((left_axis,), (right_axis,)), ((), ())), preferred_element_type=F32
    )


def nn(left, right):
    return dot(left, right, 1, 0)


def nt(left, right):
    return dot(left, right, 1, 1)


def tn(left, right):
    return dot(left, right, 0, 0)


class Branch:
    def __init__(self, index, rows, columns, hidden, width, layout):
        self.index, self.rows, self.columns, self.hidden = index, rows, columns, hidden
        self.head = columns // HEADS
        self.width, self.slots = width, len(layout)
        self.tokens = width * self.slots
        self.pieces = []
        self.bounds = []
        g_rows, l_rows = GLOBAL_ROWS[index], LOCAL_ROWS[index]
        for slot, crops in enumerate(layout):
            lane, ends = 0, []
            for crop in crops:
                length = g_rows if crop < 4 else l_rows if crop < 6 else rows - 4 * g_rows - 2 * l_rows
                self.pieces.append((slot * width + lane, length, crop))
                lane += length
                ends.append(lane)
            assert lane <= width
            self.bounds.append(ends)


def norm(values, axis):
    center = values - jnp.mean(values, axis, keepdims=True)
    scale = lax.rsqrt(jnp.mean(center * center, axis, keepdims=True) + EPSILON)
    return center * scale, scale


def fold(values):
    total = values[0:8]
    for at in range(8, values.shape[0], 8):
        total = total + values[at : at + 8]
    return total


def fold_lanes(values):
    total = values[:, 0:128]
    for at in range(128, values.shape[1], 128):
        total = total + values[:, at : at + 128]
    return total


def chunks(columns):
    return [slice(at, at + BLOCK) for at in range(0, columns, BLOCK)]


def norm_columns(load, columns, keep):
    total = sum(fold(load(rows)) for rows in chunks(columns))
    mean = jnp.sum(total, 0, keepdims=True) * (1.0 / columns)
    spread = 0.0
    for rows in chunks(columns):
        center = load(rows) - mean
        spread = spread + fold(center * center)
    spread = jnp.sum(spread, 0, keepdims=True) * (1.0 / columns)
    scale = lax.rsqrt(spread + EPSILON)
    keep(mean, scale)
    return mean, scale


def norm_columns_back(load, grad, columns, mean, scale, gain, sums, store):
    first = second = 0.0
    for rows in chunks(columns):
        unit = (load(rows) - mean) * scale
        back = grad(rows)
        both = back * unit
        sums[0, rows, :] += fold_lanes(back)
        sums[1, rows, :] += fold_lanes(both)
        first = first + fold(back * gain(rows))
        second = second + fold(both * gain(rows))
    first = jnp.sum(first, 0, keepdims=True) * (1.0 / columns)
    second = jnp.sum(second, 0, keepdims=True) * (1.0 / columns)
    for rows in chunks(columns):
        unit = (load(rows) - mean) * scale
        store(rows, scale * (grad(rows) * gain(rows) - first - unit * second))


def norm_back(grad, unit, scale, axis):
    return scale * (
        grad
        - jnp.mean(grad, axis, keepdims=True)
        - unit * jnp.mean(grad * unit, axis, keepdims=True)
    )


def smooth_parts(values):
    chance = 0.5 + 0.5 * lax.erf(values * (0.5**0.5))
    slope = chance + values * (jnp.exp(values * values * -0.5) * 0.3989422804014327)
    return values * chance, slope


def pick(at, values):
    if isinstance(at, int):
        return values[at]
    result = values[-1]
    for place in range(len(values) - 2, -1, -1):
        result = jnp.where(at == place, values[place], result)
    return result


def iota(shape, axis):
    return lax.broadcasted_iota(jnp.int32, shape, axis)


def each_slot(branch, body, between=None):
    if between is None:
        lax.fori_loop(0, branch.slots, lambda slot, carry: body(slot) or carry, 0)
        return
    for slot in range(branch.slots):
        body(slot)
        between(slot)


def slot_columns(branch, slot):
    if isinstance(slot, int):
        return slice(slot * branch.width, (slot + 1) * branch.width)
    return pl.ds(pl.multiple_of(slot * branch.width, branch.width), branch.width)


def places(counts, b):
    starts = [jnp.int32(0)] * 7
    begin, globals_seen, locals_seen = jnp.int32(0), jnp.int32(0), jnp.int32(0)
    for crop in range(6):
        rows = counts[b.index, crop]
        is_global = counts[0, crop] == GLOBAL_ROWS[0]
        for k in range(4):
            starts[k] = jnp.where(is_global & (globals_seen == k), begin, starts[k])
        for k in range(2):
            starts[4 + k] = jnp.where((~is_global) & (locals_seen == k), begin, starts[4 + k])
        begin = begin + rows
        globals_seen = globals_seen + jnp.where(is_global, 1, 0)
        locals_seen = locals_seen + jnp.where(is_global, 0, 1)
    starts[6] = begin
    return starts


def lay_out(b, r, counts):
    starts = places(counts, b)
    lane = iota((1, b.tokens), 1)
    source = jnp.full((1, b.tokens), -1, jnp.int32)
    patch = jnp.full((1, b.tokens), -1, jnp.int32)
    cls = jnp.full((1, b.tokens), -1, jnp.int32)
    for first, length, crop in b.pieces:
        inside = (lane >= first) & (lane < first + length)
        source = jnp.where(inside, lane - first + starts[crop], source)
        if crop < 6:
            patch = jnp.where(inside & (lane > first), crop, patch)
            cls = jnp.where(lane == first, crop, cls)
    r.index[0:1, :] = source
    r.index[1:2, :] = patch
    r.index[2:3, :] = cls
    at = iota((CLS, 1), 0)
    first_rows = jnp.full((CLS, 1), -1, jnp.int32)
    for crop in range(6):
        first_rows = jnp.where(at == crop, starts[crop], first_rows)
    chosen = low((iota((CLS, b.rows), 1) == first_rows).astype(F32))
    r.cot_cls[...] = nt(chosen, r.cot[...])


def bring_in(b, r):
    def body(slot):
        cols = slot_columns(b, slot)
        chosen = low((iota((b.rows, b.width), 0) == r.index[0:1, cols]).astype(F32))
        r.x[:, cols] = low(nn(r.rows[...], chosen))
        keep = r.index[2:3, cols] < 0
        r.cotT[:, cols] = low(jnp.where(keep, nn(r.cot[...], chosen), 0.0))

    each_slot(b, body)


def slot_mask(b, slot):
    ends = [pick(slot, [e[min(i, len(e) - 1)] for e in b.bounds]) for i in range(3)]

    def segment(axis):
        at = iota((b.width, b.width), axis)
        total = jnp.zeros((b.width, b.width), jnp.int32)
        for end in ends[: max(len(e) for e in b.bounds)]:
            total = total + (at >= end).astype(jnp.int32)
        return total

    return jnp.where(segment(0) == segment(1), 0.0, NEGATIVE)


def squares(b, refs):
    result = []
    for ref in refs:
        for row in range(0, ref.shape[0] - b.width + 1, b.width):
            for lane in range(0, ref.shape[1] - b.width + 1, b.width):
                result.append(ref.at[row : row + b.width, lane : lane + b.width])
    return result


def parts_of(b, h):
    first = [part * b.columns + h * b.head for part in range(3)]
    return [slice(at, at + b.head) for at in first]


def interleave(before, middle, after, count, ahead):
    for h in range(min(2, count)):
        before(h)
    for h in range(HEADS):
        if ahead and h + 2 < HEADS:
            before(h + 2)
        middle(h)
        if not ahead and h + 2 < HEADS:
            before(h + 2)
        if not ahead:
            after(h)
        elif h > 0:
            after(h - 1)
    if ahead:
        after(HEADS - 1)


def forward_attention(b, r, wide_work, low_work, between=None):
    columns, width = b.columns, b.width
    factor = float(b.head) ** (-0.5) * LOG2E
    wide, lows = squares(b, wide_work), squares(b, low_work)
    many = min(len(wide), len(lows), HEADS)
    mask_ref = r.mask.at[0:width, 0:width]

    def body(slot):
        cols = slot_columns(b, slot)

        def tokens(rows):
            return r.x[rows, cols].astype(F32)

        def keep(at):
            def put(mean, scale):
                r.stats[at : at + 1, cols] = mean
                r.stats[at + 1 : at + 2, cols] = scale

            return put

        mean, scale = norm_columns(tokens, columns, keep(0))
        for rows in chunks(columns):
            unit = (tokens(rows) - mean) * scale
            r.a[rows, cols] = low(unit * r.tabT[rows, 0:1] + r.tabT[rows, 5:6])
        a = r.a[0:columns, cols]
        for third, bias in ((0, 6), (1, None), (2, 7)):
            rows = slice(third * columns, (third + 1) * columns)
            product = nn(r.w_inT[rows, :], a)
            r.qkv[rows, cols] = low(product if bias is None else product + r.tabT[:, bias : bias + 1])
        mask_ref[...] = slot_mask(b, slot)
        for begin in range(0, HEADS, many):
            heads = range(begin, min(begin + many, HEADS))
            for h in heads:
                q, k, v = parts_of(b, h)
                wide[h - begin][...] = tn(r.qkv[k, cols], r.qkv[q, cols])
            for h in heads:
                scores = wide[h - begin][...] * factor + mask_ref[...]
                highest = jnp.max(scores, 0, keepdims=True)
                powers = jnp.exp2(scores - highest)
                total = jnp.sum(powers, 0, keepdims=True)
                r.logs[h : h + 1, cols] = highest + jnp.log2(total)
                lows[h - begin][...] = low(powers * (1.0 / total))
            for h in heads:
                q, k, v = parts_of(b, h)
                r.o[q, cols] = low(nn(r.qkv[v, cols], lows[h - begin][...]))
        r.y[:, cols] = (
            r.x[:, cols].astype(F32) + tn(r.w_out[...], r.o[0:columns, cols]) + r.tabT[:, 8:9]
        )
        mean, scale = norm_columns(lambda rows: r.y[rows, cols], columns, keep(2))
        for rows in chunks(columns):
            unit = (r.y[rows, cols] - mean) * scale
            r.c[rows, cols] = low(unit * r.tabT[rows, 1:2] + r.tabT[rows, 9:10])

    each_slot(b, body, between)


def forward_mlp(b, r, between=None):
    chunk = LANES // 2
    columns = b.columns
    r.cls[...] = jnp.zeros_like(r.cls)

    def body(slot):
        cols = slot_columns(b, slot)
        c = r.c[0:columns, cols]
        for at in range(0, b.hidden, chunk):
            bias = r.tabT[at % columns : at % columns + chunk, 19 + at // columns : 20 + at // columns]
            active, slope = smooth_parts(nn(r.w_upT[at : at + chunk, :], c) + bias)
            r.u[at : at + chunk, cols] = low(active)
            r.g[at : at + chunk, cols] = low(slope)
        r.z[:, cols] = r.y[:, cols] + nn(r.w_downT[...], r.u[0 : b.hidden, cols]) + r.tabT[:, 10:11]

        def keep(mean, scale):
            r.stats[4:5, cols] = mean
            r.stats[5:6, cols] = scale

        mean, scale = norm_columns(lambda rows: r.z[rows, cols], columns, keep)
        for rows in chunks(columns):
            z = r.z[rows, cols]
            r.out[rows, cols] = low(z)
            r.n[rows, cols] = low((z - mean) * scale * r.tabT[rows, 3:4] + r.tabT[rows, 14:15])
        chosen = low((iota((CLS, b.width), 0) == r.index[2:3, cols]).astype(F32))
        rest = low(r.z[:, cols] - r.out[:, cols].astype(F32))
        r.cls[...] += nt(chosen, r.out[:, cols]) + nt(chosen, rest)

    each_slot(b, body, between)


def backward_cross(b, r, work, between=None):
    columns, width = b.columns, b.width
    r.sums[...] = jnp.zeros_like(r.sums)
    cls_grad = r.cls_grad[...]
    high = low(cls_grad)
    pair = jnp.concatenate([high, low(cls_grad - high.astype(F32))], 0)
    maps, pair = r.maps[...].T, pair.T

    def body(slot):
        cols = slot_columns(b, slot)
        work[0:columns, 0:width] = nn(maps, r.sp[:, cols])
        chosen = low((iota((CLS, width), 0) == r.index[2:3, cols]).astype(F32))
        work[0:columns, width : 2 * width] = nn(pair, jnp.concatenate([chosen, chosen], 0))

        def store(rows, back):
            r.z[rows, cols] = r.cotT[rows, cols].astype(F32) + work[rows, width : 2 * width] + back

        norm_columns_back(
            lambda rows: r.z[rows, cols],
            lambda rows: work[rows, 0:width],
            columns,
            r.stats[4:5, cols],
            r.stats[5:6, cols],
            lambda rows: r.tabT[rows, 3:4],
            r.sums.at[:, 0:columns, :],
            store,
        )

    each_slot(b, body, between)
    r.table[3:4, :] += row_sum(r.sums[1, 0:columns, :])
    r.table[5 + 9 : 5 + 10, :] += row_sum(r.sums[0, 0:columns, :])


def row_sum(values):
    return jnp.sum(values.T, 0, keepdims=True)


def put_out(b, r, between=None):
    def replace(slot):
        cols = slot_columns(b, slot)
        cls = r.index[2:3, cols]
        chosen = low((iota((CLS, b.width), 0) == cls).astype(F32))
        new = tn(r.new_cls[...], chosen)
        r.out[:, cols] = jnp.where(cls >= 0, new, r.out[:, cols].astype(F32)).astype(BF16)

    each_slot(b, replace)
    put_back(b, r, r.out, between)


def put_back(b, r, values, between=None):
    tile = b.rows // 4

    def part(step):
        first = step * tile if isinstance(step, int) else pl.multiple_of(step * tile, tile)
        chosen = low((iota((tile, b.tokens), 0) + first == r.index[0:1, :]).astype(F32))
        if b.index == 0:
            r.staged[:, pl.ds(first, tile)] = low(nt(values[...], chosen))
        else:
            r.staged[pl.ds(first, tile), :] = low(nt(chosen, values[...]))

    if between is None:
        lax.fori_loop(0, 4, lambda step, carry: part(step) or carry, 0)
        return
    for step in range(4):
        part(step)
        between(step)


def backward_mlp(b, r, work, between=None):
    half, columns, width = b.hidden // 2, b.columns, b.width
    r.sums[...] = jnp.zeros_like(r.sums)

    def body(slot):
        cols = slot_columns(b, slot)
        r.zg[:, cols] = low(r.z[:, cols])
        z_low = r.zg[:, cols]
        for part in range(2):
            mine = slice(part * half, (part + 1) * half)
            r.g[mine, cols] = low(r.down_times(part, z_low) * r.g[mine, cols].astype(F32))
        work[0:columns, 0:width] = nn(r.up[0][...], r.g[0:half, cols]) + nn(
            r.up[1][...], r.g[half:, cols]
        )

        def store(rows, back):
            grad = r.z[rows, cols] + back
            r.z[rows, cols] = grad
            r.yg[rows, cols] = low(grad)

        norm_columns_back(
            lambda rows: r.y[rows, cols],
            lambda rows: work[rows, 0:width],
            columns,
            r.stats[2:3, cols],
            r.stats[3:4, cols],
            lambda rows: r.tabT[rows, 1:2],
            r.sums.at[:, 0:columns, :],
            store,
        )
        r.og_rows(slot, slice(0, columns))[...] = low(nn(r.w_out[...], r.yg[:, cols]))

    each_slot(b, body, between)
    r.table[1:2, :] = row_sum(r.sums[1, 0:columns, :])
    r.table[5 + 4 : 5 + 5, :] = row_sum(r.sums[0, 0:columns, :])


def backward_attention(b, r, wide_work, low_work, more_work, between=None):
    columns, width = b.columns, b.width
    factor = float(b.head) ** (-0.5)
    wide, lows, more = squares(b, wide_work), squares(b, low_work), squares(b, more_work)
    many = min(len(wide) // 2, len(lows), len(more), HEADS)
    mask_ref = r.mask.at[0:width, 0:width]

    def body(slot):
        cols = slot_columns(b, slot)
        mask_ref[...] = slot_mask(b, slot)

        def before(h):
            q, k, v = parts_of(b, h)
            wide[h % many][...] = tn(r.qkv[k, cols], r.qkv[q, cols])
            wide[many + h % many][...] = tn(r.qkv[v, cols], r.og_rows(slot, q)[...])

        def middle(h):
            chances = jnp.exp2(
                wide[h % many][...] * (factor * LOG2E) + (mask_ref[...] - r.logs[h : h + 1, cols])
            )
            lows[h % many][...] = low(chances)
            chance_grad = wide[many + h % many][...]
            inner = jnp.sum(chance_grad * chances, 0, keepdims=True)
            more[h % many][...] = low(chances * ((chance_grad - inner) * factor))

        def after(h):
            q, k, v = parts_of(b, h)
            q_low, k_low = r.qkv[q, cols], r.qkv[k, cols]
            score_grad = more[h % many][...]
            r.qkv[q, cols] = low(nn(k_low, score_grad))
            r.qkv[k, cols] = low(nt(q_low, score_grad))
            r.qkv[v, cols] = low(nt(r.og_rows(slot, q)[...], lows[h % many][...]))

        interleave(before, middle, after, many, b.index == 0)

    each_slot(b, body, between)


def backward_first_norm(b, r, work, between=None):
    columns, width = b.columns, b.width
    r.sums[...] = jnp.zeros_like(r.sums)

    def body(slot):
        cols = slot_columns(b, slot)
        work[0:columns, 0:width] = nn(r.w_in[...], r.qkv[:, cols])

        def store(rows, back):
            r.x[rows, cols] = low(r.z[rows, cols] + back)

        norm_columns_back(
            lambda rows: r.x[rows, cols].astype(F32),
            lambda rows: work[rows, 0:width],
            columns,
            r.stats[0:1, cols],
            r.stats[1:2, cols],
            lambda rows: r.tabT[rows, 0:1],
            r.sums.at[:, 0:columns, :],
            store,
        )
    each_slot(b, body, between)
    r.table[0:1, :] = row_sum(r.sums[1, 0:columns, :])
    r.table[5:6, :] = row_sum(r.sums[0, 0:columns, :])
def head_mask(columns):
    head = columns // HEADS
    at = iota((STACK, columns), 1)
    first = iota((STACK, columns), 0) // CLS * head
    return (at >= first) & (at < first + head)


def spread(values, mask):
    return jnp.where(mask, jnp.concatenate([values] * HEADS, 0), 0.0)


def gather_heads(values, mask):
    values = jnp.where(mask, values, 0.0)
    total = values[0:CLS]
    for h in range(1, HEADS):
        total = total + values[h * CLS : (h + 1) * CLS]
    return total


def column_sum(values):
    return jnp.sum(values, 0, keepdims=True)


def cross(b, r, o, ro, g):
    wide = o.columns
    factor = float(o.head) ** (-0.5)
    mask = head_mask(wide)
    og, ob = ro.gains, ro.shifts

    def row(table, at):
        return table[at : at + 1, :].astype(F32)

    enter_on, enter_back, leave_on, leave_back = (nn, nt, nt, nn) if b.index == 0 else (nt, nn, nn, nt)

    xc = r.cls[...]
    yield
    unit2, scale2 = norm(xc, 1)
    lifted, slope2 = smooth_parts(unit2 * row(r.gains, 2) + row(r.shifts, 6))
    lifted = low(lifted)
    yield
    moved = enter_on(lifted, r.enter[...]) + row(ob, 8)
    yield
    unit3, scale3 = norm(moved, 1)
    query_norm = low(unit3 * row(og, 3) + row(ob, 9))
    yield
    q = low(nn(query_norm, ro.cross_in[:, 0:wide]) + row(ob, 10))
    own_k = low(nn(query_norm, ro.cross_in[:, wide : 2 * wide]))
    own_v = low(nn(query_norm, ro.cross_in[:, 2 * wide : 3 * wide]) + row(ob, 11))
    q_all = spread(q.astype(F32), mask)
    k_all = spread(own_k.astype(F32), mask)
    v_all = spread(own_v.astype(F32), mask)
    yield
    key_map = low(nt(low(q_all), ro.cross_in[:, wide : 2 * wide]))
    yield
    own_score = jnp.sum(q_all * k_all, 1, keepdims=True) * factor
    usable = ro.index[1:2, :] == iota((STACK, o.tokens), 0) % CLS
    yield
    scores = jnp.where(usable, nn(key_map, ro.n[...]) * factor, NEGATIVE)
    yield
    highest = jnp.maximum(own_score, jnp.max(scores, 1, keepdims=True))
    powers = jnp.exp(scores - highest)
    own_power = jnp.exp(own_score - highest)
    yield
    inverse = 1.0 / (own_power + jnp.sum(powers, 1, keepdims=True))
    chances = powers * inverse
    own_chance = own_power * inverse
    chances_low = low(chances)
    own_low = low(own_chance).astype(F32)
    ro.sp[STACK : 2 * STACK, :] = chances_low
    total = jnp.sum(chances_low.astype(F32), 1, keepdims=True)
    yield
    mean_row = low(nt(chances_low, ro.n[...]))
    value_bias = row(ob, 11)
    yield
    mixed = own_low * v_all + nn(mean_row, ro.cross_in[:, 2 * wide : 3 * wide]) + total * value_bias
    attended = low(gather_heads(mixed, mask))
    yield
    joined = moved + nn(attended, ro.cross_out[...]) + row(ob, 12)
    yield
    unit4, scale4 = norm(joined, 1)
    spread_out, slope4 = smooth_parts(unit4 * row(og, 4) + row(ob, 13))
    spread_out = low(spread_out)
    r.new_cls[...] = low(leave_on(spread_out, r.leave[...]) + row(r.shifts, 7))

    yield
    new_grad = r.cot_cls[...]
    new_low = low(new_grad)
    r.table[5 + 7 : 5 + 8, :] = column_sum(new_grad)
    yield
    g.leave(tn(new_low, spread_out) if b.index == 0 else tn(spread_out, new_low))
    yield
    back = leave_back(new_low, r.leave[...]) * slope4
    ro.table[4:5, :] = column_sum(back * unit4)
    ro.table[5 + 13 : 5 + 14, :] = column_sum(back)
    yield
    joined_grad = norm_back(back * row(og, 4), unit4, scale4, 1)
    ro.table[5 + 12 : 5 + 13, :] = column_sum(joined_grad)
    joined_low = low(joined_grad)
    yield
    g.cross_out(tn(attended, joined_low))
    yield
    mixed_grad = low(nt(joined_low, ro.cross_out[...])).astype(F32)
    yield
    mixed_all = spread(mixed_grad, mask)
    mixed_all_low = low(mixed_all)
    own_v_grad = gather_heads(own_low * mixed_all, mask)
    own_chance_grad = jnp.sum(mixed_all * v_all, 1, keepdims=True)
    yield
    value_map = low(nt(mixed_all_low, ro.cross_in[:, 2 * wide : 3 * wide]))
    yield
    chance_grad = nn(value_map, ro.n[...]) + jnp.sum(mixed_all * value_bias, 1, keepdims=True)
    yield
    inner = own_chance_grad * own_chance + jnp.sum(chance_grad * chances, 1, keepdims=True)
    score_grad = low(chances * (chance_grad - inner) * factor)
    own_score_grad = low(own_chance * (own_chance_grad - inner) * factor).astype(F32)
    ro.sp[0:STACK, :] = score_grad
    yield
    mean_back = low(nt(score_grad, ro.n[...]))
    yield
    q_grad = gather_heads(
        own_score_grad * k_all + nn(mean_back, ro.cross_in[:, wide : 2 * wide]), mask
    )
    own_k_grad = gather_heads(own_score_grad * q_all, mask)
    ro.table[5 + 10 : 5 + 11, :] = column_sum(q_grad)
    ro.table[5 + 11 : 5 + 12, :] = column_sum(own_v_grad) + column_sum(total * mixed_all)
    q_low, k_low, v_low = low(q_grad), low(own_k_grad), low(own_v_grad)
    yield
    g.cross_in(
        0,
        tn(query_norm, q_low),
    )
    yield
    g.cross_in(
        1,
        tn(
            jnp.concatenate([query_norm, mean_back], 0),
            jnp.concatenate([k_low, low(q_all)], 0),
        ),
    )
    yield
    g.cross_in(
        2,
        tn(
            jnp.concatenate([query_norm, mean_row], 0),
            jnp.concatenate([v_low, mixed_all_low], 0),
        ),
    )
    yield
    back = (
        nt(q_low, ro.cross_in[:, 0:wide])
        + nt(k_low, ro.cross_in[:, wide : 2 * wide])
        + nt(v_low, ro.cross_in[:, 2 * wide : 3 * wide])
    )
    ro.table[3:4, :] = column_sum(back * unit3)
    ro.table[5 + 9 : 5 + 10, :] = column_sum(back)
    yield
    moved_grad = joined_grad + norm_back(back * row(og, 3), unit3, scale3, 1)
    ro.table[5 + 8 : 5 + 9, :] = column_sum(moved_grad)
    moved_low = low(moved_grad)
    yield
    g.enter(tn(lifted, moved_low) if b.index == 0 else tn(moved_low, lifted))
    yield
    back = enter_back(moved_low, r.enter[...]) * slope2
    r.table[2:3, :] = column_sum(back * unit2)
    r.table[5 + 6 : 5 + 7, :] = column_sum(back)
    r.cls_grad[...] = norm_back(back * row(r.gains, 2), unit2, scale2, 1)
    ro.maps[0:STACK, :] = key_map
    ro.maps[STACK : 2 * STACK, :] = value_map


def bit_of(value, place):
    return (value // (1 << place)) % 2


class Links:
    def __init__(self, dp_bits):
        self.bits = ["t"] + list(range(dp_bits))

    def bind(self, solo=None):
        self.dp = self.tensor = 0
        if solo is None:
            self.dp, self.tensor = lax.axis_index("dp"), lax.axis_index("tensor")

    def bit(self, name):
        return self.tensor if name == "t" else bit_of(self.dp, name)

    def partner(self, names):
        dp, tensor = self.dp, self.tensor
        for name in names:
            if name == "t":
                tensor = 1 - self.tensor
            else:
                dp = dp + (1 - 2 * bit_of(self.dp, name)) * (1 << name)
        return (dp, tensor)


def subsets(names):
    for number in range(1, 1 << len(names)):
        yield number, [name for at, name in enumerate(names) if number >> at & 1]


class Pool:
    def __init__(self):
        self.rows, self.copies, self.signals = 0, 0, 0

    def signal(self):
        self.signals += 1
        return self.signals - 1

    def take(self, rows, copies):
        at = (self.rows, self.copies)
        self.rows, self.copies = self.rows + rows, self.copies + copies
        return at


class Group:
    def __init__(self, pool, first, rows, phases, apart=None):
        self.first, self.rows, self.apart = first, rows, apart
        self.steps, size, bases = [], rows, 1 if apart is None else 2
        self.frees = {}
        phases = list(phases)
        while phases:
            names, kind = phases.pop(0)
            count = 1 << len(names)
            if kind == "halve" and size % (16 * count):
                kind = "full"
                if len(names) > 1:
                    phases = [((name,), "halve") for name in names] + phases
                    continue
            if kind == "merge":
                bases = 1
                self.steps.append((kind, names, size, pool.take(size, 1), 1))
            elif kind == "halve":
                at = pool.take(bases * (count - 1) * (size // count), 2 * bases * (count - 1))
                self.steps.append((kind, names, size, at, bases))
                self.frees[len(self.steps) - 1] = pool.signal()
                size //= count
            else:
                at = pool.take(bases * (count - 1) * size, bases * (count - 1))
                self.steps.append((kind, names, size, at, bases))
        self.plan = [("reduce", step, self.frees.get(at)) for at, step in enumerate(self.steps)]
        self.plan += [("gather",) + step[1:] for step in reversed(self.plan) if step[2] is not None]

    def bind(self, links, buffer, received, send, recv, free):
        self.links, self.buffer, self.received = links, buffer, received
        self.send, self.recv, self.free = send, recv, free
        self.lo, self.at, self.flight, self.offsets = 0, 0, [], {}
        return self

    def chunk(self, names, flipped):
        index = 0
        for place, name in enumerate(names):
            bit = self.links.bit(name)
            index = index + (1 - bit if name in flipped else bit) * (1 << place)
        return index

    def rows_at(self, base, first, size):
        return pl.ds(pl.multiple_of(base + first, 16), size)

    def copy(self, source, target, sem, partner):
        return pltpu.make_async_remote_copy(
            src_ref=source,
            dst_ref=target,
            send_sem=self.send.at[sem],
            recv_sem=self.recv.at[sem],
            device_id=partner,
            device_id_type=pl.DeviceIdType.MESH,
        )

    def bases(self, count):
        return (self.first, self.apart)[:count]

    def begin(self):
        if self.at == len(self.plan):
            return
        way, (kind, names, size, (row, sem), count), free = self.plan[self.at]
        flight = []
        if kind == "merge":
            source = self.buffer.at[self.rows_at(self.apart, self.lo, size), :]
            target = self.received.at[pl.ds(row, size), :]
            flight.append(self.copy(source, target, sem, self.links.partner(names)))
        elif way == "reduce":
            part = size // (1 << len(names)) if kind == "halve" else size
            for base in self.bases(count):
                for number, flipped in subsets(names):
                    first = self.lo
                    if kind == "halve":
                        first = first + self.chunk(names, flipped) * part
                    source = self.buffer.at[self.rows_at(base, first, part), :]
                    target = self.received.at[pl.ds(row, part), :]
                    flight.append(self.copy(source, target, sem, self.links.partner(flipped)))
                    row, sem = row + part, sem + 1
        else:
            part = size // (1 << len(names))
            before = self.offsets[(kind, tuple(names), size)]
            pl.semaphore_wait(self.free.at[free], (1 << len(names)) - 1)
            sem = sem + count * ((1 << len(names)) - 1)
            first = before + self.chunk(names, []) * part
            for number, flipped in subsets(names):
                mine = self.buffer.at[self.rows_at(self.first, first, part), :]
                flight.append(self.copy(mine, mine, sem, self.links.partner(flipped)))
                sem += 1
        for copy in flight:
            copy.start()
        self.flight = flight

    def end(self):
        if not self.flight:
            return
        way, (kind, names, size, (row, sem), count), free = self.plan[self.at]
        for copy in self.flight:
            copy.wait()
        self.flight = []
        self.at += 1
        if way == "gather":
            return
        if kind == "merge":
            self.add(self.first, self.lo, size, [row])
            return
        part = size
        parts = (1 << len(names)) - 1
        if kind == "halve":
            part = size // (parts + 1)
            self.offsets[(kind, tuple(names), size)] = self.lo
            self.lo = self.lo + self.chunk(names, []) * part
            for number, flipped in subsets(names):
                pl.semaphore_signal(
                    self.free.at[free],
                    inc=1,
                    device_id=self.links.partner(flipped),
                    device_id_type=pl.DeviceIdType.MESH,
                )
        for base in self.bases(count):
            self.add(base, self.lo, part, [row + i * part for i in range(parts)])
            row += parts * part

    def add(self, base, first, size, rows):
        block = max(block for block in range(16, 257, 16) if size % block == 0)

        def body(step, carry):
            here = self.rows_at(base, first + step * block, block)
            terms = [self.buffer[here, :]]
            for row in rows:
                at = pl.ds(pl.multiple_of(row + step * block, 16), block)
                terms.append(self.received[at, :])
            if len(rows) > 1:
                terms = [term.astype(F32) for term in terms]
            while len(terms) > 1:
                terms = [a + b for a, b in zip(terms[0::2], terms[1::2])]
            self.buffer[here, :] = low(terms[0])
            return carry

        if size == block:
            body(0, 0)
        else:
            lax.fori_loop(0, size // block, body, 0)

    def advance(self):
        self.end()
        self.begin()

    @property
    def done(self):
        return self.at == len(self.plan)


def greet(links, partners):
    barrier = pltpu.get_barrier_semaphore()
    for names in partners:
        pl.semaphore_signal(
            barrier, inc=1, device_id=links.partner(names), device_id_type=pl.DeviceIdType.MESH
        )


def all_here(partners):
    pl.semaphore_wait(pltpu.get_barrier_semaphore(), len(partners))


class Swap:
    def __init__(self, links, pairs, sends, receives):
        self.links, self.pairs, self.sends, self.receives = links, pairs, sends, receives

    def copies(self, step):
        result = []
        for at, (mine, theirs) in enumerate(self.pairs):
            half = mine.shape[0] // 2
            rows = pl.ds(pl.multiple_of(self.links.bit(0) * half, 16), half)
            result.append(
                pltpu.make_async_remote_copy(
                    src_ref=(mine if step == 0 else theirs).at[rows, :],
                    dst_ref=theirs.at[rows, :],
                    send_sem=self.sends.at[step, at],
                    recv_sem=self.receives.at[step, at],
                    device_id=self.links.partner(["t"] if step == 0 else [0]),
                    device_id_type=pl.DeviceIdType.MESH,
                )
            )
        return result

    def start(self, step):
        for copy in self.copies(step):
            copy.start()

    def wait(self, step):
        for copy in self.copies(step):
            copy.wait()


class Place:
    def __init__(self, small, large):
        ds, dl = small.columns, large.columns
        self.first, self.size, at = {}, {}, 0
        for name, rows in (
            ("small_up", ds), ("small_down", ds), ("large_up", 2 * dl), ("large_down", 2 * dl),
            ("other", 2 * ds + 4 * dl),
            ("large_cross", 4 * dl), ("small_enter", ds), ("small_leave", ds),
            ("large_enter", ds), ("large_leave", ds), ("small_cross", 2 * ds),
            ("large_out", dl), ("large_in", 3 * dl), ("small_heads", 2 * ds), ("tables", 64),
        ):
            self.first[name], self.size[name] = at, rows
            at += rows
        self.total = at

    def rows(self, name, part=0, size=None):
        first = self.first[name] + part
        return slice(first, first + (self.size[name] if size is None else size))


class CrossGrads:
    def __init__(self, own, other, place, buffer):
        self.own, self.other, self.place, self.buffer = own, other, place, buffer
        self.kept = {}

    def put(self, name, part, values):
        first = self.place.first[name] + part
        self.buffer[first : first + values.shape[0], :] = low(values)

    def cross_in(self, third, values):
        if self.other.index == 1:
            self.put("large_cross", third * self.other.columns, values)
            return
        self.kept[third] = values
        if third == 1:
            self.put("small_cross", 0, jnp.concatenate([self.kept[0], values], 1))
        if third == 2:
            self.put(
                "small_cross", self.other.columns, jnp.concatenate([values, self.kept["out"]], 1)
            )

    def cross_out(self, values):
        if self.other.index == 1:
            self.put("large_cross", 3 * self.other.columns, values)
        else:
            self.kept["out"] = values

    def enter(self, values):
        if self.own.index == 0:
            self.put("small_enter", 0, values)
        else:
            self.put("large_enter", 0, values)

    def leave(self, values):
        if self.own.index == 1:
            self.put("large_leave", 0, values)
        else:
            self.put("small_leave", 0, values)


def mlp_grads(b, r, place, buffer, tick):
    half, columns = b.hidden // 2, b.columns
    name = ("small", "large")[b.index]
    for part in range(2):
        first = place.first["other"] * part + place.first[name + "_up"]
        for at in range(0, half, LANES):
            up = nt(r.c[...], r.g[part * half + at : part * half + at + LANES, :])
            buffer[first : first + columns, :] = low(up[0:columns])
            first += columns
            row = b.index + at // LANES
            r.bias_rows[part, row : row + 1, :] = up[columns : columns + 1]
        tick(part)
    r.table[5 + 5 : 5 + 6, :] = nt(r.u[b.hidden : b.hidden + 16, :], r.zg[...])[0:1]
    for part in range(2):
        mine = slice(part * half, (part + 1) * half)
        first = place.first["other"] * part + place.first[name + "_down"]
        if b.index == 0:
            buffer[first : first + columns, :] = low(nt(r.zg[...], r.u[mine, :]))
        else:
            buffer[first : first + half, :] = low(nt(r.u[mine, :], r.zg[...]))
        tick(2 + part)


def out_grads(b, r):
    w_out = nt(r.o[...], r.yg[...])
    r.table[5 + 3 : 5 + 4, :] = w_out[b.columns : b.columns + 1, :]
    return w_out[0 : b.columns]


def in_grads(b, r, third):
    columns = b.columns
    w_in = nt(r.a[...], r.qkv[third * columns : (third + 1) * columns, :])
    if third != 1:
        row = 5 + 1 + third // 2
        r.table[row : row + 1, :] = w_in[columns : columns + 1, :]
    return w_in[0:columns]


def large_in_grads(b, r, place, buffer):
    for third in range(3):
        first = place.first["large_in"] + third * b.columns
        buffer[first : first + b.columns, :] = low(in_grads(b, r, third))


def small_head_grads(b, r, place, buffer):
    columns, first = b.columns, place.first["small_heads"]
    thirds = [in_grads(b, r, third) for third in range(3)] + [out_grads(b, r)]
    for half in range(2):
        at = first + half * columns
        buffer[at : at + columns, :] = low(jnp.concatenate(thirds[2 * half : 2 * half + 2], 1))


NAMES = (
    "counts", "small_rows", "large_rows", "small_cot", "large_cot",
    "small_in", "small_out", "small_up", "small_down",
    "large_in", "large_out", "large_up", "large_down",
    "small_enter", "large_cross_in", "large_cross_out", "small_leave",
    "large_enter", "small_cross_in", "small_cross_out", "large_leave",
    "small_gains", "small_shifts", "large_gains", "large_shifts", "small_up_bias", "large_up_bias",
)
OUTS = (
    "small_out", "large_out", "small_rows", "large_rows",
    "small_heads_in", "small_heads_out", "small_up", "small_up_bias", "small_down",
    "large_heads_in", "large_heads_out", "large_up", "large_up_bias", "large_down",
    "small_enter", "large_cross_in", "large_cross_out", "small_leave",
    "large_enter", "small_cross_in", "small_cross_out", "large_leave",
    "small_gains", "small_shifts", "large_gains", "large_shifts",
)
def scratch_of(b):
    d, t, h = b.columns, b.tokens, b.hidden
    scratch = dict(
        logs=pltpu.VMEM((8, t), F32),
        stats=pltpu.VMEM((8, t), F32),
        index=pltpu.VMEM((8, t), jnp.int32),
        x=pltpu.VMEM((d, t), BF16),
        cotT=pltpu.VMEM((d, t), BF16),
        a=pltpu.VMEM((d + 16, t), BF16),
        qkv=pltpu.VMEM((3 * d, t), BF16),
        o=pltpu.VMEM((d + 16, t), BF16),
        y=pltpu.VMEM((d, t), F32),
        c=pltpu.VMEM((d + 16, t), BF16),
        u=pltpu.VMEM((h + 16, t), BF16),
        g=pltpu.VMEM((h, t), BF16),
        z=pltpu.VMEM((d, t), F32),
        n=pltpu.VMEM((d, t), BF16),
        out=pltpu.VMEM((d, t), BF16),
        sp=pltpu.VMEM((2 * STACK, t), BF16),
        maps=pltpu.VMEM((2 * STACK, d), BF16),
        cls=pltpu.VMEM((CLS, d), F32),
        cot_cls=pltpu.VMEM((CLS, d), F32),
        new_cls=pltpu.VMEM((CLS, d), BF16),
        cls_grad=pltpu.VMEM((CLS, d), F32),
        table=pltpu.VMEM((24, d), F32),
        tabT=pltpu.VMEM((d, 128), F32),
        w_inT=pltpu.VMEM((3 * d, d), BF16),
        w_upT=pltpu.VMEM((h, d), BF16),
        w_downT=pltpu.VMEM((d, h), BF16),
        other_up=pltpu.VMEM((d, h // 2), BF16),
    )
    if b.index == 0:
        scratch.update(og=pltpu.VMEM((d, t), BF16), other_down=pltpu.VMEM((d, h // 2), BF16))
    else:
        scratch.update(other_down=pltpu.VMEM((h // 2, d), BF16))
    return scratch


def columns_of(rows):
    rows = rows.astype(F32)
    return jnp.concatenate([rows, jnp.zeros((128 - rows.shape[0], rows.shape[1]), F32)], 0).T


def prepare(b, r):
    r.tabT[...] = columns_of(jnp.concatenate([r.gains[...].astype(F32), r.shifts[...].astype(F32)], 0))
    r.w_inT[...] = r.w_in[...].T
    r.a[b.columns : b.columns + 16, :] = jnp.ones((16, b.tokens), BF16)
    r.o[b.columns : b.columns + 16, :] = jnp.ones((16, b.tokens), BF16)
    r.c[b.columns : b.columns + 16, :] = jnp.ones((16, b.tokens), BF16)
    r.u[b.hidden : b.hidden + 16, :] = jnp.ones((16, b.tokens), BF16)
    r.table[...] = jnp.zeros_like(r.table)


def prepare_mlp(b, r, part):
    half, columns = b.hidden // 2, b.columns
    mine = slice(part * half, (part + 1) * half)
    biases = columns_of(r.up_bias[part][0:16, :])
    for at in range(0, half, columns):
        place = b.index + at // LANES
        column = 19 + (part * half + at) // columns
        r.tabT[:, column : column + 1] = biases[at % LANES : at % LANES + columns, place : place + 1]
    r.w_upT[mine, :] = r.up[part][...].T
    r.w_downT[:, mine] = r.down[part][...].T if b.index else r.down[part][...]


class Refs:
    pass


PHASES = {
    "tables": (((0,), "full"), (("t", 1,), "full"), ((2, 3,), "full")),
    "tail": (((0,), "halve"), (("t", 1,), "halve"), ((2,), "full"), ((3,), "full")),
    "large_up": (((0,), "halve"), ((1,), "halve"), (("t",), "merge"), ((2, 3,), "halve")),
    "large_in": (((0,), "halve"), (("t", 1,), "halve"), ((2,), "halve"), ((3,), "full")),
    "cross_b": (((0,), "halve"), ((1,), "halve"), ((2, 3,), "halve"), (("t",), "full")),
    "cross_c": (((0,), "halve"), ((1,), "halve"), ((2,), "full"), ((3,), "full"), (("t",), "halve")),
    "large_down": (((0,), "halve"), ((1,), "halve"), ((2,), "halve"), (("t",), "merge"), ((3,), "full")),
    "small_mlp": (((0,), "halve"), ((1,), "halve"), (("t",), "merge"), ((2,), "full"), ((3,), "full")),
    "mixed": (((0,), "halve"), (("t",), "halve"), ((2, 3,), "halve"), ((1,), "halve")),
    "cross_a": (((0,), "halve"), (("t",), "halve"), ((1,), "full"), ((2,), "halve"), ((3,), "halve")),
}
TICKS = {
    "crossend": ("cross_b",),
    "bcross_l2": ("cross_b", "cross_c", "cross_a",),
    "bmlp_l0": ("cross_c", "cross_a",),
    "bmlp_l2": ("cross_b",),
    "gmlp_l1": ("cross_c", "cross_a", "large_up",),
    "gmlp_l3": ("large_up", "large_down",),
    "gol": ("mixed",),
    "batt_l0": ("cross_b", "cross_c", "large_down", "mixed", "cross_a",),
    "batt_l1": ("cross_b",),
    "batt_l2": ("large_up", "cross_c", "mixed", "cross_a",),
    "ghead_l": ("large_in",),
    "bmlp_s0": ("large_in",),
    "bmlp_s2": ("large_up", "cross_b", "large_down",),
    "bmlp_s3": ("cross_c",),
    "bmlp_s4": ("mixed",),
    "gmlp_s1": ("cross_a",),
    "gmlp_s3": ("small_mlp",),
    "batt_s1": ("large_in", "cross_c", "small_mlp",),
    "batt_s2": ("large_up",),
    "batt_s3": ("large_down",),
    "batt_s4": ("cross_b", "mixed", "cross_a",),
    "ghead_s": ("large_in", "cross_c", "tail",),
    "bnorm_l0": ("cross_b",),
    "bnorm_l1": ("tail", "cross_c", "large_down",),
    "bnorm_s2": ("large_up", "small_mlp",),
    "bnorm_s3": ("mixed", "cross_a",),
    "tables": ("tables",),
    "out_l0": ("large_in",),
    "out_l1": ("tables", "tail",),
    "out_l3": ("small_mlp",),
    "out_s0": ("large_down",),
    "out_s1": ("large_up", "large_in",),
    "out_s3": ("tail", "large_up",),
    "back_l0": ("mixed",),
    "back_l1": ("small_mlp", "cross_a",),
    "back_l3": ("large_down",),
    "back_s0": ("tables", "cross_a",),
    "back_s1": ("tail",),
}
REST = (
    "large_in", "small_mlp", "large_down", "large_in", "mixed", "large_down", "mixed", "small_mlp", "tail", "tables", "small_mlp", "tail",
)


class Plan:
    def __init__(self, place, small, large, dp):
        ds, dl, first = small.columns, large.columns, place.first
        self.dp_bits = dp.bit_length() - 1
        assert dp == 1 << self.dp_bits
        more = [(tuple(range(at, min(at + 2, self.dp_bits))), "halve") for at in range(4, self.dp_bits, 2)]
        self.pool = Pool()
        other, cross, heads = first["other"], first["large_cross"], first["large_in"]
        tail = heads + 1024
        places = {
            "large_up": (first["large_up"], 2 * dl, other + first["large_up"]),
            "large_down": (first["large_down"], 2 * dl, other + first["large_down"]),
            "small_mlp": (first["small_up"], 2 * ds, other + first["small_up"]),
            "cross_a": (cross + 0, 1024, None),
            "cross_b": (cross + 1024, 1024, None),
            "cross_c": (cross + 2048, 512, None),
            "mixed": (cross + 2560, first["large_in"] - cross - 2560, None),
            "large_in": (heads, 1024, None),
            "tail": (tail, first["tables"] - tail, None),
            "tables": (first["tables"], 64, None),
        }
        self.groups, self.met = {}, []
        for name, (begin, rows, apart) in places.items():
            group = Group(self.pool, begin, rows, list(PHASES[name]) + more, apart)
            self.groups[name] = group
            for step in group.steps:
                for number, flipped in subsets(step[1]):
                    if flipped not in self.met:
                        self.met.append(flipped)


def layer_kernel(small, large, place, plan, keys, solo, *refs):
    ins = dict(zip(NAMES, refs))
    refs = refs[len(NAMES) :]
    sources = {name: ins[name] for name in FETCH}
    packed, small_out, large_out, small_grad, large_grad = refs[:5]
    refs = refs[5:]
    groups = []
    links = Links(plan.dp_bits)
    links.bind(solo)
    for b in (small, large):
        r = Refs()
        for key in keys[b.index]:
            setattr(r, key, refs[0])
            refs = refs[1:]
        groups.append((b, r))
    (bs, rs), (bl, rl) = groups
    for name in FETCH:
        if name not in ("large_rows", "large_cot"):
            ins[name], refs = refs[0], refs[1:]
    work, mask, sums, own_biases = refs[:4]
    biases, other_biases, buffer, received, send, recv, free, swap_send, swap_recv, out_sem, in_sem = refs[4:]
    for b, r in groups:
        name = ("small", "large")[b.index]
        r.w_in, r.w_out = ins[name + "_in"], ins[name + "_out"]
        r.up = (ins[name + "_up"], r.other_up)
        r.down = (ins[name + "_down"], r.other_down)
        r.gains, r.shifts = ins[name + "_gains"], ins[name + "_shifts"]
        r.enter, r.leave = ins[name + "_enter"], ins[name + "_leave"]
        r.cross_in, r.cross_out = ins[name + "_cross_in"], ins[name + "_cross_out"]
        r.zg, r.yg = r.n, r.cotT
        r.bias_rows, r.mask, r.sums = biases, mask, sums
        r.up_bias = (own_biases, other_biases)
    half_s = bs.hidden // 2
    rs.down_times = lambda part, z: tn(rs.w_downT[:, part * half_s : (part + 1) * half_s], z)
    rl.down_times = lambda part, z: nn(rl.down[part][...], z)
    rs.og_rows = lambda slot, rows: rs.og.at[rows, slot_columns(bs, slot)]

    def large_og(slot, rows):
        size = rows.stop - rows.start
        if isinstance(slot, int):
            return rl.w_upT.at[slot * bl.columns + rows.start : slot * bl.columns + rows.stop, :]
        return rl.w_upT.at[pl.ds(pl.multiple_of(slot * bl.columns + rows.start, 64), size), :]

    rl.og_rows = large_og
    rs.staged = rs.sp.at[:, 0 : bs.rows]
    rl.staged = rl.w_inT.at[0 : bl.rows, :]
    biases[...] = jnp.zeros_like(biases)
    bias = [ins["small_up_bias"][...]]
    bias += [ins["large_up_bias"][at : at + LANES] for at in range(0, bl.hidden // 2, LANES)]
    bias = [value.astype(F32).reshape(1, LANES) for value in bias]
    own_biases[...] = low(jnp.concatenate(bias + [jnp.zeros((32 - len(bias), LANES), F32)], 0))
    for group in plan.groups.values():
        group.bind(links, buffer, received, send, recv, free)
    swap = Swap(
        links,
        (
            (ins["large_up"], rl.other_up),
            (ins["large_down"], rl.other_down),
            (ins["small_up"], rs.other_up),
            (ins["small_down"], rs.other_down),
            (own_biases, other_biases),
        ),
        swap_send,
        swap_recv,
    )
    fetched = {}

    def fetch(names):
        for name in names:
            if name in ("large_rows", "large_cot"):
                at = ("large_rows", "large_cot").index(name)
                target = rl.u.at[0 : bl.rows, at * bl.columns : (at + 1) * bl.columns]
            else:
                target = ins[name]
            fetched[name] = pltpu.make_async_copy(
                sources[name], target, in_sem.at[FETCH.index(name)]
            )
            fetched[name].start()

    fetch(FETCH[:8])

    def need(*names):
        for name in names:
            fetched.pop(name).wait()

    rs.rows, rs.cot = ins["small_rows"], ins["small_cot"]
    rl.rows = rl.g.at[0 : bl.columns, 0 : bl.rows]
    rl.cot = rl.g.at[bl.columns : 2 * bl.columns, 0 : bl.rows]

    out_copies = {}

    def write_out(name, source, target):
        copy = pltpu.make_async_copy(source, target, out_sem.at[len(out_copies)])
        copy.start()
        out_copies[name] = copy

    def step(name):
        group = plan.groups[name]
        if solo is None and not group.done:
            group.advance()
            if group.done:
                rows = slice(group.first, group.first + group.rows)
                write_out(name, buffer.at[rows, :], packed.at[rows, :])

    def tick(label):
        for name in TICKS.get(label, ()):
            step(name)

    def ticks(stage, count):
        if any(stage + str(part) in TICKS for part in range(count)):
            return lambda part: tick(stage + str(part))
        return None

    def always(stage):
        return lambda part: tick(stage + str(part))

    if solo is None:
        greet(links, plan.met)
    need("small_rows", "small_cot")
    lay_out(bs, rs, ins["counts"])
    fetch(FETCH[8:])
    bring_in(bs, rs)
    need("large_up", "large_down", "small_up", "small_down")
    if solo is None:
        all_here(plan.met)
        swap.start(0)
    else:
        for mine, theirs in swap.pairs:
            theirs[...] = mine[...]
    need("large_rows", "large_cot")
    for at, target in enumerate((rl.rows, rl.cot)):
        target[...] = rl.u[0 : bl.rows, at * bl.columns : (at + 1) * bl.columns].T
    lay_out(bl, rl, ins["counts"])
    bring_in(bl, rl)
    need("small_in", "large_in")
    prepare(bs, rs)
    prepare(bl, rl)
    need("small_out", "large_out")
    forward_attention(bl, rl, [rl.z], [rl.w_downT])
    forward_attention(bs, rs, [rl.z, work], [rl.w_downT])
    if solo is None:
        swap.wait(0)
        swap.start(1)
    for b, r in groups:
        prepare_mlp(b, r, 0)
    if solo is None:
        swap.wait(1)
    for b, r in groups:
        prepare_mlp(b, r, 1)
    forward_mlp(bl, rl)
    forward_mlp(bs, rs)
    need(*tuple(fetched))
    both = [
        cross(bs, rs, bl, rl, CrossGrads(bs, bl, place, buffer)),
        cross(bl, rl, bs, rs, CrossGrads(bl, bs, place, buffer)),
    ]
    while both:
        both = [one for one in both if next(one, both) is None]
    def large_block():
        backward_cross(bl, rl, work, ticks("bcross_l", bl.slots))
        backward_mlp(bl, rl, work, ticks("bmlp_l", bl.slots))
        mlp_grads(bl, rl, place, buffer, always("gmlp_l"))
        first = place.first["large_out"]
        buffer[first : first + bl.columns, :] = low(out_grads(bl, rl))
        tick("gol")

    def large_attention():
        wide = [rl.y, work]
        backward_attention(bl, rl, wide, [rl.w_downT], [rl.w_inT], ticks("batt_l", bl.slots))
        large_in_grads(bl, rl, place, buffer)
        tick("ghead_l")

    def small_block():
        backward_cross(bs, rs, work, ticks("bcross_s", bs.slots))
        backward_mlp(bs, rs, work, ticks("bmlp_s", bs.slots))
        mlp_grads(bs, rs, place, buffer, always("gmlp_s"))

    def small_attention():
        wide = [rl.y, work]
        backward_attention(bs, rs, wide, [rl.w_downT], [rl.g], ticks("batt_s", bs.slots))
        small_head_grads(bs, rs, place, buffer)
        tick("ghead_s")

    def norms():
        backward_first_norm(bl, rl, work, ticks("bnorm_l", bl.slots))
        backward_first_norm(bs, rs, work, ticks("bnorm_s", bs.slots))
        put_tables(links, place, buffer, rs, rl, biases)
        tick("tables")

    def outputs():
        put_out(bl, rl, ticks("out_l", 4))
        write_out("large_out", rl.staged, large_out)
        put_out(bs, rs, ticks("out_s", 4))
        write_out("small_out", rs.staged, small_out)
        out_copies["large_out"].wait()
        put_back(bl, rl, rl.x, ticks("back_l", 4))
        write_out("large_grad", rl.staged, large_grad)
        out_copies["small_out"].wait()
        put_back(bs, rs, rs.x, ticks("back_s", 4))
        write_out("small_grad", rs.staged, small_grad)

    tick("crossend")
    large_block()
    large_attention()
    small_block()
    small_attention()
    norms()
    outputs()
    for name in REST:
        step(name)
    while any(not group.done for group in plan.groups.values()) and solo is None:
        for name in plan.groups:
            step(name)
    for name, copy in out_copies.items():
        if name not in ("large_out", "small_out"):
            copy.wait()


def put_tables(links, place, buffer, rs, rl, biases):
    ds = rs.table.shape[1]
    own, other = biases[0, 0:8, :], biases[1, 0:8, :]
    first = links.tensor == 0
    rows = [
        rl.table[...],
        jnp.concatenate([rs.table[...], jnp.zeros((24, LANES - ds), F32)], 1),
        jnp.where(first, own, other),
        jnp.where(first, other, own),
    ]
    buffer[place.rows("tables"), :] = low(jnp.concatenate(rows, 0))


def unpack_kernel(place, ds, dl, parts, *refs):
    (packed, small_out, large_out, small_grad, large_grad), refs = refs[:5], refs[5:]
    outs, refs = dict(zip(OUTS, refs)), refs[len(OUTS) :]
    got, got_small, got_large, out_small, out_large = refs[:5]
    refs = refs[5:]
    stages, refs = dict(zip(OUTS[2:], refs)), refs[len(OUTS) - 2 :]
    in_sem, out_sem = refs
    copies, arriving = [], {}

    def bring(name, source, target):
        arriving[name] = pltpu.make_async_copy(source, target, in_sem.at[len(arriving)])
        arriving[name].start()

    def leave(source, target):
        copies.append(pltpu.make_async_copy(source, target, out_sem.at[len(copies)]))
        copies[-1].start()

    for name, first, rows in parts:
        bring(name, packed.at[first : first + rows, :], got.at[first : first + rows, :])
    bring("small_rows", small_grad, got_small)
    bring("large_rows", large_grad, got_large)
    bring("small_out", small_out, out_small)
    bring("large_out", large_out, out_large)

    def read(name, part, rows):
        first = place.first[name] + part
        return got[first : first + rows, :].astype(F32)

    def done(*names):
        for name in names:
            leave(stages[name], outs[name])

    arriving["mlp"].wait()
    for part in range(2):
        stages["large_up"][:, part * dl : (part + 1) * dl] = read("large_up", part * dl, dl)
    done("large_up")
    stages["large_down"][...] = read("large_down", 0, 2 * dl)
    stages["small_up"][...] = read("small_up", 0, ds)
    stages["small_down"][...] = read("small_down", 0, ds)
    done("large_down", "small_up", "small_down")
    for name, into, out, at in (("cross", "large_cross", "large_cross", 3), ("heads", "large_in", "large_out", 0)):
        arriving[name].wait()
        for third in range(3):
            stages["large_" + name + "_in"][:, third * dl : (third + 1) * dl] = read(
                into, third * dl, dl
            )
        stages["large_" + name + "_out"][...] = read(out, at * dl, dl)
        second = read("small_" + name, ds, ds)
        stages["small_" + name + "_in"][:, 0:LANES] = read("small_" + name, 0, ds)
        stages["small_" + name + "_in"][:, LANES:] = second[:, 0:ds]
        stages["small_" + name + "_out"][...] = second[:, ds:]
        done("large_" + name + "_in", "large_" + name + "_out", "small_" + name + "_in", "small_" + name + "_out")
        if name == "cross":
            for key in ("small_enter", "small_leave", "large_enter", "large_leave"):
                stages[key][...] = read(key, 0, ds)
                done(key)
    for name, ref in (("small_rows", got_small), ("large_rows", got_large)):
        arriving[name].wait()
        stages[name][...] = ref[...].astype(F32)
        done(name)
    for name, ref in (("small_out", out_small), ("large_out", out_large)):
        arriving[name].wait()
        leave(ref, outs[name])
    arriving["tables"].wait()
    first = place.first["tables"]
    tables = got[first : first + 64, :].astype(F32)
    stages["large_gains"][...] = tables[0:5]
    stages["large_shifts"][...] = tables[5:19]
    stages["small_gains"][...] = tables[24:29, 0:ds]
    stages["small_shifts"][...] = tables[29:43, 0:ds]
    mine = jnp.where(lax.axis_index("tensor") == 0, tables[48:56], tables[56:64])
    stages["small_up_bias"][...] = mine[0]
    stages["large_up_bias"][0:LANES] = mine[1]
    stages["large_up_bias"][LANES:] = mine[2]
    done("large_gains", "large_shifts", "small_gains", "small_shifts", "small_up_bias", "large_up_bias")
    for copy in copies:
        copy.wait()


FETCH = (
    "small_rows", "small_cot", "large_up", "large_down", "small_up", "small_down", "large_rows", "large_cot",
    "small_in", "large_in", "small_out", "large_out",
    "large_cross_in", "large_cross_out", "small_cross_in", "small_cross_out",
    "small_enter", "small_leave", "large_enter", "large_leave",
)
TURNED = ("small_out", "small_rows", "small_down", "small_leave", "large_enter")


def run_layer(args, dp, solo=None):
    (
        small_rows, large_rows, counts, small_cot, large_cot,
        small_in, small_out, small_up, small_up_bias, small_down,
        large_in, large_out, large_up, large_up_bias, large_down,
        small_enter, large_cross_in, large_cross_out, small_leave, large_enter,
    ) = args[:20]
    ds, dl = small_rows.shape[1], large_rows.shape[1]
    small = Branch(0, small_rows.shape[0], ds, 2 * small_up.shape[1], 256, ((0, 4), (1, 5), (2,), (3,), (6,)))
    large = Branch(1, large_rows.shape[0], dl, 2 * large_up.shape[1], 384, ((0, 1, 4), (2, 3, 5), (6,)))
    place = Place(small, large)
    plan = Plan(place, small, large, dp)
    inputs = (
        counts, small_rows.T, large_rows, small_cot.T, large_cot,
        small_in, small_out, small_up, small_down.T,
        large_in, large_out, large_up, large_down,
        small_enter, large_cross_in, large_cross_out, small_leave.T, large_enter.T,
    ) + args[20:] + (small_up_bias, large_up_bias)
    keys = tuple(tuple(scratch_of(b)) for b in (small, large))
    scratch = [s for b in (small, large) for s in scratch_of(b).values()]
    copies = pltpu.SemaphoreType.DMA
    for name in FETCH:
        if name not in ("large_rows", "large_cot"):
            scratch.append(pltpu.VMEM(inputs[NAMES.index(name)].shape, BF16))
    scratch += [
        pltpu.VMEM((dl, large.tokens), F32),
        pltpu.VMEM((large.width, large.width), F32),
        pltpu.VMEM((2, dl, 128), F32),
        pltpu.VMEM((32, LANES), BF16),
        pltpu.VMEM((2, 16, LANES), F32),
        pltpu.VMEM((32, LANES), BF16),
        pltpu.VMEM((place.total, LANES), BF16),
        pltpu.VMEM((plan.pool.rows, LANES), BF16),
        copies((plan.pool.copies,)),
        copies((plan.pool.copies,)),
        pltpu.SemaphoreType.REGULAR((plan.pool.signals,)),
        copies((2, 5)),
        copies((2, 5)),
        copies((20,)),
        copies((len(FETCH),)),
    ]
    shape = jax.ShapeDtypeStruct
    vmem, hbm = pl.BlockSpec(memory_space=pltpu.VMEM), pl.BlockSpec(memory_space=pl.ANY)
    middle = (
        shape((place.total, LANES), BF16),
        shape((ds, small.rows), BF16),
        shape((large.rows, dl), BF16),
        shape((ds, small.rows), BF16),
        shape((large.rows, dl), BF16),
    )
    values = pl.pallas_call(
        functools.partial(layer_kernel, small, large, place, plan, keys, solo),
        out_shape=middle,
        in_specs=[pl.BlockSpec(memory_space=pltpu.SMEM)]
        + [hbm if name in FETCH else vmem for name in NAMES[1:]],
        out_specs=(hbm,) * 5,
        scratch_shapes=scratch,
        compiler_params=pltpu.CompilerParams(
            vmem_limit_bytes=VMEM_LIMIT,
            collective_id=0 if solo is None else None,
            has_side_effects=True,
        ),
        name="layer",
    )(*inputs)
    shapes = dict(
        small_out=shape((ds, small.rows), BF16),
        large_out=shape(large_rows.shape, BF16),
        small_rows=shape((ds, small.rows), F32),
        large_rows=shape(large_rows.shape, F32),
        small_up_bias=shape(small_up_bias.shape, F32),
        large_up_bias=shape(large_up_bias.shape, F32),
    )
    for name, value in zip(OUTS[4:], args[5:]):
        turned = value.shape[::-1] if name in TURNED else value.shape
        shapes.setdefault(name, shape(turned, F32))
    first = place.first
    cross_first = first["large_cross"]
    parts = (
        ("mlp", 0, first["other"]),
        ("cross", cross_first, first["large_out"] - cross_first),
        ("heads", first["large_out"], first["tables"] - first["large_out"]),
        ("tables", first["tables"], 64),
    )
    results = pl.pallas_call(
        functools.partial(unpack_kernel, place, ds, dl, parts),
        out_shape=tuple(shapes[name] for name in OUTS),
        in_specs=(hbm,) * 5,
        out_specs=(hbm,) * len(OUTS),
        scratch_shapes=[
            pltpu.VMEM((place.total, LANES), BF16),
        ]
        + [pltpu.VMEM((ds, small.rows), BF16), pltpu.VMEM(large_rows.shape, BF16)] * 2
        + [pltpu.VMEM(shapes[name].shape, F32) for name in OUTS[2:]]
        + [copies((8,)), copies((len(OUTS),))],
        compiler_params=pltpu.CompilerParams(vmem_limit_bytes=VMEM_LIMIT),
        name="unpack",
    )(*values)

    def restore(name, value):
        return value.T if name in TURNED else value

    return tuple(restore(name, value) for name, value in zip(OUTS, results))


def solution(mesh):
    both = ("dp", "tensor")
    rows = P(both, None)
    mlp = (P(None, "tensor"), P("tensor"), P("tensor", None))

    def shards(*args):
        return run_layer(args, mesh.shape["dp"])

    return jax.shard_map(
        shards,
        mesh=mesh,
        in_specs=(rows, rows, P(None, both), rows, rows)
        + ((P(), P()) + mlp) * 2
        + (P(),) * 12,
        out_specs=(rows,) * 4 + ((P(), P()) + mlp) * 2 + (P(),) * 12,
        check_vma=False,
    )
```

```python
import functools
import collections
import jax
import jax.numpy as jnp
from jax import lax
from jax.experimental import pallas as pl
from jax.experimental.pallas import tpu as pltpu
from jax.sharding import PartitionSpec as P

HEADS = 6
VMEM_LIMIT = 64 * 1024 * 1024
NEGATIVE = -1e30
EPSILON = 1e-06
F32, BF16 = jnp.float32, jnp.bfloat16
LANES = 384
CLS = 16
STACK = HEADS * CLS

GLOBAL_ROWS, LOCAL_ROWS = (197, 145), (37, 65)
BLOCK = 32
LOG2E = 1.4426950408889634


def low(values):
    return values.astype(BF16)


def dot(left, right, left_axis, right_axis):
    return lax.dot_general(
        left, right, (((left_axis,), (right_axis,)), ((), ())), preferred_element_type=F32
    )


def nn(left, right):
    return dot(left, right, 1, 0)


def nt(left, right):
    return dot(left, right, 1, 1)


def tn(left, right):
    return dot(left, right, 0, 0)


class Branch:
    def __init__(self, index, rows, columns, hidden, width, layout):
        self.index, self.rows, self.columns, self.hidden = index, rows, columns, hidden
        self.head = columns // HEADS
        self.width, self.slots = width, len(layout)
        self.tokens = width * self.slots
        self.pieces = []
        self.bounds = []
        g_rows, l_rows = GLOBAL_ROWS[index], LOCAL_ROWS[index]
        for slot, crops in enumerate(layout):
            lane, ends = 0, []
            for crop in crops:
                length = g_rows if crop < 4 else l_rows if crop < 6 else rows - 4 * g_rows - 2 * l_rows
                self.pieces.append((slot * width + lane, length, crop))
                lane += length
                ends.append(lane)
            assert lane <= width
            self.bounds.append(ends)


def norm(values, axis):
    center = values - jnp.mean(values, axis, keepdims=True)
    scale = lax.rsqrt(jnp.mean(center * center, axis, keepdims=True) + EPSILON)
    return center * scale, scale


def fold(values):
    total = values[0:8]
    for at in range(8, values.shape[0], 8):
        total = total + values[at : at + 8]
    return total


def fold_lanes(values):
    total = values[:, 0:128]
    for at in range(128, values.shape[1], 128):
        total = total + values[:, at : at + 128]
    return total


def chunks(columns):
    return [slice(at, at + BLOCK) for at in range(0, columns, BLOCK)]


def norm_columns(load, columns, keep):
    total = sum(fold(load(rows)) for rows in chunks(columns))
    mean = jnp.sum(total, 0, keepdims=True) * (1.0 / columns)
    spread = 0.0
    for rows in chunks(columns):
        center = load(rows) - mean
        spread = spread + fold(center * center)
    spread = jnp.sum(spread, 0, keepdims=True) * (1.0 / columns)
    scale = lax.rsqrt(spread + EPSILON)
    keep(mean, scale)
    return mean, scale


def norm_columns_back(load, grad, columns, mean, scale, gain, sums, store):
    first = second = 0.0
    for rows in chunks(columns):
        unit = (load(rows) - mean) * scale
        back = grad(rows)
        both = back * unit
        sums[0, rows, :] += fold_lanes(back)
        sums[1, rows, :] += fold_lanes(both)
        first = first + fold(back * gain(rows))
        second = second + fold(both * gain(rows))
    first = jnp.sum(first, 0, keepdims=True) * (1.0 / columns)
    second = jnp.sum(second, 0, keepdims=True) * (1.0 / columns)
    for rows in chunks(columns):
        unit = (load(rows) - mean) * scale
        store(rows, scale * (grad(rows) * gain(rows) - first - unit * second))


def norm_back(grad, unit, scale, axis):
    return scale * (
        grad
        - jnp.mean(grad, axis, keepdims=True)
        - unit * jnp.mean(grad * unit, axis, keepdims=True)
    )


def smooth_parts(values):
    chance = 0.5 + 0.5 * lax.erf(values * (0.5**0.5))
    slope = chance + values * (jnp.exp(values * values * -0.5) * 0.3989422804014327)
    return values * chance, slope


def pick(at, values):
    if isinstance(at, int):
        return values[at]
    result = values[-1]
    for place in range(len(values) - 2, -1, -1):
        result = jnp.where(at == place, values[place], result)
    return result


def iota(shape, axis):
    return lax.broadcasted_iota(jnp.int32, shape, axis)


def each_slot(branch, body, between=None):
    if between is None:
        lax.fori_loop(0, branch.slots, lambda slot, carry: body(slot) or carry, 0)
        return
    for slot in range(branch.slots):
        body(slot)
        between(slot)


def slot_columns(branch, slot):
    if isinstance(slot, int):
        return slice(slot * branch.width, (slot + 1) * branch.width)
    return pl.ds(pl.multiple_of(slot * branch.width, branch.width), branch.width)


def places(counts, b):
    starts = [jnp.int32(0)] * 7
    begin, globals_seen, locals_seen = jnp.int32(0), jnp.int32(0), jnp.int32(0)
    for crop in range(6):
        rows = counts[b.index, crop]
        is_global = counts[0, crop] == GLOBAL_ROWS[0]
        for k in range(4):
            starts[k] = jnp.where(is_global & (globals_seen == k), begin, starts[k])
        for k in range(2):
            starts[4 + k] = jnp.where((~is_global) & (locals_seen == k), begin, starts[4 + k])
        begin = begin + rows
        globals_seen = globals_seen + jnp.where(is_global, 1, 0)
        locals_seen = locals_seen + jnp.where(is_global, 0, 1)
    starts[6] = begin
    return starts


def lay_out(b, r, counts):
    starts = places(counts, b)
    lane = iota((1, b.tokens), 1)
    source = jnp.full((1, b.tokens), -1, jnp.int32)
    patch = jnp.full((1, b.tokens), -1, jnp.int32)
    cls = jnp.full((1, b.tokens), -1, jnp.int32)
    for first, length, crop in b.pieces:
        inside = (lane >= first) & (lane < first + length)
        source = jnp.where(inside, lane - first + starts[crop], source)
        if crop < 6:
            patch = jnp.where(inside & (lane > first), crop, patch)
            cls = jnp.where(lane == first, crop, cls)
    r.index[0:1, :] = source
    r.index[1:2, :] = patch
    r.index[2:3, :] = cls
    at = iota((CLS, 1), 0)
    first_rows = jnp.full((CLS, 1), -1, jnp.int32)
    for crop in range(6):
        first_rows = jnp.where(at == crop, starts[crop], first_rows)
    chosen = low((iota((CLS, b.rows), 1) == first_rows).astype(F32))
    r.cot_cls[...] = nt(chosen, r.cot[...])


def bring_in(b, r):
    def body(slot):
        cols = slot_columns(b, slot)
        chosen = low((iota((b.rows, b.width), 0) == r.index[0:1, cols]).astype(F32))
        r.x[:, cols] = low(nn(r.rows[...], chosen))
        keep = r.index[2:3, cols] < 0
        r.cotT[:, cols] = low(jnp.where(keep, nn(r.cot[...], chosen), 0.0))

    each_slot(b, body, lambda slot: None)


def slot_mask(b, slot):
    ends = [pick(slot, [e[min(i, len(e) - 1)] for e in b.bounds]) for i in range(3)]

    def segment(axis):
        at = iota((b.width, b.width), axis)
        total = jnp.zeros((b.width, b.width), jnp.int32)
        for end in ends[: max(len(e) for e in b.bounds)]:
            total = total + (at >= end).astype(jnp.int32)
        return total

    return jnp.where(segment(0) == segment(1), 0.0, NEGATIVE)


def squares(b, refs):
    result = []
    for ref in refs:
        for row in range(0, ref.shape[0] - b.width + 1, b.width):
            for lane in range(0, ref.shape[1] - b.width + 1, b.width):
                result.append(ref.at[row : row + b.width, lane : lane + b.width])
    return result


def parts_of(b, h):
    first = [part * b.columns + h * b.head for part in range(3)]
    return [slice(at, at + b.head) for at in first]


def interleave(before, middle, after, count, ahead):
    for h in range(min(2, count)):
        before(h)
    for h in range(HEADS):
        if ahead and h + 2 < HEADS:
            before(h + 2)
        middle(h)
        if not ahead and h + 2 < HEADS:
            before(h + 2)
        if not ahead:
            after(h)
        elif h > 0:
            after(h - 1)
    if ahead:
        after(HEADS - 1)


def forward_attention(b, r, wide_work, low_work, between=None):
    columns, width = b.columns, b.width
    factor = float(b.head) ** (-0.5) * LOG2E
    wide, lows = squares(b, wide_work), squares(b, low_work)
    many = min(len(wide), len(lows), HEADS)
    mask_ref = r.mask.at[0:width, 0:width]

    def body(slot):
        cols = slot_columns(b, slot)

        def tokens(rows):
            return r.x[rows, cols].astype(F32)

        def keep(at):
            def put(mean, scale):
                r.stats[at : at + 1, cols] = mean
                r.stats[at + 1 : at + 2, cols] = scale

            return put

        mean, scale = norm_columns(tokens, columns, keep(0))
        for rows in chunks(columns):
            unit = (tokens(rows) - mean) * scale
            r.a[rows, cols] = low(unit * r.tabT[rows, 0:1] + r.tabT[rows, 5:6])
        a = r.a[0:columns, cols]
        for third, bias in ((0, 6), (1, None), (2, 7)):
            rows = slice(third * columns, (third + 1) * columns)
            product = nn(r.w_inT[rows, :], a)
            r.qkv[rows, cols] = low(product if bias is None else product + r.tabT[:, bias : bias + 1])
        mask_ref[...] = slot_mask(b, slot)
        for begin in range(0, HEADS, many):
            heads = range(begin, min(begin + many, HEADS))
            for h in heads:
                q, k, v = parts_of(b, h)
                wide[h - begin][...] = tn(r.qkv[k, cols], r.qkv[q, cols])
            for h in heads:
                scores = wide[h - begin][...] * factor + mask_ref[...]
                highest = jnp.max(scores, 0, keepdims=True)
                powers = jnp.exp2(scores - highest)
                total = jnp.sum(powers, 0, keepdims=True)
                r.logs[h : h + 1, cols] = highest + jnp.log2(total)
                lows[h - begin][...] = low(powers * (1.0 / total))
            for h in heads:
                q, k, v = parts_of(b, h)
                r.o[q, cols] = low(nn(r.qkv[v, cols], lows[h - begin][...]))
        r.y[:, cols] = (
            r.x[:, cols].astype(F32) + tn(r.w_out[...], r.o[0:columns, cols]) + r.tabT[:, 8:9]
        )
        mean, scale = norm_columns(lambda rows: r.y[rows, cols], columns, keep(2))
        for rows in chunks(columns):
            unit = (r.y[rows, cols] - mean) * scale
            r.c[rows, cols] = low(unit * r.tabT[rows, 1:2] + r.tabT[rows, 9:10])

    each_slot(b, body, between)


def forward_mlp(b, r, between=None):
    chunk = LANES // 2
    columns = b.columns
    r.cls[...] = jnp.zeros_like(r.cls)

    def body(slot):
        cols = slot_columns(b, slot)
        c = r.c[0:columns, cols]
        for at in range(0, b.hidden, chunk):
            bias = r.tabT[at % columns : at % columns + chunk, 19 + at // columns : 20 + at // columns]
            active, slope = smooth_parts(nn(r.w_upT[at : at + chunk, :], c) + bias)
            r.u[at : at + chunk, cols] = low(active)
            r.g[at : at + chunk, cols] = low(slope)
        r.z[:, cols] = r.y[:, cols] + nn(r.w_downT[...], r.u[0 : b.hidden, cols]) + r.tabT[:, 10:11]

        def keep(mean, scale):
            r.stats[4:5, cols] = mean
            r.stats[5:6, cols] = scale

        mean, scale = norm_columns(lambda rows: r.z[rows, cols], columns, keep)
        for rows in chunks(columns):
            z = r.z[rows, cols]
            r.out[rows, cols] = low(z)
            r.n[rows, cols] = low((z - mean) * scale * r.tabT[rows, 3:4] + r.tabT[rows, 14:15])
        chosen = low((iota((CLS, b.width), 0) == r.index[2:3, cols]).astype(F32))
        rest = low(r.z[:, cols] - r.out[:, cols].astype(F32))
        r.cls[...] += nt(chosen, r.out[:, cols]) + nt(chosen, rest)

    each_slot(b, body, between)


def backward_cross(b, r, work, between=None):
    columns, width = b.columns, b.width
    r.sums[...] = jnp.zeros_like(r.sums)
    cls_grad = r.cls_grad[...]
    high = low(cls_grad)
    pair = jnp.concatenate([high, low(cls_grad - high.astype(F32))], 0)
    maps, pair = r.maps[...].T, pair.T

    def body(slot):
        cols = slot_columns(b, slot)
        work[0:columns, 0:width] = nn(maps, r.sp[:, cols])
        chosen = low((iota((CLS, width), 0) == r.index[2:3, cols]).astype(F32))
        work[0:columns, width : 2 * width] = nn(pair, jnp.concatenate([chosen, chosen], 0))

        def store(rows, back):
            r.z[rows, cols] = r.cotT[rows, cols].astype(F32) + work[rows, width : 2 * width] + back

        norm_columns_back(
            lambda rows: r.z[rows, cols],
            lambda rows: work[rows, 0:width],
            columns,
            r.stats[4:5, cols],
            r.stats[5:6, cols],
            lambda rows: r.tabT[rows, 3:4],
            r.sums.at[:, 0:columns, :],
            store,
        )

    each_slot(b, body, between)
    r.table[3:4, :] += row_sum(r.sums[1, 0:columns, :])
    r.table[5 + 9 : 5 + 10, :] += row_sum(r.sums[0, 0:columns, :])


def row_sum(values):
    return jnp.sum(values.T, 0, keepdims=True)


def put_out(b, r, between=None):
    def replace(slot):
        cols = slot_columns(b, slot)
        cls = r.index[2:3, cols]
        chosen = low((iota((CLS, b.width), 0) == cls).astype(F32))
        new = tn(r.new_cls[...], chosen)
        r.out[:, cols] = jnp.where(cls >= 0, new, r.out[:, cols].astype(F32)).astype(BF16)

    each_slot(b, replace)
    put_back(b, r, r.out, between)


def put_back(b, r, values, between=None):
    tile = b.rows // 4

    def part(step):
        first = step * tile if isinstance(step, int) else pl.multiple_of(step * tile, tile)
        chosen = low((iota((tile, b.tokens), 0) + first == r.index[0:1, :]).astype(F32))
        if b.index == 0:
            r.staged[:, pl.ds(first, tile)] = low(nt(values[...], chosen))
        else:
            r.staged[pl.ds(first, tile), :] = low(nt(chosen, values[...]))

    if between is None:
        lax.fori_loop(0, 4, lambda step, carry: part(step) or carry, 0)
        return
    for step in range(4):
        part(step)
        between(step)


def backward_mlp(b, r, work, between=None):
    half, columns, width = b.hidden // 2, b.columns, b.width
    r.sums[...] = jnp.zeros_like(r.sums)

    def body(slot):
        cols = slot_columns(b, slot)
        r.zg[:, cols] = low(r.z[:, cols])
        z_low = r.zg[:, cols]
        for part in range(2):
            mine = slice(part * half, (part + 1) * half)
            r.g[mine, cols] = low(r.down_times(part, z_low) * r.g[mine, cols].astype(F32))
        work[0:columns, 0:width] = nn(r.up[0][...], r.g[0:half, cols]) + nn(
            r.up[1][...], r.g[half:, cols]
        )

        def store(rows, back):
            grad = r.z[rows, cols] + back
            r.z[rows, cols] = grad
            r.yg[rows, cols] = low(grad)

        norm_columns_back(
            lambda rows: r.y[rows, cols],
            lambda rows: work[rows, 0:width],
            columns,
            r.stats[2:3, cols],
            r.stats[3:4, cols],
            lambda rows: r.tabT[rows, 1:2],
            r.sums.at[:, 0:columns, :],
            store,
        )
        r.og_rows(slot, slice(0, columns))[...] = low(nn(r.w_out[...], r.yg[:, cols]))

    each_slot(b, body, between)
    r.table[1:2, :] = row_sum(r.sums[1, 0:columns, :])
    r.table[5 + 4 : 5 + 5, :] = row_sum(r.sums[0, 0:columns, :])


def backward_attention(b, r, wide_work, low_work, more_work, between=None):
    columns, width = b.columns, b.width
    factor = float(b.head) ** (-0.5)
    wide, lows, more = squares(b, wide_work), squares(b, low_work), squares(b, more_work)
    many = min(len(wide) // 2, len(lows), len(more), HEADS)
    mask_ref = r.mask.at[0:width, 0:width]

    def body(slot):
        cols = slot_columns(b, slot)
        mask_ref[...] = slot_mask(b, slot)

        def before(h):
            q, k, v = parts_of(b, h)
            wide[h % many][...] = tn(r.qkv[k, cols], r.qkv[q, cols])
            wide[many + h % many][...] = tn(r.qkv[v, cols], r.og_rows(slot, q)[...])

        def middle(h):
            chances = jnp.exp2(
                wide[h % many][...] * (factor * LOG2E) + (mask_ref[...] - r.logs[h : h + 1, cols])
            )
            lows[h % many][...] = low(chances)
            chance_grad = wide[many + h % many][...]
            inner = jnp.sum(chance_grad * chances, 0, keepdims=True)
            more[h % many][...] = low(chances * ((chance_grad - inner) * factor))

        def after(h):
            q, k, v = parts_of(b, h)
            q_low, k_low = r.qkv[q, cols], r.qkv[k, cols]
            score_grad = more[h % many][...]
            r.qkv[q, cols] = low(nn(k_low, score_grad))
            r.qkv[k, cols] = low(nt(q_low, score_grad))
            r.qkv[v, cols] = low(nt(r.og_rows(slot, q)[...], lows[h % many][...]))

        interleave(before, middle, after, many, b.index == 0)

    each_slot(b, body, between)


def backward_first_norm(b, r, work, between=None):
    columns, width = b.columns, b.width
    r.sums[...] = jnp.zeros_like(r.sums)

    def body(slot):
        cols = slot_columns(b, slot)
        work[0:columns, 0:width] = nn(r.w_in[...], r.qkv[:, cols])

        def store(rows, back):
            r.x[rows, cols] = low(r.z[rows, cols] + back)

        norm_columns_back(
            lambda rows: r.x[rows, cols].astype(F32),
            lambda rows: work[rows, 0:width],
            columns,
            r.stats[0:1, cols],
            r.stats[1:2, cols],
            lambda rows: r.tabT[rows, 0:1],
            r.sums.at[:, 0:columns, :],
            store,
        )
    each_slot(b, body, between)
    r.table[0:1, :] = row_sum(r.sums[1, 0:columns, :])
    r.table[5:6, :] = row_sum(r.sums[0, 0:columns, :])
def head_mask(columns):
    head = columns // HEADS
    at = iota((STACK, columns), 1)
    first = iota((STACK, columns), 0) // CLS * head
    return (at >= first) & (at < first + head)


def spread(values, mask):
    return jnp.where(mask, jnp.concatenate([values] * HEADS, 0), 0.0)


def gather_heads(values, mask):
    values = jnp.where(mask, values, 0.0)
    total = values[0:CLS]
    for h in range(1, HEADS):
        total = total + values[h * CLS : (h + 1) * CLS]
    return total


def column_sum(values):
    return jnp.sum(values, 0, keepdims=True)


def cross(b, r, o, ro, g):
    wide = o.columns
    factor = float(o.head) ** (-0.5)
    mask = head_mask(wide)
    og, ob = ro.gains, ro.shifts

    def row(table, at):
        return table[at : at + 1, :].astype(F32)

    enter_on, enter_back, leave_on, leave_back = (nn, nt, nt, nn) if b.index == 0 else (nt, nn, nn, nt)

    xc = r.cls[...]
    yield
    unit2, scale2 = norm(xc, 1)
    lifted, slope2 = smooth_parts(unit2 * row(r.gains, 2) + row(r.shifts, 6))
    lifted = low(lifted)
    yield
    moved = enter_on(lifted, r.enter[...]) + row(ob, 8)
    yield
    unit3, scale3 = norm(moved, 1)
    query_norm = low(unit3 * row(og, 3) + row(ob, 9))
    yield
    q = low(nn(query_norm, ro.cross_in[:, 0:wide]) + row(ob, 10))
    own_k = low(nn(query_norm, ro.cross_in[:, wide : 2 * wide]))
    own_v = low(nn(query_norm, ro.cross_in[:, 2 * wide : 3 * wide]) + row(ob, 11))
    q_all = spread(q.astype(F32), mask)
    k_all = spread(own_k.astype(F32), mask)
    v_all = spread(own_v.astype(F32), mask)
    yield
    key_map = low(nt(low(q_all), ro.cross_in[:, wide : 2 * wide]))
    yield
    own_score = jnp.sum(q_all * k_all, 1, keepdims=True) * factor
    usable = ro.index[1:2, :] == iota((STACK, o.tokens), 0) % CLS
    yield
    scores = jnp.where(usable, nn(key_map, ro.n[...]) * factor, NEGATIVE)
    yield
    highest = jnp.maximum(own_score, jnp.max(scores, 1, keepdims=True))
    powers = jnp.exp(scores - highest)
    own_power = jnp.exp(own_score - highest)
    yield
    inverse = 1.0 / (own_power + jnp.sum(powers, 1, keepdims=True))
    chances = powers * inverse
    own_chance = own_power * inverse
    chances_low = low(chances)
    own_low = low(own_chance).astype(F32)
    ro.sp[STACK : 2 * STACK, :] = chances_low
    total = jnp.sum(chances_low.astype(F32), 1, keepdims=True)
    yield
    mean_row = low(nt(chances_low, ro.n[...]))
    value_bias = row(ob, 11)
    yield
    mixed = own_low * v_all + nn(mean_row, ro.cross_in[:, 2 * wide : 3 * wide]) + total * value_bias
    attended = low(gather_heads(mixed, mask))
    yield
    joined = moved + nn(attended, ro.cross_out[...]) + row(ob, 12)
    yield
    unit4, scale4 = norm(joined, 1)
    spread_out, slope4 = smooth_parts(unit4 * row(og, 4) + row(ob, 13))
    spread_out = low(spread_out)
    r.new_cls[...] = low(leave_on(spread_out, r.leave[...]) + row(r.shifts, 7))

    yield
    new_grad = r.cot_cls[...]
    new_low = low(new_grad)
    r.table[5 + 7 : 5 + 8, :] = column_sum(new_grad)
    yield
    g.leave(tn(new_low, spread_out) if b.index == 0 else tn(spread_out, new_low))
    yield
    back = leave_back(new_low, r.leave[...]) * slope4
    ro.table[4:5, :] = column_sum(back * unit4)
    ro.table[5 + 13 : 5 + 14, :] = column_sum(back)
    yield
    joined_grad = norm_back(back * row(og, 4), unit4, scale4, 1)
    ro.table[5 + 12 : 5 + 13, :] = column_sum(joined_grad)
    joined_low = low(joined_grad)
    yield
    g.cross_out(tn(attended, joined_low))
    yield
    mixed_grad = low(nt(joined_low, ro.cross_out[...])).astype(F32)
    yield
    mixed_all = spread(mixed_grad, mask)
    mixed_all_low = low(mixed_all)
    own_v_grad = gather_heads(own_low * mixed_all, mask)
    own_chance_grad = jnp.sum(mixed_all * v_all, 1, keepdims=True)
    yield
    value_map = low(nt(mixed_all_low, ro.cross_in[:, 2 * wide : 3 * wide]))
    yield
    chance_grad = nn(value_map, ro.n[...]) + jnp.sum(mixed_all * value_bias, 1, keepdims=True)
    yield
    inner = own_chance_grad * own_chance + jnp.sum(chance_grad * chances, 1, keepdims=True)
    score_grad = low(chances * (chance_grad - inner) * factor)
    own_score_grad = low(own_chance * (own_chance_grad - inner) * factor).astype(F32)
    ro.sp[0:STACK, :] = score_grad
    yield
    mean_back = low(nt(score_grad, ro.n[...]))
    yield
    q_grad = gather_heads(
        own_score_grad * k_all + nn(mean_back, ro.cross_in[:, wide : 2 * wide]), mask
    )
    own_k_grad = gather_heads(own_score_grad * q_all, mask)
    ro.table[5 + 10 : 5 + 11, :] = column_sum(q_grad)
    ro.table[5 + 11 : 5 + 12, :] = column_sum(own_v_grad) + column_sum(total * mixed_all)
    q_low, k_low, v_low = low(q_grad), low(own_k_grad), low(own_v_grad)
    yield
    g.cross_in(
        0,
        tn(query_norm, q_low),
    )
    yield
    g.cross_in(
        1,
        tn(
            jnp.concatenate([query_norm, mean_back], 0),
            jnp.concatenate([k_low, low(q_all)], 0),
        ),
    )
    yield
    g.cross_in(
        2,
        tn(
            jnp.concatenate([query_norm, mean_row], 0),
            jnp.concatenate([v_low, mixed_all_low], 0),
        ),
    )
    yield
    back = (
        nt(q_low, ro.cross_in[:, 0:wide])
        + nt(k_low, ro.cross_in[:, wide : 2 * wide])
        + nt(v_low, ro.cross_in[:, 2 * wide : 3 * wide])
    )
    ro.table[3:4, :] = column_sum(back * unit3)
    ro.table[5 + 9 : 5 + 10, :] = column_sum(back)
    yield
    moved_grad = joined_grad + norm_back(back * row(og, 3), unit3, scale3, 1)
    ro.table[5 + 8 : 5 + 9, :] = column_sum(moved_grad)
    moved_low = low(moved_grad)
    yield
    g.enter(tn(lifted, moved_low) if b.index == 0 else tn(moved_low, lifted))
    yield
    back = enter_back(moved_low, r.enter[...]) * slope2
    r.table[2:3, :] = column_sum(back * unit2)
    r.table[5 + 6 : 5 + 7, :] = column_sum(back)
    r.cls_grad[...] = norm_back(back * row(r.gains, 2), unit2, scale2, 1)
    ro.maps[0:STACK, :] = key_map
    ro.maps[STACK : 2 * STACK, :] = value_map


def bit_of(value, place):
    return (value // (1 << place)) % 2


class Links:
    def __init__(self, dp_bits):
        self.bits = ["t"] + list(range(dp_bits))

    def bind(self, solo=None):
        self.dp = self.tensor = 0
        if solo is None:
            self.dp, self.tensor = lax.axis_index("dp"), lax.axis_index("tensor")

    def bit(self, name):
        return self.tensor if name == "t" else bit_of(self.dp, name)

    def partner(self, names):
        dp, tensor = self.dp, self.tensor
        for name in names:
            if name == "t":
                tensor = 1 - self.tensor
            else:
                dp = dp + (1 - 2 * bit_of(self.dp, name)) * (1 << name)
        return (dp, tensor)


def subsets(names):
    for number in range(1, 1 << len(names)):
        yield number, [name for at, name in enumerate(names) if number >> at & 1]


class Pool:
    def __init__(self):
        self.rows, self.copies, self.signals = 0, 0, 0

    def signal(self):
        self.signals += 1
        return self.signals - 1

    def take(self, rows, copies):
        at = (self.rows, self.copies)
        self.rows, self.copies = self.rows + rows, self.copies + copies
        return at


class Group:
    def __init__(self, pool, first, rows, phases, apart=None):
        self.first, self.rows, self.apart = first, rows, apart
        self.steps, size, bases = [], rows, 1 if apart is None else 2
        self.frees = {}
        phases = list(phases)
        while phases:
            names, kind = phases.pop(0)
            count = 1 << len(names)
            if kind == "halve" and size % (16 * count):
                kind = "full"
                if len(names) > 1:
                    phases = [((name,), "halve") for name in names] + phases
                    continue
            if kind == "merge":
                bases = 1
                self.steps.append((kind, names, size, pool.take(size, 1), 1))
            elif kind == "halve":
                at = pool.take(bases * (count - 1) * (size // count), 2 * bases * (count - 1))
                self.steps.append((kind, names, size, at, bases))
                self.frees[len(self.steps) - 1] = pool.signal()
                size //= count
            else:
                at = pool.take(bases * (count - 1) * size, bases * (count - 1))
                self.steps.append((kind, names, size, at, bases))
        self.plan = [("reduce", step, self.frees.get(at)) for at, step in enumerate(self.steps)]
        self.plan += [("gather",) + step[1:] for step in reversed(self.plan) if step[2] is not None]

    def bind(self, links, buffer, received, send, recv, free):
        self.links, self.buffer, self.received = links, buffer, received
        self.send, self.recv, self.free = send, recv, free
        self.lo, self.at, self.flight, self.offsets = 0, 0, [], {}
        return self

    def chunk(self, names, flipped):
        index = 0
        for place, name in enumerate(names):
            bit = self.links.bit(name)
            index = index + (1 - bit if name in flipped else bit) * (1 << place)
        return index

    def rows_at(self, base, first, size):
        return pl.ds(pl.multiple_of(base + first, 16), size)

    def copy(self, source, target, sem, partner):
        return pltpu.make_async_remote_copy(
            src_ref=source,
            dst_ref=target,
            send_sem=self.send.at[sem],
            recv_sem=self.recv.at[sem],
            device_id=partner,
            device_id_type=pl.DeviceIdType.MESH,
        )

    def bases(self, count):
        return (self.first, self.apart)[:count]

    def begin(self):
        if self.at == len(self.plan):
            return
        way, (kind, names, size, (row, sem), count), free = self.plan[self.at]
        flight = []
        if kind == "merge":
            source = self.buffer.at[self.rows_at(self.apart, self.lo, size), :]
            target = self.received.at[pl.ds(row, size), :]
            flight.append(self.copy(source, target, sem, self.links.partner(names)))
        elif way == "reduce":
            part = size // (1 << len(names)) if kind == "halve" else size
            for base in self.bases(count):
                for number, flipped in subsets(names):
                    first = self.lo
                    if kind == "halve":
                        first = first + self.chunk(names, flipped) * part
                    source = self.buffer.at[self.rows_at(base, first, part), :]
                    target = self.received.at[pl.ds(row, part), :]
                    flight.append(self.copy(source, target, sem, self.links.partner(flipped)))
                    row, sem = row + part, sem + 1
        else:
            part = size // (1 << len(names))
            before = self.offsets[(kind, tuple(names), size)]
            pl.semaphore_wait(self.free.at[free], (1 << len(names)) - 1)
            sem = sem + count * ((1 << len(names)) - 1)
            first = before + self.chunk(names, []) * part
            for number, flipped in subsets(names):
                mine = self.buffer.at[self.rows_at(self.first, first, part), :]
                flight.append(self.copy(mine, mine, sem, self.links.partner(flipped)))
                sem += 1
        for copy in flight:
            copy.start()
        self.flight = flight

    def end(self):
        if not self.flight:
            return
        way, (kind, names, size, (row, sem), count), free = self.plan[self.at]
        for copy in self.flight:
            copy.wait()
        self.flight = []
        self.at += 1
        if way == "gather":
            return
        if kind == "merge":
            self.add(self.first, self.lo, size, [row])
            return
        part = size
        parts = (1 << len(names)) - 1
        if kind == "halve":
            part = size // (parts + 1)
            self.offsets[(kind, tuple(names), size)] = self.lo
            self.lo = self.lo + self.chunk(names, []) * part
            for number, flipped in subsets(names):
                pl.semaphore_signal(
                    self.free.at[free],
                    inc=1,
                    device_id=self.links.partner(flipped),
                    device_id_type=pl.DeviceIdType.MESH,
                )
        for base in self.bases(count):
            self.add(base, self.lo, part, [row + i * part for i in range(parts)])
            row += parts * part

    def add(self, base, first, size, rows):
        block = max(block for block in range(16, 257, 16) if size % block == 0)

        def body(step, carry):
            here = self.rows_at(base, first + step * block, block)
            terms = [self.buffer[here, :]]
            for row in rows:
                at = pl.ds(pl.multiple_of(row + step * block, 16), block)
                terms.append(self.received[at, :])
            if len(rows) > 1:
                terms = [term.astype(F32) for term in terms]
            while len(terms) > 1:
                terms = [a + b for a, b in zip(terms[0::2], terms[1::2])]
            self.buffer[here, :] = low(terms[0])
            return carry

        if size == block:
            body(0, 0)
        else:
            lax.fori_loop(0, size // block, body, 0)

    def advance(self):
        self.end()
        self.begin()

    @property
    def done(self):
        return self.at == len(self.plan)


def greet(links, partners):
    barrier = pltpu.get_barrier_semaphore()
    for names in partners:
        pl.semaphore_signal(
            barrier, inc=1, device_id=links.partner(names), device_id_type=pl.DeviceIdType.MESH
        )


def all_here(partners):
    pl.semaphore_wait(pltpu.get_barrier_semaphore(), len(partners))


class Swap:
    def __init__(self, links, pairs, sends, receives):
        self.links, self.pairs, self.sends, self.receives = links, pairs, sends, receives

    def copies(self, step):
        result = []
        for at, (mine, theirs) in enumerate(self.pairs):
            half = mine.shape[0] // 2
            rows = pl.ds(pl.multiple_of(self.links.bit(0) * half, 16), half)
            result.append(
                pltpu.make_async_remote_copy(
                    src_ref=(mine if step == 0 else theirs).at[rows, :],
                    dst_ref=theirs.at[rows, :],
                    send_sem=self.sends.at[step, at],
                    recv_sem=self.receives.at[step, at],
                    device_id=self.links.partner(["t"] if step == 0 else [0]),
                    device_id_type=pl.DeviceIdType.MESH,
                )
            )
        return result

    def start(self, step):
        for copy in self.copies(step):
            copy.start()

    def wait(self, step):
        for copy in self.copies(step):
            copy.wait()


class Place:
    def __init__(self, small, large):
        ds, dl = small.columns, large.columns
        self.first, self.size, at = {}, {}, 0
        for name, rows in (
            ("small_up", ds), ("small_down", ds), ("large_up", 2 * dl), ("large_down", 2 * dl),
            ("other", 2 * ds + 4 * dl),
            ("large_cross", 4 * dl), ("small_enter", ds), ("small_leave", ds),
            ("large_enter", ds), ("large_leave", ds), ("small_cross", 2 * ds),
            ("large_out", dl), ("large_in", 3 * dl), ("small_heads", 2 * ds), ("tables", 64),
        ):
            self.first[name], self.size[name] = at, rows
            at += rows
        self.total = at

    def rows(self, name, part=0, size=None):
        first = self.first[name] + part
        return slice(first, first + (self.size[name] if size is None else size))


class CrossGrads:
    def __init__(self, own, other, place, buffer):
        self.own, self.other, self.place, self.buffer = own, other, place, buffer
        self.kept = {}

    def put(self, name, part, values):
        first = self.place.first[name] + part
        self.buffer[first : first + values.shape[0], :] = low(values)

    def cross_in(self, third, values):
        if self.other.index == 1:
            self.put("large_cross", third * self.other.columns, values)
            return
        self.kept[third] = values
        if third == 1:
            self.put("small_cross", 0, jnp.concatenate([self.kept[0], values], 1))
        if third == 2:
            self.put(
                "small_cross", self.other.columns, jnp.concatenate([values, self.kept["out"]], 1)
            )

    def cross_out(self, values):
        if self.other.index == 1:
            self.put("large_cross", 3 * self.other.columns, values)
        else:
            self.kept["out"] = values

    def enter(self, values):
        if self.own.index == 0:
            self.put("small_enter", 0, values)
        else:
            self.put("large_enter", 0, values)

    def leave(self, values):
        if self.own.index == 1:
            self.put("large_leave", 0, values)
        else:
            self.put("small_leave", 0, values)


def mlp_grads(b, r, place, buffer, tick):
    half, columns = b.hidden // 2, b.columns
    name = ("small", "large")[b.index]
    for part in range(2):
        first = place.first["other"] * part + place.first[name + "_up"]
        for at in range(0, half, LANES):
            up = nt(r.c[...], r.g[part * half + at : part * half + at + LANES, :])
            buffer[first : first + columns, :] = low(up[0:columns])
            first += columns
            row = b.index + at // LANES
            r.bias_rows[part, row : row + 1, :] = up[columns : columns + 1]
        tick(part)
    r.table[5 + 5 : 5 + 6, :] = nt(r.u[b.hidden : b.hidden + 16, :], r.zg[...])[0:1]
    for part in range(2):
        mine = slice(part * half, (part + 1) * half)
        first = place.first["other"] * part + place.first[name + "_down"]
        if b.index == 0:
            buffer[first : first + columns, :] = low(nt(r.zg[...], r.u[mine, :]))
        else:
            buffer[first : first + half, :] = low(nt(r.u[mine, :], r.zg[...]))
        tick(2 + part)


def out_grads(b, r):
    w_out = nt(r.o[...], r.yg[...])
    r.table[5 + 3 : 5 + 4, :] = w_out[b.columns : b.columns + 1, :]
    return w_out[0 : b.columns]


def in_grads(b, r, third):
    columns = b.columns
    w_in = nt(r.a[...], r.qkv[third * columns : (third + 1) * columns, :])
    if third != 1:
        row = 5 + 1 + third // 2
        r.table[row : row + 1, :] = w_in[columns : columns + 1, :]
    return w_in[0:columns]


def large_in_grads(b, r, place, buffer):
    for third in range(3):
        first = place.first["large_in"] + third * b.columns
        buffer[first : first + b.columns, :] = low(in_grads(b, r, third))


def small_head_grads(b, r, place, buffer):
    columns, first = b.columns, place.first["small_heads"]
    thirds = [in_grads(b, r, third) for third in range(3)] + [out_grads(b, r)]
    for half in range(2):
        at = first + half * columns
        buffer[at : at + columns, :] = low(jnp.concatenate(thirds[2 * half : 2 * half + 2], 1))


NAMES = (
    "counts", "small_rows", "large_rows", "small_cot", "large_cot",
    "small_in", "small_out", "small_up", "small_down",
    "large_in", "large_out", "large_up", "large_down",
    "small_enter", "large_cross_in", "large_cross_out", "small_leave",
    "large_enter", "small_cross_in", "small_cross_out", "large_leave",
    "small_gains", "small_shifts", "large_gains", "large_shifts", "small_up_bias", "large_up_bias",
)
OUTS = (
    "small_out", "large_out", "small_rows", "large_rows",
    "small_heads_in", "small_heads_out", "small_up", "small_up_bias", "small_down",
    "large_heads_in", "large_heads_out", "large_up", "large_up_bias", "large_down",
    "small_enter", "large_cross_in", "large_cross_out", "small_leave",
    "large_enter", "small_cross_in", "small_cross_out", "large_leave",
    "small_gains", "small_shifts", "large_gains", "large_shifts",
)
def scratch_of(b):
    d, t, h = b.columns, b.tokens, b.hidden
    scratch = dict(
        logs=pltpu.VMEM((8, t), F32),
        stats=pltpu.VMEM((8, t), F32),
        index=pltpu.VMEM((8, t), jnp.int32),
        x=pltpu.VMEM((d, t), BF16),
        cotT=pltpu.VMEM((d, t), BF16),
        a=pltpu.VMEM((d + 16, t), BF16),
        qkv=pltpu.VMEM((3 * d, t), BF16),
        o=pltpu.VMEM((d + 16, t), BF16),
        y=pltpu.VMEM((d, t), F32),
        c=pltpu.VMEM((d + 16, t), BF16),
        u=pltpu.VMEM((h + 16, t), BF16),
        g=pltpu.VMEM((h, t), BF16),
        z=pltpu.VMEM((d, t), F32),
        n=pltpu.VMEM((d, t), BF16),
        out=pltpu.VMEM((d, t), BF16),
        sp=pltpu.VMEM((2 * STACK, t), BF16),
        maps=pltpu.VMEM((2 * STACK, d), BF16),
        cls=pltpu.VMEM((CLS, d), F32),
        cot_cls=pltpu.VMEM((CLS, d), F32),
        new_cls=pltpu.VMEM((CLS, d), BF16),
        cls_grad=pltpu.VMEM((CLS, d), F32),
        table=pltpu.VMEM((24, d), F32),
        tabT=pltpu.VMEM((d, 128), F32),
        w_inT=pltpu.VMEM((3 * d, d), BF16),
        w_upT=pltpu.VMEM((h, d), BF16),
        w_downT=pltpu.VMEM((d, h), BF16),
        other_up=pltpu.VMEM((d, h // 2), BF16),
    )
    if b.index == 0:
        scratch.update(og=pltpu.VMEM((d, t), BF16), other_down=pltpu.VMEM((d, h // 2), BF16))
    else:
        scratch.update(other_down=pltpu.VMEM((h // 2, d), BF16))
    return scratch


def columns_of(rows):
    rows = rows.astype(F32)
    return jnp.concatenate([rows, jnp.zeros((128 - rows.shape[0], rows.shape[1]), F32)], 0).T


def prepare(b, r):
    r.tabT[...] = columns_of(jnp.concatenate([r.gains[...].astype(F32), r.shifts[...].astype(F32)], 0))
    r.w_inT[...] = r.w_in[...].T
    r.a[b.columns : b.columns + 16, :] = jnp.ones((16, b.tokens), BF16)
    r.o[b.columns : b.columns + 16, :] = jnp.ones((16, b.tokens), BF16)
    r.c[b.columns : b.columns + 16, :] = jnp.ones((16, b.tokens), BF16)
    r.u[b.hidden : b.hidden + 16, :] = jnp.ones((16, b.tokens), BF16)
    r.table[...] = jnp.zeros_like(r.table)


def prepare_mlp(b, r, part):
    half, columns = b.hidden // 2, b.columns
    mine = slice(part * half, (part + 1) * half)
    biases = columns_of(r.up_bias[part][0:16, :])
    for at in range(0, half, columns):
        place = b.index + at // LANES
        column = 19 + (part * half + at) // columns
        r.tabT[:, column : column + 1] = biases[at % LANES : at % LANES + columns, place : place + 1]
    r.w_upT[mine, :] = r.up[part][...].T
    r.w_downT[:, mine] = r.down[part][...].T if b.index else r.down[part][...]


class Refs:
    pass


PHASES = {
    "tables": (((0,), "full"), (("t", 1,), "full"), ((2, 3,), "full")),
    "tail": (((0,), "halve"), (("t", 1,), "halve"), ((2,), "full"), ((3,), "full")),
    "large_up": (((0,), "halve"), ((1,), "halve"), (("t",), "merge"), ((2, 3,), "halve")),
    "large_in": (((0,), "halve"), (("t", 1,), "halve"), ((2,), "halve"), ((3,), "full")),
    "cross_b": (((0,), "halve"), ((1,), "halve"), ((2, 3,), "halve"), (("t",), "full")),
    "cross_c": (((0,), "halve"), ((1,), "halve"), ((2,), "full"), ((3,), "full"), (("t",), "halve")),
    "large_down": (((0,), "halve"), ((1,), "halve"), ((2,), "halve"), (("t",), "merge"), ((3,), "full")),
    "small_mlp": (((0,), "halve"), ((1,), "halve"), (("t",), "merge"), ((2,), "full"), ((3,), "full")),
    "mixed": (((0,), "halve"), (("t",), "halve"), ((2, 3,), "halve"), ((1,), "halve")),
    "cross_a": (((0,), "halve"), (("t",), "halve"), ((1,), "full"), ((2,), "halve"), ((3,), "halve")),
}
TICKS = {
    "crossend": ("cross_b",),
    "bcross_l2": ("cross_b", "cross_c", "cross_a",),
    "bmlp_l0": ("cross_c", "cross_a",),
    "bmlp_l2": ("cross_b",),
    "gmlp_l1": ("cross_c", "cross_a", "large_up",),
    "gmlp_l3": ("large_up", "large_down",),
    "gol": ("mixed",),
    "batt_l0": ("cross_b", "cross_c", "large_down", "mixed", "cross_a",),
    "batt_l1": ("cross_b",),
    "batt_l2": ("large_up", "cross_c", "mixed", "cross_a",),
    "ghead_l": ("large_in",),
    "bmlp_s0": ("large_in",),
    "bmlp_s2": ("large_up", "cross_b", "large_down",),
    "bmlp_s3": ("cross_c",),
    "bmlp_s4": ("mixed",),
    "gmlp_s1": ("cross_a",),
    "gmlp_s3": ("small_mlp",),
    "batt_s1": ("large_in", "cross_c", "small_mlp",),
    "batt_s2": ("large_up",),
    "batt_s3": ("large_down",),
    "batt_s4": ("cross_b", "mixed", "cross_a",),
    "ghead_s": ("large_in", "cross_c", "tail",),
    "bnorm_l0": ("cross_b",),
    "bnorm_l1": ("tail", "cross_c", "large_down",),
    "bnorm_s2": ("large_up", "small_mlp",),
    "bnorm_s3": ("mixed", "cross_a",),
    "tables": ("tables",),
    "out_l0": ("large_in",),
    "out_l1": ("tables", "tail",),
    "out_l3": ("small_mlp",),
    "out_s0": ("large_down",),
    "out_s1": ("large_up", "large_in",),
    "out_s3": ("tail", "large_up",),
    "back_l0": ("mixed",),
    "back_l1": ("small_mlp", "cross_a",),
    "back_l3": ("large_down",),
    "back_s0": ("tables", "cross_a",),
    "back_s1": ("tail",),
}
REST = (
    "large_in", "small_mlp", "large_down", "large_in", "mixed", "large_down", "mixed", "small_mlp", "tail", "tables", "small_mlp", "tail",
)


class Plan:
    def __init__(self, place, small, large, dp):
        ds, dl, first = small.columns, large.columns, place.first
        self.dp_bits = dp.bit_length() - 1
        assert dp == 1 << self.dp_bits
        more = [(tuple(range(at, min(at + 2, self.dp_bits))), "halve") for at in range(4, self.dp_bits, 2)]
        self.pool = Pool()
        other, cross, heads = first["other"], first["large_cross"], first["large_in"]
        tail = heads + 1024
        places = {
            "large_up": (first["large_up"], 2 * dl, other + first["large_up"]),
            "large_down": (first["large_down"], 2 * dl, other + first["large_down"]),
            "small_mlp": (first["small_up"], 2 * ds, other + first["small_up"]),
            "cross_a": (cross + 0, 1024, None),
            "cross_b": (cross + 1024, 1024, None),
            "cross_c": (cross + 2048, 512, None),
            "mixed": (cross + 2560, first["large_in"] - cross - 2560, None),
            "large_in": (heads, 1024, None),
            "tail": (tail, first["tables"] - tail, None),
            "tables": (first["tables"], 64, None),
        }
        self.groups, self.met = {}, []
        for name, (begin, rows, apart) in places.items():
            group = Group(self.pool, begin, rows, list(PHASES[name]) + more, apart)
            self.groups[name] = group
            for step in group.steps:
                for number, flipped in subsets(step[1]):
                    if flipped not in self.met:
                        self.met.append(flipped)


def layer_kernel(small, large, place, plan, keys, solo, *refs):
    ins = dict(zip(NAMES, refs))
    refs = refs[len(NAMES) :]
    sources = {name: ins[name] for name in FETCH}
    packed, small_out, large_out, small_grad, large_grad = refs[:5]
    refs = refs[5:]
    groups = []
    links = Links(plan.dp_bits)
    links.bind(solo)
    for b in (small, large):
        r = Refs()
        for key in keys[b.index]:
            setattr(r, key, refs[0])
            refs = refs[1:]
        groups.append((b, r))
    (bs, rs), (bl, rl) = groups
    for name in FETCH:
        if name not in ("large_rows", "large_cot"):
            ins[name], refs = refs[0], refs[1:]
    work, mask, sums, own_biases = refs[:4]
    biases, other_biases, buffer, received, send, recv, free, swap_send, swap_recv, out_sem, in_sem = refs[4:]
    for b, r in groups:
        name = ("small", "large")[b.index]
        r.w_in, r.w_out = ins[name + "_in"], ins[name + "_out"]
        r.up = (ins[name + "_up"], r.other_up)
        r.down = (ins[name + "_down"], r.other_down)
        r.gains, r.shifts = ins[name + "_gains"], ins[name + "_shifts"]
        r.enter, r.leave = ins[name + "_enter"], ins[name + "_leave"]
        r.cross_in, r.cross_out = ins[name + "_cross_in"], ins[name + "_cross_out"]
        r.zg, r.yg = r.n, r.cotT
        r.bias_rows, r.mask, r.sums = biases, mask, sums
        r.up_bias = (own_biases, other_biases)
    half_s = bs.hidden // 2
    rs.down_times = lambda part, z: tn(rs.w_downT[:, part * half_s : (part + 1) * half_s], z)
    rl.down_times = lambda part, z: nn(rl.down[part][...], z)
    rs.og_rows = lambda slot, rows: rs.og.at[rows, slot_columns(bs, slot)]

    def large_og(slot, rows):
        size = rows.stop - rows.start
        if isinstance(slot, int):
            return rl.w_upT.at[slot * bl.columns + rows.start : slot * bl.columns + rows.stop, :]
        return rl.w_upT.at[pl.ds(pl.multiple_of(slot * bl.columns + rows.start, 64), size), :]

    rl.og_rows = large_og
    rs.staged = rs.sp.at[:, 0 : bs.rows]
    rl.staged = rl.w_inT.at[0 : bl.rows, :]
    biases[...] = jnp.zeros_like(biases)
    bias = [ins["small_up_bias"][...]]
    bias += [ins["large_up_bias"][at : at + LANES] for at in range(0, bl.hidden // 2, LANES)]
    bias = [value.astype(F32).reshape(1, LANES) for value in bias]
    own_biases[...] = low(jnp.concatenate(bias + [jnp.zeros((32 - len(bias), LANES), F32)], 0))
    for group in plan.groups.values():
        group.bind(links, buffer, received, send, recv, free)
    swap = Swap(
        links,
        (
            (ins["large_up"], rl.other_up),
            (ins["large_down"], rl.other_down),
            (ins["small_up"], rs.other_up),
            (ins["small_down"], rs.other_down),
            (own_biases, other_biases),
        ),
        swap_send,
        swap_recv,
    )
    fetched = {}

    def fetch(names):
        for name in names:
            if name in ("large_rows", "large_cot"):
                at = ("large_rows", "large_cot").index(name)
                target = rl.u.at[0 : bl.rows, at * bl.columns : (at + 1) * bl.columns]
            else:
                target = ins[name]
            fetched[name] = pltpu.make_async_copy(
                sources[name], target, in_sem.at[FETCH.index(name)]
            )
            fetched[name].start()

    fetch(FETCH[:8])

    def need(*names):
        for name in names:
            fetched.pop(name).wait()

    rs.rows, rs.cot = ins["small_rows"], ins["small_cot"]
    rl.rows = rl.g.at[0 : bl.columns, 0 : bl.rows]
    rl.cot = rl.g.at[bl.columns : 2 * bl.columns, 0 : bl.rows]

    out_copies = {}

    def write_out(name, source, target):
        copy = pltpu.make_async_copy(source, target, out_sem.at[len(out_copies)])
        copy.start()
        out_copies[name] = copy

    def step(name):
        group = plan.groups[name]
        if solo is None and not group.done:
            group.advance()
            if group.done:
                rows = slice(group.first, group.first + group.rows)
                write_out(name, buffer.at[rows, :], packed.at[rows, :])

    def tick(label):
        for name in TICKS.get(label, ()):
            step(name)

    def ticks(stage, count):
        if any(stage + str(part) in TICKS for part in range(count)):
            return lambda part: tick(stage + str(part))
        return None

    def always(stage):
        return lambda part: tick(stage + str(part))

    if solo is None:
        greet(links, plan.met)
    need("small_rows", "small_cot")
    lay_out(bs, rs, ins["counts"])
    fetch(FETCH[8:])
    bring_in(bs, rs)
    need("large_up", "large_down", "small_up", "small_down")
    if solo is None:
        all_here(plan.met)
        swap.start(0)
    else:
        for mine, theirs in swap.pairs:
            theirs[...] = mine[...]
    need("large_rows", "large_cot")
    for at, target in enumerate((rl.rows, rl.cot)):
        target[...] = rl.u[0 : bl.rows, at * bl.columns : (at + 1) * bl.columns].T
    lay_out(bl, rl, ins["counts"])
    bring_in(bl, rl)
    need("small_in", "large_in")
    prepare(bs, rs)
    prepare(bl, rl)
    need("small_out", "large_out")
    forward_attention(bl, rl, [rl.z], [rl.w_downT])

    def pass_on(slot):
        if slot == 3 and solo is None:
            swap.wait(0)
            swap.start(1)

    forward_attention(bs, rs, [rl.z, work], [rl.w_downT], pass_on)
    for b, r in groups:
        prepare_mlp(b, r, 0)
    if solo is None:
        swap.wait(1)
    for b, r in groups:
        prepare_mlp(b, r, 1)
    forward_mlp(bs, rs, lambda slot: None)
    need(*tuple(fetched))
    both = [
        cross(bs, rs, bl, rl, CrossGrads(bs, bl, place, buffer)),
        cross(bl, rl, bs, rs, CrossGrads(bl, bs, place, buffer)),
    ]

    def class_rows(slot):
        if slot < 2:
            for part in range(4 - slot):
                next(both[0])

    forward_mlp(bl, rl, class_rows)
    while both:
        both = [one for one in both if next(one, both) is None]
    def large_block():
        backward_cross(bl, rl, work, ticks("bcross_l", bl.slots))
        backward_mlp(bl, rl, work, ticks("bmlp_l", bl.slots))
        mlp_grads(bl, rl, place, buffer, always("gmlp_l"))
        first = place.first["large_out"]
        buffer[first : first + bl.columns, :] = low(out_grads(bl, rl))
        tick("gol")

    def large_attention():
        wide = [rl.y, work]
        backward_attention(bl, rl, wide, [rl.w_downT], [rl.w_inT], ticks("batt_l", bl.slots))
        large_in_grads(bl, rl, place, buffer)
        tick("ghead_l")

    def small_block():
        backward_cross(bs, rs, work, ticks("bcross_s", bs.slots))
        backward_mlp(bs, rs, work, ticks("bmlp_s", bs.slots))
        mlp_grads(bs, rs, place, buffer, always("gmlp_s"))

    def small_attention():
        wide = [rl.y, work]
        backward_attention(bs, rs, wide, [rl.w_downT], [rl.g], ticks("batt_s", bs.slots))
        small_head_grads(bs, rs, place, buffer)
        tick("ghead_s")

    def norms():
        backward_first_norm(bl, rl, work, ticks("bnorm_l", bl.slots))
        backward_first_norm(bs, rs, work, ticks("bnorm_s", bs.slots))
        put_tables(links, place, buffer, rs, rl, biases)
        tick("tables")

    def outputs():
        put_out(bl, rl, ticks("out_l", 4))
        write_out("large_out", rl.staged, large_out)
        put_out(bs, rs, ticks("out_s", 4))
        write_out("small_out", rs.staged, small_out)
        out_copies["large_out"].wait()
        put_back(bl, rl, rl.x, ticks("back_l", 4))
        write_out("large_grad", rl.staged, large_grad)
        out_copies["small_out"].wait()
        put_back(bs, rs, rs.x, ticks("back_s", 4))
        write_out("small_grad", rs.staged, small_grad)

    tick("crossend")
    large_block()
    large_attention()
    small_block()
    small_attention()
    norms()
    outputs()
    for name in REST:
        step(name)
    while any(not group.done for group in plan.groups.values()) and solo is None:
        for name in plan.groups:
            step(name)
    for name, copy in out_copies.items():
        if name not in ("large_out", "small_out"):
            copy.wait()


def put_tables(links, place, buffer, rs, rl, biases):
    ds = rs.table.shape[1]
    own, other = biases[0, 0:8, :], biases[1, 0:8, :]
    first = links.tensor == 0
    rows = [
        rl.table[...],
        jnp.concatenate([rs.table[...], jnp.zeros((24, LANES - ds), F32)], 1),
        jnp.where(first, own, other),
        jnp.where(first, other, own),
    ]
    buffer[place.rows("tables"), :] = low(jnp.concatenate(rows, 0))


def unpack_kernel(place, ds, dl, parts, *refs):
    (packed, small_out, large_out, small_grad, large_grad), refs = refs[:5], refs[5:]
    outs, refs = dict(zip(OUTS, refs)), refs[len(OUTS) :]
    got, got_small, got_large, out_small, out_large = refs[:5]
    refs = refs[5:]
    stages, refs = dict(zip(OUTS[2:], refs)), refs[len(OUTS) - 2 :]
    in_sem, out_sem = refs
    copies, arriving = [], {}

    def bring(name, source, target):
        arriving[name] = pltpu.make_async_copy(source, target, in_sem.at[len(arriving)])
        arriving[name].start()

    def leave(source, target):
        copies.append(pltpu.make_async_copy(source, target, out_sem.at[len(copies)]))
        copies[-1].start()

    for name, first, rows in parts:
        bring(name, packed.at[first : first + rows, :], got.at[first : first + rows, :])
    bring("small_rows", small_grad, got_small)
    bring("large_rows", large_grad, got_large)
    bring("small_out", small_out, out_small)
    bring("large_out", large_out, out_large)

    def read(name, part, rows):
        first = place.first[name] + part
        return got[first : first + rows, :].astype(F32)

    def done(*names):
        for name in names:
            leave(stages[name], outs[name])

    arriving["mlp"].wait()
    for part in range(2):
        stages["large_up"][:, part * dl : (part + 1) * dl] = read("large_up", part * dl, dl)
    done("large_up")
    stages["large_down"][...] = read("large_down", 0, 2 * dl)
    stages["small_up"][...] = read("small_up", 0, ds)
    stages["small_down"][...] = read("small_down", 0, ds)
    done("large_down", "small_up", "small_down")
    for name, into, out, at in (("cross", "large_cross", "large_cross", 3), ("heads", "large_in", "large_out", 0)):
        arriving[name].wait()
        for third in range(3):
            stages["large_" + name + "_in"][:, third * dl : (third + 1) * dl] = read(
                into, third * dl, dl
            )
        stages["large_" + name + "_out"][...] = read(out, at * dl, dl)
        second = read("small_" + name, ds, ds)
        stages["small_" + name + "_in"][:, 0:LANES] = read("small_" + name, 0, ds)
        stages["small_" + name + "_in"][:, LANES:] = second[:, 0:ds]
        stages["small_" + name + "_out"][...] = second[:, ds:]
        done("large_" + name + "_in", "large_" + name + "_out", "small_" + name + "_in", "small_" + name + "_out")
        if name == "cross":
            for key in ("small_enter", "small_leave", "large_enter", "large_leave"):
                stages[key][...] = read(key, 0, ds)
                done(key)
    for name, ref in (("small_rows", got_small), ("large_rows", got_large)):
        arriving[name].wait()
        stages[name][...] = ref[...].astype(F32)
        done(name)
    for name, ref in (("small_out", out_small), ("large_out", out_large)):
        arriving[name].wait()
        leave(ref, outs[name])
    arriving["tables"].wait()
    first = place.first["tables"]
    tables = got[first : first + 64, :].astype(F32)
    stages["large_gains"][...] = tables[0:5]
    stages["large_shifts"][...] = tables[5:19]
    stages["small_gains"][...] = tables[24:29, 0:ds]
    stages["small_shifts"][...] = tables[29:43, 0:ds]
    mine = jnp.where(lax.axis_index("tensor") == 0, tables[48:56], tables[56:64])
    stages["small_up_bias"][...] = mine[0]
    stages["large_up_bias"][0:LANES] = mine[1]
    stages["large_up_bias"][LANES:] = mine[2]
    done("large_gains", "large_shifts", "small_gains", "small_shifts", "small_up_bias", "large_up_bias")
    for copy in copies:
        copy.wait()


FETCH = (
    "small_rows", "small_cot", "large_up", "large_down", "small_up", "small_down", "large_rows", "large_cot",
    "small_in", "large_in", "small_out", "large_out",
    "large_cross_in", "large_cross_out", "small_cross_in", "small_cross_out",
    "small_enter", "small_leave", "large_enter", "large_leave",
)
TURNED = ("small_out", "small_rows", "small_down", "small_leave", "large_enter")


def run_layer(args, dp, solo=None):
    (
        small_rows, large_rows, counts, small_cot, large_cot,
        small_in, small_out, small_up, small_up_bias, small_down,
        large_in, large_out, large_up, large_up_bias, large_down,
        small_enter, large_cross_in, large_cross_out, small_leave, large_enter,
    ) = args[:20]
    ds, dl = small_rows.shape[1], large_rows.shape[1]
    small = Branch(0, small_rows.shape[0], ds, 2 * small_up.shape[1], 256, ((0, 4), (1, 5), (2,), (3,), (6,)))
    large = Branch(1, large_rows.shape[0], dl, 2 * large_up.shape[1], 384, ((0, 1, 4), (2, 3, 5), (6,)))
    place = Place(small, large)
    plan = Plan(place, small, large, dp)
    inputs = (
        counts, small_rows.T, large_rows, small_cot.T, large_cot,
        small_in, small_out, small_up, small_down.T,
        large_in, large_out, large_up, large_down,
        small_enter, large_cross_in, large_cross_out, small_leave.T, large_enter.T,
    ) + args[20:] + (small_up_bias, large_up_bias)
    keys = tuple(tuple(scratch_of(b)) for b in (small, large))
    scratch = [s for b in (small, large) for s in scratch_of(b).values()]
    copies = pltpu.SemaphoreType.DMA
    for name in FETCH:
        if name not in ("large_rows", "large_cot"):
            scratch.append(pltpu.VMEM(inputs[NAMES.index(name)].shape, BF16))
    scratch += [
        pltpu.VMEM((dl, large.tokens), F32),
        pltpu.VMEM((large.width, large.width), F32),
        pltpu.VMEM((2, dl, 128), F32),
        pltpu.VMEM((32, LANES), BF16),
        pltpu.VMEM((2, 16, LANES), F32),
        pltpu.VMEM((32, LANES), BF16),
        pltpu.VMEM((place.total, LANES), BF16),
        pltpu.VMEM((plan.pool.rows, LANES), BF16),
        copies((plan.pool.copies,)),
        copies((plan.pool.copies,)),
        pltpu.SemaphoreType.REGULAR((plan.pool.signals,)),
        copies((2, 5)),
        copies((2, 5)),
        copies((20,)),
        copies((len(FETCH),)),
    ]
    shape = jax.ShapeDtypeStruct
    vmem, hbm = pl.BlockSpec(memory_space=pltpu.VMEM), pl.BlockSpec(memory_space=pl.ANY)
    middle = (
        shape((place.total, LANES), BF16),
        shape((ds, small.rows), BF16),
        shape((large.rows, dl), BF16),
        shape((ds, small.rows), BF16),
        shape((large.rows, dl), BF16),
    )
    values = pl.pallas_call(
        functools.partial(layer_kernel, small, large, place, plan, keys, solo),
        out_shape=middle,
        in_specs=[pl.BlockSpec(memory_space=pltpu.SMEM)]
        + [hbm if name in FETCH else vmem for name in NAMES[1:]],
        out_specs=(hbm,) * 5,
        scratch_shapes=scratch,
        compiler_params=pltpu.CompilerParams(
            vmem_limit_bytes=VMEM_LIMIT,
            collective_id=0 if solo is None else None,
            has_side_effects=True,
        ),
        name="layer",
    )(*inputs)
    shapes = dict(
        small_out=shape((ds, small.rows), BF16),
        large_out=shape(large_rows.shape, BF16),
        small_rows=shape((ds, small.rows), F32),
        large_rows=shape(large_rows.shape, F32),
        small_up_bias=shape(small_up_bias.shape, F32),
        large_up_bias=shape(large_up_bias.shape, F32),
    )
    for name, value in zip(OUTS[4:], args[5:]):
        turned = value.shape[::-1] if name in TURNED else value.shape
        shapes.setdefault(name, shape(turned, F32))
    first = place.first
    cross_first = first["large_cross"]
    parts = (
        ("mlp", 0, first["other"]),
        ("cross", cross_first, first["large_out"] - cross_first),
        ("heads", first["large_out"], first["tables"] - first["large_out"]),
        ("tables", first["tables"], 64),
    )
    results = pl.pallas_call(
        functools.partial(unpack_kernel, place, ds, dl, parts),
        out_shape=tuple(shapes[name] for name in OUTS),
        in_specs=(hbm,) * 5,
        out_specs=(hbm,) * len(OUTS),
        scratch_shapes=[
            pltpu.VMEM((place.total, LANES), BF16),
        ]
        + [pltpu.VMEM((ds, small.rows), BF16), pltpu.VMEM(large_rows.shape, BF16)] * 2
        + [pltpu.VMEM(shapes[name].shape, F32) for name in OUTS[2:]]
        + [copies((8,)), copies((len(OUTS),))],
        compiler_params=pltpu.CompilerParams(vmem_limit_bytes=VMEM_LIMIT),
        name="unpack",
    )(*values)

    def restore(name, value):
        return value.T if name in TURNED else value

    return tuple(restore(name, value) for name, value in zip(OUTS, results))


def solution(mesh):
    both = ("dp", "tensor")
    rows = P(both, None)
    mlp = (P(None, "tensor"), P("tensor"), P("tensor", None))

    def shards(*args):
        return run_layer(args, mesh.shape["dp"])

    return jax.shard_map(
        shards,
        mesh=mesh,
        in_specs=(rows, rows, P(None, both), rows, rows)
        + ((P(), P()) + mlp) * 2
        + (P(),) * 12,
        out_specs=(rows,) * 4 + ((P(), P()) + mlp) * 2 + (P(),) * 12,
        check_vma=False,
    )
```
